32 devices in a mesh: section: 2 (over y), fsdp: 4 (over z), dp: 4 (over x, core).
Axes of the slice: x: 2, y: 2, z: 4, core: 2. Of those that a mesh axis runs over, the one named last changes fastest.
Arguments:
- inputs: bfloat16 [2, 16, 256, 1024], P(None, ('fsdp', 'dp')), may hold values from -6 to 6
- cotangent: bfloat16 [2, 16, 256, 1024], P(None, ('fsdp', 'dp')), may hold values from -6 to 6
- segments: int32 [2, 16, 256], P(None, ('fsdp', 'dp')), may hold values from 0 to 3, never falling along the last dimension, each value on 1 to 128 neighbouring positions
- norm_gain: bfloat16 [2, 1024], P('section', 'fsdp'), may hold values from 0.5 to 1.5
- in_weight: bfloat16 [2, 1024, 4384], P('section', 'fsdp'), may hold values from -0.1875 to 0.1875
- conv_weight: bfloat16 [2, 4, 2304], P('section', None, 'fsdp'), may hold values from -3 to 3
- conv_bias: bfloat16 [2, 2304], P('section', 'fsdp'), may hold values from -3 to 3
- dt_bias: bfloat16 [2, 32], P('section', 'fsdp'), may hold values from -3 to 0.5
- decay_log: bfloat16 [2, 32], P('section', 'fsdp'), may hold values from -3 to 1.5
- skip_gain: bfloat16 [2, 32], P('section', 'fsdp'), may hold values from 0.5 to 1.5
- gate_gain: bfloat16 [2, 2048], P('section', 'fsdp'), may hold values from 0.5 to 1.5
- out_weight: bfloat16 [2, 2048, 1024], P('section', 'fsdp'), may hold values from -0.125 to 0.125
Outputs:
- output: bfloat16 [2, 16, 256, 1024], P('section', ('fsdp', 'dp'))
- input_grad: float32 [2, 16, 256, 1024], P('section', ('fsdp', 'dp'))
- norm_gain_grad: float32 [2, 1024], P('section', 'fsdp')
- in_weight_grad: float32 [2, 1024, 4384], P('section', 'fsdp')
- conv_weight_grad: float32 [2, 4, 2304], P('section', None, 'fsdp')
- conv_bias_grad: float32 [2, 2304], P('section', 'fsdp')
- dt_bias_grad: float32 [2, 32], P('section', 'fsdp')
- decay_log_grad: float32 [2, 32], P('section', 'fsdp')
- skip_gain_grad: float32 [2, 32], P('section', 'fsdp')
- gate_gain_grad: float32 [2, 2048], P('section', 'fsdp')
- out_weight_grad: float32 [2, 2048, 1024], P('section', 'fsdp')
The draws below stay inside these ranges and needn't reach their ends.
Inputs may be any that keep to these rules, and one draw needn't show every extreme that they name: `segments`: in each sequence the document numbers never fall; a document has 1 to 128 positions and one of them has exactly 128.
All inputs are finite; a program needn't handle non-finite values.
Results may differ from the reference program's by a relative error of at most 0.02.
Values may be sent and summed in bfloat16 or wider, within the bound.
No kernel may reach another device: no remote copies, remote signals or barrier semaphores. Data moves between devices by JAX's collectives and lax.ppermute only.
A program may use at most 320 MiB of HBM per device.

```python
import math
import jax
import jax.numpy as jnp
import numpy as np
from jax import lax

D = 1024
H = 32
K = 4
STRETCH = 256
SEQ = 256
MICRO = 2
DI = 2048
CONVW = 2304
PROJ = 4384
SEQS = 16
N_SECTION = 2


def shard_levels(key, dims, split, low, top_value):
    loudness, own = 1.0, jax.random.fold_in(key, 6)
    for dim, blocks in split:
        steps = jnp.exp(jax.random.uniform(jax.random.fold_in(own, dim), (blocks,), jnp.float32, low / len(split), top_value / len(split)))
        loudness = loudness * jnp.repeat(steps, dims[dim] // blocks).reshape([-1 if axis == dim else 1 for axis in range(len(dims))])
    return loudness


def length_profile(count, total, limit, lean):
    loads = [(1 << 20) // math.isqrt(rank ** lean) + 1 for rank in range(2, count + 1)]
    surplus, given = total - limit - (count - 1), [1] * (count - 1)
    while surplus > 0:
        free = [i for i in range(count - 1) if given[i] < limit]
        pool, remaining = sum([loads[i] for i in free]), surplus
        for i in free:
            addition = min(limit - given[i], max(1, remaining * loads[i] // pool), surplus)
            given[i] = given[i] + addition
            surplus = surplus - addition
    return np.array([limit] + given)


def uneven(rng, amount, total, reach, lean):
    if amount == 2:
        one = jax.random.randint(rng, (), max(1, total - reach), min(reach, total - 1) + 1)
        return jnp.stack([one, total - one])
    sizes = jnp.asarray(length_profile(amount, total, reach, lean), jnp.int32)
    twos = (amount - 1) // 2
    donor, receiver = sizes[1:1 + 2 * twos:2], sizes[2:2 + 2 * twos:2]
    margin = jnp.minimum(donor - 1, reach - receiver)
    passed = jax.random.randint(jax.random.fold_in(rng, 1), (twos,), 0, 1 << 20) % (margin + 1)
    sizes = sizes.at[1:1 + 2 * twos:2].set(donor - passed).at[2:2 + 2 * twos:2].set(receiver + passed)
    return sizes[jax.random.permutation(jax.random.fold_in(rng, 2), amount)]


def scatter_about(stream_key, dims, scale, limit, shards=(), dtype=jnp.bfloat16):
    values = jax.random.normal(stream_key, dims, jnp.float32) * scale
    if len(shards) > 0:
        values = shard_levels(stream_key, dims, shards, -0.22, 0.18) * values
    return jnp.clip(values, min=-limit, max=limit).astype(dtype)


def setup_inputs(seed: int = 0) -> dict:
    key_of = jax.random.split(jax.random.key(seed), 13)
    return {
        "inputs": scatter_about(key_of[0], (MICRO, SEQS, SEQ, D), 1.0, 6.0, ((1, 16),)),
        "cotangent": scatter_about(key_of[1], (MICRO, SEQS, SEQ, D), 1.0, 6.0, ((1, 16),)),
        "segments": jax.vmap(lambda own: jnp.searchsorted(jnp.cumsum(uneven(own, 4, SEQ, SEQ // 2, 0)), jnp.arange(SEQ), side="right"))(jax.random.split(key_of[2], MICRO * SEQS)).reshape((MICRO, SEQS, SEQ)).astype(jnp.int32),
        "norm_gain": jnp.clip(1.0 + 0.1 * jax.random.normal(key_of[3], (N_SECTION, D), jnp.float32), 0.5, 1.5).astype(jnp.bfloat16),
        "in_weight": scatter_about(key_of[4], (N_SECTION, D, PROJ), D ** -0.5, 0.1875, ((0, 2), (1, 4))),
        "conv_weight": scatter_about(key_of[5], (N_SECTION, K, CONVW), K ** -0.5, 3.0, ((0, 2), (2, 4))),
        "conv_bias": scatter_about(key_of[6], (N_SECTION, CONVW), 0.5, 3.0, ((0, 2), (1, 4))),
        "dt_bias": jnp.clip(-3.0 + 3.5 * jax.random.uniform(key_of[7], (N_SECTION, H), jnp.float32) ** shard_levels(key_of[7], (N_SECTION, H), ((0, 2), (1, 4)), -0.2, 0.2), -3.0, 0.5).astype(jnp.bfloat16),
        "decay_log": jnp.clip(-3.0 + 4.5 * jax.random.uniform(key_of[8], (N_SECTION, H), jnp.float32) ** shard_levels(key_of[8], (N_SECTION, H), ((0, 2), (1, 4)), -0.2, 0.2), -3.0, 1.5).astype(jnp.bfloat16),
        "skip_gain": jnp.clip(0.5 + 1.0 * jax.random.uniform(key_of[9], (N_SECTION, H), jnp.float32) ** shard_levels(key_of[9], (N_SECTION, H), ((0, 2), (1, 4)), -0.2, 0.2), 0.5, 1.5).astype(jnp.bfloat16),
        "gate_gain": jnp.clip(1.0 + 0.1 * jax.random.normal(key_of[10], (N_SECTION, DI), jnp.float32), 0.5, 1.5).astype(jnp.bfloat16),
        "out_weight": scatter_about(key_of[11], (N_SECTION, DI, D), DI ** -0.5, 0.125, ((0, 2), (1, 4))),
    }


EPS = 1e-05
HIGH = lax.Precision.HIGHEST

@jax.custom_vjp
def low(v):
    return lax.optimization_barrier(v.astype(jnp.bfloat16)).astype(jnp.float32)

@jax.custom_vjp
def low_back(v):
    return v

def low_keep(v):
    return (low(v), None)

def low_pass(kept, grad):
    return (grad,)

def back_keep(v):
    return (v, None)

def back_low(kept, grad):
    return (low(grad),)
low.defvjp(low_keep, low_pass)
low_back.defvjp(back_keep, back_low)

def rms_norm(value, gain):
    return value * lax.rsqrt(lax.optimization_barrier(jnp.mean(value * value, axis=-1, keepdims=True)) + EPS) * gain

def stretch_step(state, pieces):
    decay_in, inputs_dt, keys_b, queries_c, seg_block, before = pieces
    width = decay_in.shape[0]
    cumul = jnp.cumsum(decay_in, axis=0)
    order = jnp.arange(width)
    within = (order[:, None] >= order[None, :]) & (seg_block[:, None] == seg_block[None, :])
    gaps = cumul.T[:, :, None] - cumul.T[:, None, :]
    decay = jnp.where(within[None], jnp.exp(jnp.where(within[None], gaps, 0.0)), 0.0)
    scores = jnp.dot(queries_c, keys_b.T, precision=HIGH)
    mixed = jnp.einsum('hij,jhp->ihp', decay * scores[None], inputs_dt, precision=HIGH)
    carried = (seg_block == before).astype(jnp.float32)
    from_state = jnp.einsum('in,hpn->ihp', queries_c, state, precision=HIGH)
    mixed = mixed + from_state * (jnp.exp(cumul) * carried[:, None])[:, :, None]
    final = seg_block[-1]
    tail = jnp.where((seg_block == final)[:, None], jnp.exp(cumul[-1][None, :] - cumul), 0.0)
    keep = jnp.exp(cumul[-1]) * (final == before).astype(jnp.float32)
    state = state * keep[:, None, None] + jnp.einsum('jhp,jn->hpn', inputs_dt * tail[:, :, None], keys_b, precision=HIGH)
    return (state, mixed)

def mixer(proj, seg, conv_weight, conv_bias, dt_bias, decay_log, skip_gain, gate_gain):
    length = proj.shape[0]
    inner = gate_gain.shape[0]
    heads = dt_bias.shape[0]
    conv_width = conv_bias.shape[0]
    state_size = (conv_width - inner) // 2
    head_dim = inner // heads
    taps = conv_weight.shape[0]
    gate = proj[:, :inner]
    stream = proj[:, inner:inner + conv_width]
    dt_raw = proj[:, inner + conv_width:]
    total = conv_bias + stream * conv_weight[taps - 1]
    for lag in range(1, taps):
        shifted = jnp.pad(stream, ((lag, 0), (0, 0)))[:length]
        earlier = jnp.pad(seg, (lag, 0), constant_values=-1)[:length]
        total = total + jnp.where((earlier == seg)[:, None], shifted, 0.0) * conv_weight[taps - 1 - lag]
    conv_out = jax.nn.silu(total)
    values = conv_out[:, :inner].reshape(length, heads, head_dim)
    keys_b = conv_out[:, inner:inner + state_size]
    queries_c = conv_out[:, inner + state_size:]
    step = jax.nn.softplus(dt_raw + dt_bias)
    decay_in = -jnp.exp(decay_log) * step
    inputs_dt = values * step[:, :, None]
    blocks = length // STRETCH
    seg_blocks = seg.reshape(blocks, STRETCH).astype(jnp.int32)
    before = jnp.concatenate([jnp.full((1,), -1, jnp.int32), seg_blocks[:-1, -1].astype(jnp.int32)])
    start = jnp.zeros((heads, head_dim, state_size), jnp.float32)
    _, mixed = lax.scan(jax.checkpoint(stretch_step), start, (decay_in.reshape(blocks, STRETCH, heads), inputs_dt.reshape(blocks, STRETCH, heads, head_dim), keys_b.reshape(blocks, STRETCH, state_size), queries_c.reshape(blocks, STRETCH, state_size), seg_blocks, before))
    mixed = mixed.reshape(length, heads, head_dim) + skip_gain[None, :, None] * values
    gated = mixed.reshape(length, inner) * jax.nn.silu(gate)
    return rms_norm(gated, gate_gain)

def layer(stream_in, seg, params):
    norm_gain, in_weight, conv_weight, conv_bias, dt_bias, decay_log, skip_gain, gate_gain, out_weight = params
    normed = low(rms_norm(stream_in, norm_gain))
    proj = low_back(jnp.einsum('bld,de->ble', normed, in_weight, precision=HIGH))
    mixed = jax.vmap(mixer, in_axes=(0, 0, None, None, None, None, None, None))(proj, seg, conv_weight, conv_bias, dt_bias, decay_log, skip_gain, gate_gain)
    mixed = low(mixed)
    out = low_back(jnp.einsum('bli,id->bld', mixed, out_weight, precision=HIGH))
    return stream_in + out

def model(inputs, params, seg):
    stream = inputs
    for level in range(N_SECTION):
        if level > 0:
            stream = low_back(low(stream))
        stream = layer(stream, seg, tuple((p[level] for p in params)))
    return stream

def reference(inputs, cotangent, segments, norm_gain, in_weight, conv_weight, conv_bias, dt_bias, decay_log, skip_gain, gate_gain, out_weight):
    params = tuple((p.astype(jnp.float32) for p in (norm_gain, in_weight, conv_weight, conv_bias, dt_bias, decay_log, skip_gain, gate_gain, out_weight)))
    count = MICRO * SEQS
    group = 4
    stream_all = inputs.astype(jnp.float32).reshape(count // group, group, SEQ, D)
    grad_all = cotangent.astype(jnp.float32).reshape(count // group, group, SEQ, D)
    seg_all = segments.reshape(count // group, group, SEQ).astype(jnp.int32)
    zeros = tuple((jnp.zeros_like(p) for p in params))

    def group_step(accum, item):
        stream_g, grad_g, seg_g = item

        def forward(values, weights):
            return model(values, weights, seg_g)
        result, pull = jax.vjp(forward, stream_g, params)
        grad_in, grad_params = pull(grad_g)
        return (tuple((a + b for a, b in zip(accum, grad_params))), (result.astype(jnp.bfloat16), grad_in))
    grads, (results, input_grads) = lax.scan(group_step, zeros, (stream_all, grad_all, seg_all))
    return (results.reshape(MICRO, SEQS, SEQ, D), input_grads.reshape(MICRO, SEQS, SEQ, D), grads[0], grads[1], grads[2], grads[3], grads[4], grads[5], grads[6], grads[7], grads[8])
```

```python
import functools

import jax
import jax.numpy as jnp
from jax import lax
from jax.experimental import pallas as pl
from jax.experimental.pallas import tpu as pltpu
from jax.sharding import PartitionSpec as P

EPS = 1e-05
LOG2E = 1.4426950408889634
HIGH = lax.Precision.HIGHEST
F32 = jnp.float32
BF16 = jnp.bfloat16
LANES = 128
WIDE = 256
VMEM_BYTES = 56 * 1024 * 1024


def sigmoid(v):
    return 0.5 * jnp.tanh(0.5 * v) + 0.5


def dot(a, b):
    return lax.dot_general(a, b, (((1,), (0,)), ((), ())), preferred_element_type=F32)


def dot_nt(a, b):
    return lax.dot_general(a, b, (((1,), (1,)), ((), ())), preferred_element_type=F32)


def dot_tn(a, b):
    return lax.dot_general(a, b, (((0,), (0,)), ((), ())), preferred_element_type=F32)


def twice(v):
    return jnp.concatenate([v, v], axis=1)


def fold(v):
    return v[:, :LANES] + v[:, LANES:]


def cols(start, width=WIDE):
    return pl.ds(pl.multiple_of(start, LANES), width)


def write_masks(segc_ref, mask_ref, taps):
    seg = segc_ref[...]
    row = lax.broadcasted_iota(jnp.int32, seg.shape, 0)
    for lag in range(1, taps):
        same = (pltpu.roll(seg, lag, 0) == seg) & (row >= lag)
        mask_ref[lag - 1] = jnp.where(same, 1.0, 0.0)


def conv_chunk(s, start, cw_ref, cb_ref, mask_ref, taps):
    at = cols(start)
    total = cb_ref[:, at] + s * cw_ref[pl.ds(taps - 1, 1), at]
    for lag in range(1, taps):
        shifted = pltpu.roll(s, lag, 0) * twice(mask_ref[lag - 1])
        total = total + shifted * cw_ref[pl.ds(taps - 1 - lag, 1), at]
    return total


def step_sizes(dt, dtb_ref, dl_ref, heads):
    length = dt.shape[0]
    pad = jnp.zeros((length, LANES - heads), F32)
    v = jnp.concatenate([dt, pad], axis=1) + dtb_ref[...]
    step = jnp.maximum(v, 0.0) + jnp.log1p(jnp.exp(-jnp.abs(v)))
    rate = -jnp.exp(dl_ref[...]) * step
    i = lax.broadcasted_iota(jnp.int32, (length, length), 0)
    j = lax.broadcasted_iota(jnp.int32, (length, length), 1)
    lower = jnp.where(i >= j, 1.0, 0.0)
    scaled = rate * LOG2E
    cumul = lax.dot_general(lower, scaled, (((1,), (0,)), ((), ())), precision=HIGH, preferred_element_type=F32)
    return v, step, rate, cumul


def head_lanes(v, quad, per):
    return pltpu.roll(v, lax.rem(LANES - per * quad, LANES), 1)


def spread(v, i0, head_dim):
    length = v.shape[0]
    lane = lax.broadcasted_iota(jnp.int32, (length, LANES), 1)
    a = jnp.broadcast_to(v[:, i0 : i0 + 1], (length, LANES))
    b = jnp.broadcast_to(v[:, i0 + 1 : i0 + 2], (length, LANES))
    return jnp.where(lane < head_dim, a, b)


def forward_body(
    sizes, u_ref, segc_ref, segr_ref, ng_ref, cw_ref, cb_ref, dtb_ref, dl_ref, sk_ref, gg_ref, w_hbm, ow_hbm,
    out_ref, gate_ref, stream_ref, dt_ref, y_ref, normed_ref, mixed_ref,
    w, ow, mask_ref, s_ref, gated_ref, cum_ref, step_ref, cumt_ref, sem, osem,
):
    length, width, inner, conv, heads, taps = sizes
    state = (conv - inner) // 2
    head_dim = inner // heads
    per = WIDE // head_dim
    quads = inner // WIDE
    half = length // 2
    proj = w.shape[1]
    tail = 2 * inner

    def stream_copy(q):
        at = cols(inner + q * WIDE)
        return pltpu.make_async_copy(w_hbm.at[:, at], w.at[:, at], sem.at[1 + 2 * q])

    def gate_copy(q):
        at = cols(q * WIDE)
        return pltpu.make_async_copy(w_hbm.at[:, at], w.at[:, at], sem.at[2 + 2 * q])

    tail_copy = pltpu.make_async_copy(
        w_hbm.at[:, tail:proj], w.at[:, tail:proj], sem.at[0]
    )
    tail_copy.start()
    for q in range(quads):
        stream_copy(q).start()
        gate_copy(q).start()
    out_copy = pltpu.make_async_copy(ow_hbm, ow, osem)
    out_copy.start()

    u = u_ref[...].astype(F32)
    scale = lax.rsqrt(jnp.mean(u * u, axis=-1, keepdims=True) + EPS)
    normed_ref[...] = (u * scale * ng_ref[...]).astype(BF16)
    write_masks(segc_ref, mask_ref, taps)

    tail_copy.wait()
    dt = dot(normed_ref[...], w[:, inner + conv : proj])
    dt_ref[...] = dt
    _, step, _, cumul = step_sizes(dt, dtb_ref, dl_ref, heads)
    step_ref[...] = step
    cum_ref[...] = cumul
    cumt_ref[...] = jnp.transpose(cumul)

    def conv_of(start, s):
        low = s.astype(BF16)
        stream_ref[:, cols(start)] = low
        total = conv_chunk(low.astype(F32), start, cw_ref, cb_ref, mask_ref, taps)
        return total * sigmoid(total)

    bc = conv_of(inner, dot(normed_ref[...], w[:, tail : tail + 2 * state]))
    keys = bc[:, :state].astype(BF16)
    queries = bc[:, state:].astype(BF16)
    i = lax.broadcasted_iota(jnp.int32, (length, length), 0)
    j = lax.broadcasted_iota(jnp.int32, (length, length), 1)
    within = (i >= j) & (segc_ref[:, :1] == segr_ref[:1, :])
    s_ref[...] = jnp.where(within, dot_nt(queries, keys), 0.0)

    def quad_step(q, squares):
        at = cols(q * WIDE)
        stream_copy(q).wait()
        gate_copy(q).wait()
        x = conv_of(q * WIDE, dot(normed_ref[...], w[:, cols(inner + q * WIDE)]))
        z = dot(normed_ref[...], w[:, at]).astype(BF16)
        gate_ref[:, at] = z
        z = z.astype(F32)
        cum_q = head_lanes(cum_ref[...], q, per)
        step_q = head_lanes(step_ref[...], q, per)
        ys = []
        for pair in range(per // 2):
            part = slice(pair * LANES, (pair + 1) * LANES)
            xdt = (x[:, part] * spread(step_q, 2 * pair, head_dim)).astype(BF16)
            got = []
            for k in range(2):
                h = 2 * pair + k
                col = cum_q[:, h : h + 1]
                row = cumt_ref[pl.ds(per * q + h, 1), :]
                top = jnp.exp2(jnp.minimum(col[:half] - row[:, :half], 0.0)) * s_ref[:half, :half]
                low = jnp.exp2(jnp.minimum(col[half:] - row, 0.0)) * s_ref[half:, :]
                got.append(
                    jnp.concatenate(
                        [dot(top.astype(BF16), xdt[:half]), dot(low.astype(BF16), xdt)], axis=0
                    )
                )
            lane = lax.broadcasted_iota(jnp.int32, (length, LANES), 1)
            ys.append(jnp.where(lane < head_dim, got[0], got[1]))
        y = jnp.concatenate(ys, axis=1)
        y_ref[:, at] = y
        gated = (y + sk_ref[:, at] * x) * (z * sigmoid(z))
        gated_ref[:, at] = gated
        return squares + fold(gated * gated)

    squares = lax.fori_loop(0, quads, quad_step, jnp.zeros((length, LANES), F32))
    scale2 = lax.rsqrt(jnp.sum(squares, axis=-1, keepdims=True) * (1.0 / inner) + EPS)

    def mixed_step(q, _):
        at = cols(q * WIDE)
        mixed_ref[:, at] = (gated_ref[:, at] * scale2 * gg_ref[:, at]).astype(BF16)
        return 0

    lax.fori_loop(0, quads, mixed_step, 0)
    out_copy.wait()

    def out_step(n, _):
        at = cols(n * WIDE)
        out_ref[:, at] = (u_ref[:, at].astype(F32) + dot(mixed_ref[...], ow[:, at])).astype(BF16)
        return 0

    lax.fori_loop(0, width // WIDE, out_step, 0)


def vmem():
    return pl.BlockSpec(memory_space=pltpu.VMEM)


def hbm():
    return pl.BlockSpec(memory_space=pl.ANY)


def forward(u, seg_col, seg_row, small, w, ow):
    length, width = u.shape
    ng, cw, cb, dtb, dl, sk, gg, heads = small
    inner, conv, taps = gg.shape[1], cb.shape[1], cw.shape[0]
    proj = w.shape[1]
    quads = inner // WIDE
    shape = jax.ShapeDtypeStruct
    return pl.pallas_call(
        functools.partial(forward_body, (length, width, inner, conv, heads, taps)),
        out_shape=(
            shape((length, width), BF16),
            shape((length, inner), BF16),
            shape((length, conv), BF16),
            shape((length, heads), F32),
            shape((length, inner), F32),
            shape((length, width), BF16),
            shape((length, inner), BF16),
        ),
        in_specs=[vmem()] * 10 + [hbm()] * 2,
        out_specs=[vmem()] * 7,
        scratch_shapes=[
            pltpu.VMEM((width, proj), BF16),
            pltpu.VMEM((inner, width), BF16),
            pltpu.VMEM((taps - 1, length, LANES), F32),
            pltpu.VMEM((length, length), F32),
            pltpu.VMEM((length, inner), F32),
            pltpu.VMEM((length, LANES), F32),
            pltpu.VMEM((length, LANES), F32),
            pltpu.VMEM((LANES, length), F32),
            pltpu.SemaphoreType.DMA((1 + 2 * quads,)),
            pltpu.SemaphoreType.DMA,
        ],
        compiler_params=pltpu.CompilerParams(vmem_limit_bytes=VMEM_BYTES),
        cost_estimate=pl.CostEstimate(
            flops=2 * length * (width * proj + inner * width + 2 * length * inner),
            bytes_accessed=2 * (width * proj + inner * width),
            transcendentals=length * (length * heads + 2 * inner),
        ),
        name="layer_forward",
    )(u, seg_col, seg_row, ng, cw, cb, dtb, dl, sk, gg, w, ow)


def backward_body(
    sizes, u_ref, g_ref, segc_ref, segr_ref, ng_ref, cw_ref, cb_ref, dtb_ref, dl_ref, sk_ref, gg_ref,
    gate_ref, stream_ref, dt_ref, y_ref, w_hbm, ow_hbm,
    dlow_ref, gin_ref, dng_ref, dcw_ref, dcb_ref, ddtb_ref, ddl_ref, dsk_ref, dgg_ref,
    w, ow, mask_ref, x_ref, slope_ref, dm_ref, st_ref, dst_ref, cum_ref, step_ref, cumt_ref, heads_ref, direct_ref,
    dn_ref, sem, osem,
):
    length, width, inner, conv, heads, taps = sizes
    state = (conv - inner) // 2
    head_dim = inner // heads
    per = WIDE // head_dim
    quads = inner // WIDE
    half = length // 2
    proj = w.shape[1]

    def out_copy(q):
        at = pl.ds(pl.multiple_of(q * WIDE, WIDE), WIDE)
        return pltpu.make_async_copy(ow_hbm.at[at, :], ow.at[at, :], osem.at[q])

    for q in range(quads):
        out_copy(q).start()
    in_copy = pltpu.make_async_copy(w_hbm, w, sem)
    in_copy.start()

    write_masks(segc_ref, mask_ref, taps)
    v, step, rate, cumul = step_sizes(dt_ref[...], dtb_ref, dl_ref, heads)
    step_ref[...] = step
    cum_ref[...] = cumul
    cumt_ref[...] = jnp.transpose(cumul)
    heads_ref[...] = jnp.zeros_like(heads_ref)
    direct_ref[...] = jnp.zeros_like(direct_ref)
    dst_ref[...] = jnp.zeros_like(dst_ref)

    def conv_of(start):
        at = cols(start)
        total = conv_chunk(stream_ref[:, at].astype(F32), start, cw_ref, cb_ref, mask_ref, taps)
        sig = sigmoid(total)
        x = total * sig
        x_ref[:, at] = x
        slope_ref[:, at] = sig + x * (1.0 - sig)
        return x

    def first_step(q, carry):
        squares, cross = carry
        at = cols(q * WIDE)
        out_copy(q).wait()
        dm = dot_nt(g_ref[...], ow[pl.ds(pl.multiple_of(q * WIDE, WIDE), WIDE), :])
        x = conv_of(q * WIDE)
        z = gate_ref[:, at].astype(F32)
        gated = (y_ref[:, at] + sk_ref[:, at] * x) * (z * sigmoid(z))
        dm_ref[:, at] = dm
        return squares + fold(gated * gated), cross + fold(gated * (dm * gg_ref[:, at]))

    zero = jnp.zeros((length, LANES), F32)
    squares, cross = lax.fori_loop(0, quads, first_step, (zero, zero))
    scale2 = lax.rsqrt(jnp.sum(squares, axis=-1, keepdims=True) * (1.0 / inner) + EPS)
    back2 = jnp.sum(cross, axis=-1, keepdims=True) * scale2 * scale2 * scale2 * (1.0 / inner)

    bc = conv_of(inner)
    keys = bc[:, :state].astype(BF16)
    queries = bc[:, state:].astype(BF16)
    j = lax.broadcasted_iota(jnp.int32, (length, length), 0)
    i = lax.broadcasted_iota(jnp.int32, (length, length), 1)
    within = (i >= j) & (segc_ref[:, :1] == segr_ref[:1, :])
    st_ref[...] = jnp.where(within, dot_nt(keys, queries), 0.0)

    def conv_back(start, d_conv):
        at = cols(start)
        d_total = d_conv * slope_ref[:, at]
        s = stream_ref[:, at].astype(F32)
        dcb_ref[:, at] = jnp.sum(d_total, axis=0, keepdims=True)
        dcw_ref[pl.ds(taps - 1, 1), at] = jnp.sum(d_total * s, axis=0, keepdims=True)
        d_stream = d_total * cw_ref[pl.ds(taps - 1, 1), at]
        for lag in range(1, taps):
            back = pltpu.roll(d_total * twice(mask_ref[lag - 1]), length - lag, 0)
            dcw_ref[pl.ds(taps - 1 - lag, 1), at] = jnp.sum(back * s, axis=0, keepdims=True)
            d_stream = d_stream + back * cw_ref[pl.ds(taps - 1 - lag, 1), at]
        dlow_ref[:, cols(inner + start)] = d_stream.astype(BF16)

    def second_step(q, _):
        at = cols(q * WIDE)
        x = x_ref[:, at]
        y = y_ref[:, at]
        dm = dm_ref[:, at]
        z = gate_ref[:, at].astype(F32)
        sig = sigmoid(z)
        zs = z * sig
        yf = y + sk_ref[:, at] * x
        gated = yf * zs
        scaled = dm * scale2
        dgg_ref[:, at] = jnp.sum(scaled * gated, axis=0, keepdims=True)
        d_gated = scaled * gg_ref[:, at] - gated * back2
        dy = d_gated * zs
        dlow_ref[:, at] = (d_gated * yf * (sig + zs * (1.0 - sig))).astype(BF16)
        dsk_ref[:, at] = jnp.sum(dy * x, axis=0, keepdims=True)
        dy_low = dy.astype(BF16)
        cum_q = head_lanes(cum_ref[...], q, per)
        step_q = head_lanes(step_ref[...], q, per)
        lane = lax.broadcasted_iota(jnp.int32, (length, LANES), 1)
        dst_top = jnp.zeros((half, length), F32)
        dst_low = jnp.zeros((half, half), F32)
        xdts, dxdts, steps = [], [], []
        for pair in range(per // 2):
            part = slice(pair * LANES, (pair + 1) * LANES)
            step_p = spread(step_q, 2 * pair, head_dim)
            xdt = (x[:, part] * step_p).astype(BF16)
            dyp = dy_low[:, part]
            got = []
            for k in range(2):
                h = 2 * pair + k
                mine = (lane < head_dim) if k == 0 else (lane >= head_dim)
                xm = jnp.where(mine, xdt.astype(F32), 0.0).astype(BF16)
                col = cum_q[:, h : h + 1]
                row = cumt_ref[pl.ds(per * q + h, 1), :]
                decay_top = jnp.exp2(jnp.minimum(row - col[:half], 0.0))
                decay_low = jnp.exp2(jnp.minimum(row[:, half:] - col[half:], 0.0))
                top = (decay_top * st_ref[:half, :]).astype(BF16)
                low = (decay_low * st_ref[half:, half:]).astype(BF16)
                got.append(jnp.concatenate([dot(top, dyp), dot(low, dyp[half:])], axis=0))
                dst_top = dst_top + dot_nt(xm[:half], dyp) * decay_top
                dst_low = dst_low + dot_nt(xm[half:], dyp[half:]) * decay_low
            xdts.append(xdt.astype(F32))
            steps.append(step_p)
            dxdts.append(jnp.where(lane < head_dim, got[0], got[1]))
        dst_ref[:half, :] += dst_top
        dst_ref[half:, half:] += dst_low
        xdt = jnp.concatenate(xdts, axis=1)
        dxdt = jnp.concatenate(dxdts, axis=1)
        steps = jnp.concatenate(steps, axis=1)
        pick_row = lax.broadcasted_iota(jnp.int32, (WIDE, LANES), 0)
        pick_col = lax.broadcasted_iota(jnp.int32, (WIDE, LANES), 1)
        pick = jnp.where(pick_row // head_dim + per * q == pick_col, 1.0, 0.0).astype(BF16)
        both = dy_low.astype(F32) * y - xdt * dxdt
        high = both.astype(BF16)
        rest = (both - high.astype(F32)).astype(BF16)
        heads_ref[...] += dot(high, pick) + dot(rest, pick)
        direct_ref[...] += dot((dxdt * x).astype(BF16), pick)
        conv_back(q * WIDE, dxdt * steps + sk_ref[:, at] * dy)
        return 0

    lax.fori_loop(0, quads, second_step, 0)

    d_scores = jnp.where(within, dst_ref[...], 0.0).astype(BF16)
    conv_back(inner, jnp.concatenate([dot(d_scores, queries), dot_tn(d_scores, keys)], axis=1))

    upper = jnp.where(i >= j, 1.0, 0.0)
    d_rate = lax.dot_general(
        upper, heads_ref[...], (((1,), (0,)), ((), ())), precision=HIGH, preferred_element_type=F32
    )
    ddl_ref[...] = jnp.sum(d_rate * rate, axis=0, keepdims=True)
    d_step = direct_ref[...] - d_rate * jnp.exp(dl_ref[...])
    d_dt = d_step / (1.0 + jnp.exp(-v))
    ddtb_ref[...] = jnp.sum(d_dt, axis=0, keepdims=True)
    d_dt_low = d_dt[:, :heads].astype(BF16)
    dlow_ref[:, inner + conv : proj] = d_dt_low

    in_copy.wait()
    u = u_ref[...].astype(F32)
    scale = lax.rsqrt(jnp.mean(u * u, axis=-1, keepdims=True) + EPS)

    def normed_step(n, _):
        rows = pl.ds(pl.multiple_of(n * WIDE, WIDE), WIDE)
        dn_ref[:, cols(n * WIDE)] = dot_nt(dlow_ref[:, : inner + conv], w[rows, : inner + conv]) + dot_nt(
            d_dt_low, w[rows, inner + conv : proj]
        )
        return 0

    lax.fori_loop(0, width // WIDE, normed_step, 0)
    dn = dn_ref[...]
    dng_ref[...] = jnp.sum(dn * u * scale, axis=0, keepdims=True)
    dn = dn * ng_ref[...]
    back = jnp.mean(dn * u, axis=-1, keepdims=True) * scale * scale * scale
    gin_ref[...] = g_ref[...].astype(F32) + dn * scale - u * back


def backward(u, g, seg_col, seg_row, small, kept, w, ow):
    length, width = u.shape
    ng, cw, cb, dtb, dl, sk, gg, heads = small
    inner, conv, taps = gg.shape[1], cb.shape[1], cw.shape[0]
    proj = w.shape[1]
    quads = inner // WIDE
    gate, stream, dt, y = kept
    shape = jax.ShapeDtypeStruct
    return pl.pallas_call(
        functools.partial(backward_body, (length, width, inner, conv, heads, taps)),
        out_shape=(
            shape((length, proj), BF16),
            shape((length, width), F32),
            shape((1, width), F32),
            shape((taps, conv), F32),
            shape((1, conv), F32),
            shape((1, LANES), F32),
            shape((1, LANES), F32),
            shape((1, inner), F32),
            shape((1, inner), F32),
        ),
        in_specs=[vmem()] * 15 + [hbm()] * 2,
        out_specs=[vmem()] * 9,
        scratch_shapes=[
            pltpu.VMEM((width, proj), BF16),
            pltpu.VMEM((inner, width), BF16),
            pltpu.VMEM((taps - 1, length, LANES), F32),
            pltpu.VMEM((length, conv), F32),
            pltpu.VMEM((length, conv), F32),
            pltpu.VMEM((length, inner), F32),
            pltpu.VMEM((length, length), F32),
            pltpu.VMEM((length, length), F32),
            pltpu.VMEM((length, LANES), F32),
            pltpu.VMEM((length, LANES), F32),
            pltpu.VMEM((LANES, length), F32),
            pltpu.VMEM((length, LANES), F32),
            pltpu.VMEM((length, LANES), F32),
            pltpu.VMEM((length, width), F32),
            pltpu.SemaphoreType.DMA,
            pltpu.SemaphoreType.DMA((quads,)),
        ],
        compiler_params=pltpu.CompilerParams(vmem_limit_bytes=VMEM_BYTES),
        cost_estimate=pl.CostEstimate(
            flops=2 * length * (width * proj + inner * width + 4 * length * inner),
            bytes_accessed=2 * (width * proj + inner * width) + 8 * length * proj,
            transcendentals=length * (length * heads + 4 * inner),
        ),
        name="layer_backward",
    )(u, g, seg_col, seg_row, ng, cw, cb, dtb, dl, sk, gg, gate, stream, dt, y, w, ow)


def flip(value, axis, distance):
    pairs = [(source, source ^ distance) for source in range(lax.axis_size(axis))]
    return lax.ppermute(value, axis, pairs)


def rotate(value, axis):
    count = lax.axis_size(axis)
    return lax.ppermute(value, axis, [(source, (source + 1) % count) for source in range(count)])


def distances(axis):
    found, d = [], 1
    while d < lax.axis_size(axis):
        found.append(d)
        d *= 2
    return found


def after(value, *others):
    return lax.optimization_barrier((value,) + others)[0]


def gather_rows(shard, start=None):
    ring, share = lax.axis_size("fsdp"), lax.axis_size("dp")
    z, q = lax.axis_index("fsdp"), lax.axis_index("dp")
    rows, columns = shard.shape[0] // share, shard.shape[1]
    own = shard.reshape(share, rows, columns)
    whole = jnp.broadcast_to(own[None], (ring, share, rows, columns))
    travelling = lax.dynamic_index_in_dim(own, q, 0, keepdims=False)
    if start is not None:
        travelling = after(travelling, start)
    for step in range(1, ring):
        travelling = rotate(travelling, "fsdp")
        source = lax.rem(z - step + ring, ring)
        parts = {0: travelling}
        for d in reversed(distances("dp")):
            parts.update({m | d: flip(v, "dp", d) for m, v in list(parts.items())})
        for m, v in parts.items():
            whole = lax.dynamic_update_slice(whole, v[None, None], (source, q ^ m, 0, 0))
    return whole, travelling


def reduce_rows(left, right):
    ring, share, rows, depth = left.shape
    z, q = lax.axis_index("fsdp"), lax.axis_index("dp")
    columns = right.shape[1]
    order = [lax.rem(z + 2 * ring - 1 - s, ring) for s in range(ring)]
    steps = distances("dp")

    def block(mask):
        mine = lax.dynamic_index_in_dim(left, q ^ mask, 1, keepdims=False)
        mine = jnp.concatenate([lax.dynamic_index_in_dim(mine, at, 0) for at in order], axis=0)
        product = jnp.dot(mine.reshape(ring * rows, depth), right, preferred_element_type=jnp.float32)
        return product.astype(BF16).reshape(ring, rows, columns)

    def total(level, mask):
        if level == 0:
            return block(mask)
        d = steps[level - 1]
        away = total(level - 1, mask | d)
        if level == len(steps):
            arrived = [flip(away[s], "dp", d) for s in range(ring)]
            here = total(level - 1, mask)
            return [here[s].astype(F32) + arrived[s].astype(F32) for s in range(ring)]
        arrived = flip(away, "dp", d)
        here = total(level - 1, mask)
        return (here.astype(F32) + arrived.astype(F32)).astype(BF16)

    parts = total(len(steps), 0)
    value = parts[0]
    for s in range(1, ring):
        value = rotate(value.astype(BF16), "fsdp").astype(F32) + parts[s]
    value = value.astype(BF16)
    owned = {0: value}
    for d in reversed(steps):
        owned.update({m | d: flip(v, "dp", d) for m, v in list(owned.items())})
    whole = jnp.zeros((share, rows, columns), F32)
    for m, v in owned.items():
        whole = lax.dynamic_update_slice(whole, v.astype(F32)[None], (q ^ m, 0, 0))
    return whole.reshape(1, share * rows, columns)


def shards(
    inputs,
    cotangent,
    segments,
    norm_gain,
    in_weight,
    conv_weight,
    conv_bias,
    dt_bias,
    decay_log,
    skip_gain,
    gate_gain,
    out_weight,
):
    first = lax.axis_index("section") == 0
    z = lax.axis_index("fsdp")
    ring, share = lax.axis_size("fsdp"), lax.axis_size("dp")
    length, width = inputs.shape[2], inputs.shape[3]
    taps = conv_weight.shape[1]
    heads = dt_bias.shape[1] * ring
    inner = gate_gain.shape[1] * ring
    head_dim = inner // heads

    pieces = (norm_gain[0], conv_bias[0], dt_bias[0], decay_log[0], skip_gain[0], gate_gain[0], conv_weight[0].reshape(-1))
    sizes = [piece.shape[0] for piece in pieces]
    packed = lax.all_gather(jnp.concatenate(pieces), "fsdp", axis=0).astype(F32)
    fields, start = [], 0
    for size in sizes:
        fields.append(packed[:, start : start + size])
        start += size
    taps_w = fields[6].reshape(ring, taps, -1).transpose(1, 0, 2).reshape(taps, -1)
    rows = [field.reshape(1, -1) for field in fields[:6]]

    def lanes(row):
        return jnp.pad(row, ((0, 0), (0, LANES - heads)))

    small = (
        rows[0],
        taps_w,
        rows[1],
        lanes(rows[2]),
        lanes(rows[3]),
        jnp.repeat(rows[4], head_dim, axis=1),
        rows[5],
        heads,
    )
    w, last = gather_rows(in_weight[0])
    w = w.reshape(width, -1)
    ow, _ = gather_rows(out_weight[0], last)
    ow = ow.reshape(inner, width)

    seg = segments[:, 0].astype(F32)
    seg_cols = [jnp.broadcast_to(seg[m][:, None], (length, LANES)) for m in range(2)]
    seg_rows = [jnp.broadcast_to(seg[m][None], (8, length)) for m in range(2)]
    pick = functools.partial(jnp.where, first)

    def to_second(value):
        return lax.ppermute(value, "section", [(0, 1)])

    def to_first(value):
        return lax.ppermute(value, "section", [(1, 0)])

    u_a, u_b = inputs[0, 0], inputs[1, 0]
    g_a, g_b = cotangent[0, 0], cotangent[1, 0]

    out0 = forward(u_a, seg_cols[0], seg_rows[0], small, w, ow)[0]
    u1 = pick(u_b, to_second(out0))
    seg1 = pick(seg_cols[1], seg_cols[0]), pick(seg_rows[1], seg_rows[0])
    out1, gate1, stream1, dt1, y1, normed1, mixed1 = forward(u1, *seg1, small, w, ow)
    stream_b = to_second(out1)
    kept1 = (gate1, stream1, dt1, y1)
    back2 = backward(u1, g_a, *seg1, small, kept1, w, ow)
    grad_a = to_first(back2[1].astype(BF16))
    u3 = pick(u_a, stream_b)
    seg3 = pick(seg_cols[0], seg_cols[1]), pick(seg_rows[0], seg_rows[1])
    out3, gate3, stream3, dt3, y3, normed3, mixed3 = forward(u3, *seg3, small, w, ow)
    g4 = pick(grad_a, g_b)
    back4 = backward(u3, g4, *seg3, small, (gate3, stream3, dt3, y3), w, ow)
    grad_b = to_first(back4[1].astype(BF16))
    back5 = backward(u1, grad_b, *seg1, small, kept1, w, ow)

    output = pick(to_first(out1), out3)
    input_grad = pick(back4[1], to_second(back5[1].astype(BF16)).astype(F32))

    def by_owner(value):
        depth, count = value.shape
        return value.T.reshape(ring, share, count // ring // share, depth)

    mixed_t = by_owner(jnp.concatenate([mixed3, mixed1], axis=0))
    normed_t = by_owner(jnp.concatenate([normed3, normed1], axis=0))
    out_grad = reduce_rows(mixed_t, jnp.concatenate([g4, pick(grad_b, g_a)], axis=0))
    in_grad = reduce_rows(normed_t, jnp.concatenate([back4[0], pick(back5[0], back2[0])], axis=0))

    def added(k):
        return back4[k] + pick(back5[k], back2[k])

    grads = (
        added(2),
        added(4),
        added(5)[:, :heads],
        added(6)[:, :heads],
        jnp.sum(added(7).reshape(heads, head_dim), axis=1)[None],
        added(8),
    )
    taps_grad = added(3).reshape(taps, ring, -1).transpose(1, 0, 2).reshape(ring, -1)
    packed = jnp.concatenate([grad.reshape(ring, -1) for grad in grads] + [taps_grad], axis=1)
    packed = lax.psum(packed, ("fsdp", "dp"))
    packed = lax.dynamic_index_in_dim(packed, z, 0)
    fields, start = [], 0
    for size in sizes:
        fields.append(packed[:, start : start + size])
        start += size
    return (
        output[None, None],
        input_grad[None, None],
        fields[0],
        in_grad,
        fields[6].reshape(1, taps, -1),
        fields[1],
        fields[2],
        fields[3],
        fields[4],
        fields[5],
        out_grad,
    )


def solution(mesh):
    spread_over = ("fsdp", "dp")
    row = P("section", "fsdp")
    matrix = P("section", "fsdp", None)
    tap = P("section", None, "fsdp")
    activation = P(None, spread_over, None, None)
    result = P("section", spread_over, None, None)
    return jax.shard_map(
        shards,
        mesh=mesh,
        in_specs=(activation, activation, P(None, spread_over, None), row, matrix, tap, row, row, row, row, row, matrix),
        out_specs=(result, result, row, matrix, tap, row, row, row, row, row, matrix),
        check_vma=False,
    )
```

```python
import functools

import jax
import jax.numpy as jnp
from jax import lax
from jax.experimental import pallas as pl
from jax.experimental.pallas import tpu as pltpu
from jax.sharding import PartitionSpec as P

EPS = 1e-05
LOG2E = 1.4426950408889634
HIGH = lax.Precision.HIGHEST
F32 = jnp.float32
BF16 = jnp.bfloat16
LANES = 128
WIDE = 256
VMEM_BYTES = 56 * 1024 * 1024


def sigmoid(v):
    return 0.5 * jnp.tanh(0.5 * v) + 0.5


def dot(a, b):
    return lax.dot_general(a, b, (((1,), (0,)), ((), ())), preferred_element_type=F32)


def dot_nt(a, b):
    return lax.dot_general(a, b, (((1,), (1,)), ((), ())), preferred_element_type=F32)


def dot_tn(a, b):
    return lax.dot_general(a, b, (((0,), (0,)), ((), ())), preferred_element_type=F32)


def twice(v):
    return jnp.concatenate([v, v], axis=1)


def fold(v):
    return v[:, :LANES] + v[:, LANES:]


def cols(start, width=WIDE):
    return pl.ds(pl.multiple_of(start, LANES), width)


def weight_copies(source, target, rows, sem, k):
    blocks, _, width = source.shape
    return [
        pltpu.make_async_copy(
            source.at[b, rows, :], target.at[rows, b * width : (b + 1) * width], sem.at[k, b]
        )
        for b in range(blocks)
    ]


def start(copies):
    for copy in copies:
        copy.start()


def wait(copies):
    for copy in copies:
        copy.wait()


def write_masks(segc_ref, mask_ref, taps):
    seg = segc_ref[...]
    row = lax.broadcasted_iota(jnp.int32, seg.shape, 0)
    for lag in range(1, taps):
        same = (pltpu.roll(seg, lag, 0) == seg) & (row >= lag)
        mask_ref[lag - 1] = jnp.where(same, 1.0, 0.0)


def conv_chunk(s, start, cw_ref, cb_ref, mask_ref, taps):
    at = cols(start)
    total = cb_ref[:, at] + s * cw_ref[pl.ds(taps - 1, 1), at]
    for lag in range(1, taps):
        shifted = pltpu.roll(s, lag, 0) * twice(mask_ref[lag - 1])
        total = total + shifted * cw_ref[pl.ds(taps - 1 - lag, 1), at]
    return total


def step_sizes(dt, dtb_ref, dl_ref, heads):
    length = dt.shape[0]
    pad = jnp.zeros((length, LANES - heads), F32)
    v = jnp.concatenate([dt, pad], axis=1) + dtb_ref[...]
    step = jnp.maximum(v, 0.0) + jnp.log1p(jnp.exp(-jnp.abs(v)))
    rate = -jnp.exp(dl_ref[...]) * step
    i = lax.broadcasted_iota(jnp.int32, (length, length), 0)
    j = lax.broadcasted_iota(jnp.int32, (length, length), 1)
    lower = jnp.where(i >= j, 1.0, 0.0)
    scaled = rate * LOG2E
    cumul = lax.dot_general(lower, scaled, (((1,), (0,)), ((), ())), precision=HIGH, preferred_element_type=F32)
    return v, step, rate, cumul


def head_lanes(v, quad, per):
    return pltpu.roll(v, lax.rem(LANES - per * quad, LANES), 1)


def spread(v, i0, head_dim):
    length = v.shape[0]
    lane = lax.broadcasted_iota(jnp.int32, (length, LANES), 1)
    a = jnp.broadcast_to(v[:, i0 : i0 + 1], (length, LANES))
    b = jnp.broadcast_to(v[:, i0 + 1 : i0 + 2], (length, LANES))
    return jnp.where(lane < head_dim, a, b)


def forward_body(
    sizes, u_ref, segc_ref, segr_ref, ng_ref, cw_ref, cb_ref, dtb_ref, dl_ref, sk_ref, gg_ref, w_hbm, ow_hbm,
    out_ref, gate_ref, stream_ref, dt_ref, y_ref, normed_ref, mixed_ref,
    w, ow, mask_ref, s_ref, gated_ref, cum_ref, step_ref, cumt_ref, sem, osem,
):
    length, width, inner, conv, heads, taps = sizes
    state = (conv - inner) // 2
    head_dim = inner // heads
    per = WIDE // head_dim
    quads = inner // WIDE
    half = length // 2
    proj = w.shape[0]
    tail = 2 * inner

    def copies(at, k):
        return weight_copies(w_hbm, w, at, sem, k)

    def stream_copy(q):
        return copies(cols(inner + q * WIDE), 1 + 2 * q)

    def gate_copy(q):
        return copies(cols(q * WIDE), 2 + 2 * q)

    tail_copy = copies(pl.ds(tail, proj - tail), 0)
    start(tail_copy)
    for q in range(quads):
        start(stream_copy(q))
        start(gate_copy(q))
    out_copy = pltpu.make_async_copy(ow_hbm, ow, osem)
    out_copy.start()

    u = u_ref[...].astype(F32)
    scale = lax.rsqrt(jnp.mean(u * u, axis=-1, keepdims=True) + EPS)
    normed_ref[...] = (u * scale * ng_ref[...]).astype(BF16)
    write_masks(segc_ref, mask_ref, taps)

    wait(tail_copy)
    dt = dot_nt(normed_ref[...], w[inner + conv : proj, :])
    dt_ref[...] = dt
    _, step, _, cumul = step_sizes(dt, dtb_ref, dl_ref, heads)
    step_ref[...] = step
    cum_ref[...] = cumul
    cumt_ref[...] = jnp.transpose(cumul)

    def conv_of(start, s):
        low = s.astype(BF16)
        stream_ref[:, cols(start)] = low
        total = conv_chunk(low.astype(F32), start, cw_ref, cb_ref, mask_ref, taps)
        return total * sigmoid(total)

    bc = conv_of(inner, dot_nt(normed_ref[...], w[tail : tail + 2 * state, :]))
    keys = bc[:, :state].astype(BF16)
    queries = bc[:, state:].astype(BF16)
    i = lax.broadcasted_iota(jnp.int32, (length, length), 0)
    j = lax.broadcasted_iota(jnp.int32, (length, length), 1)
    within = (i >= j) & (segc_ref[:, :1] == segr_ref[:1, :])
    s_ref[...] = jnp.where(within, dot_nt(queries, keys), 0.0)

    def quad_step(q, squares):
        at = cols(q * WIDE)
        wait(stream_copy(q))
        wait(gate_copy(q))
        x = conv_of(q * WIDE, dot_nt(normed_ref[...], w[cols(inner + q * WIDE), :]))
        z = dot_nt(normed_ref[...], w[at, :]).astype(BF16)
        gate_ref[:, at] = z
        z = z.astype(F32)
        cum_q = head_lanes(cum_ref[...], q, per)
        step_q = head_lanes(step_ref[...], q, per)
        ys = []
        for pair in range(per // 2):
            part = slice(pair * LANES, (pair + 1) * LANES)
            xdt = (x[:, part] * spread(step_q, 2 * pair, head_dim)).astype(BF16)
            got = []
            for k in range(2):
                h = 2 * pair + k
                col = cum_q[:, h : h + 1]
                row = cumt_ref[pl.ds(per * q + h, 1), :]
                top = jnp.exp2(jnp.minimum(col[:half] - row[:, :half], 0.0)) * s_ref[:half, :half]
                low = jnp.exp2(jnp.minimum(col[half:] - row, 0.0)) * s_ref[half:, :]
                got.append(
                    jnp.concatenate(
                        [dot(top.astype(BF16), xdt[:half]), dot(low.astype(BF16), xdt)], axis=0
                    )
                )
            lane = lax.broadcasted_iota(jnp.int32, (length, LANES), 1)
            ys.append(jnp.where(lane < head_dim, got[0], got[1]))
        y = jnp.concatenate(ys, axis=1)
        y_ref[:, at] = y
        gated = (y + sk_ref[:, at] * x) * (z * sigmoid(z))
        gated_ref[:, at] = gated
        return squares + fold(gated * gated)

    squares = lax.fori_loop(0, quads, quad_step, jnp.zeros((length, LANES), F32))
    scale2 = lax.rsqrt(jnp.sum(squares, axis=-1, keepdims=True) * (1.0 / inner) + EPS)

    def mixed_step(q, _):
        at = cols(q * WIDE)
        mixed_ref[:, at] = (gated_ref[:, at] * scale2 * gg_ref[:, at]).astype(BF16)
        return 0

    lax.fori_loop(0, quads, mixed_step, 0)
    out_copy.wait()

    def out_step(n, _):
        at = cols(n * WIDE)
        out_ref[:, at] = (u_ref[:, at].astype(F32) + dot(mixed_ref[...], ow[:, at])).astype(BF16)
        return 0

    lax.fori_loop(0, width // WIDE, out_step, 0)


def vmem():
    return pl.BlockSpec(memory_space=pltpu.VMEM)


def hbm():
    return pl.BlockSpec(memory_space=pl.ANY)


def forward(u, seg_col, seg_row, small, w, ow, keep=True):
    length, width = u.shape
    ng, cw, cb, dtb, dl, sk, gg, heads = small
    inner, conv, taps = gg.shape[1], cb.shape[1], cw.shape[0]
    blocks, proj = w.shape[:2]
    quads = inner // WIDE
    saved = (
        ((length, inner), BF16),
        ((length, conv), BF16),
        ((length, heads), F32),
        ((length, inner), F32),
        ((length, width), BF16),
        ((length, inner), BF16),
    )
    outs = (((length, width), BF16),) + (saved if keep else ())
    return pl.pallas_call(
        functools.partial(forward_body, (length, width, inner, conv, heads, taps)),
        out_shape=tuple(jax.ShapeDtypeStruct(*out) for out in outs),
        in_specs=[vmem()] * 10 + [hbm()] * 2,
        out_specs=[vmem()] * len(outs),
        scratch_shapes=([] if keep else [pltpu.VMEM(*one) for one in saved])
        + [
            pltpu.VMEM((proj, width), BF16),
            pltpu.VMEM((inner, width), BF16),
            pltpu.VMEM((taps - 1, length, LANES), F32),
            pltpu.VMEM((length, length), F32),
            pltpu.VMEM((length, inner), F32),
            pltpu.VMEM((length, LANES), F32),
            pltpu.VMEM((length, LANES), F32),
            pltpu.VMEM((LANES, length), F32),
            pltpu.SemaphoreType.DMA((1 + 2 * quads, blocks)),
            pltpu.SemaphoreType.DMA,
        ],
        compiler_params=pltpu.CompilerParams(vmem_limit_bytes=VMEM_BYTES),
        cost_estimate=pl.CostEstimate(
            flops=2 * length * (width * proj + inner * width + 2 * length * inner),
            bytes_accessed=2 * (width * proj + inner * width),
            transcendentals=length * (length * heads + 2 * inner),
        ),
        name="layer_forward",
    )(u, seg_col, seg_row, ng, cw, cb, dtb, dl, sk, gg, w, ow)


def backward_body(
    sizes, u_ref, g_ref, segc_ref, segr_ref, ng_ref, cw_ref, cb_ref, dtb_ref, dl_ref, sk_ref, gg_ref,
    gate_ref, stream_ref, dt_ref, y_ref, w_hbm, ow_hbm,
    dlowt_ref, gin_ref, dng_ref, dcw_ref, dcb_ref, ddtb_ref, ddl_ref, dsk_ref, dgg_ref,
    w, ow, mask_ref, x_ref, slope_ref, dm_ref, st_ref, dst_ref, cum_ref, step_ref, cumt_ref, heads_ref, direct_ref,
    rows_ref, dn_ref, dlow_ref, sem, osem,
):
    length, width, inner, conv, heads, taps = sizes
    state = (conv - inner) // 2
    head_dim = inner // heads
    per = WIDE // head_dim
    quads = inner // WIDE
    half = length // 2
    proj = w.shape[0]

    def out_copy(q):
        at = pl.ds(pl.multiple_of(q * WIDE, WIDE), WIDE)
        return pltpu.make_async_copy(ow_hbm.at[at, :], ow.at[at, :], osem.at[q])

    for q in range(quads):
        out_copy(q).start()
    in_copy = weight_copies(w_hbm, w, pl.ds(0, proj), sem, 0)
    start(in_copy)

    write_masks(segc_ref, mask_ref, taps)
    v, step, rate, cumul = step_sizes(dt_ref[...], dtb_ref, dl_ref, heads)
    step_ref[...] = step
    cum_ref[...] = cumul
    cumt_ref[...] = jnp.transpose(cumul)
    heads_ref[...] = jnp.zeros_like(heads_ref)
    direct_ref[...] = jnp.zeros_like(direct_ref)
    dst_ref[...] = jnp.zeros_like(dst_ref)
    rows_ref[...] = jnp.zeros_like(rows_ref)

    def conv_of(start):
        at = cols(start)
        total = conv_chunk(stream_ref[:, at].astype(F32), start, cw_ref, cb_ref, mask_ref, taps)
        sig = sigmoid(total)
        x = total * sig
        x_ref[:, at] = x
        slope_ref[:, at] = sig + x * (1.0 - sig)
        return x

    def first_step(q, carry):
        squares, cross = carry
        at = cols(q * WIDE)
        out_copy(q).wait()
        dm = dot_nt(g_ref[...], ow[pl.ds(pl.multiple_of(q * WIDE, WIDE), WIDE), :])
        x = conv_of(q * WIDE)
        z = gate_ref[:, at].astype(F32)
        gated = (y_ref[:, at] + sk_ref[:, at] * x) * (z * sigmoid(z))
        dm_ref[:, at] = dm
        return squares + fold(gated * gated), cross + fold(gated * (dm * gg_ref[:, at]))

    zero = jnp.zeros((length, LANES), F32)
    squares, cross = lax.fori_loop(0, quads, first_step, (zero, zero))
    scale2 = lax.rsqrt(jnp.sum(squares, axis=-1, keepdims=True) * (1.0 / inner) + EPS)
    back2 = jnp.sum(cross, axis=-1, keepdims=True) * scale2 * scale2 * scale2 * (1.0 / inner)

    bc = conv_of(inner)
    keys = bc[:, :state].astype(BF16)
    queries = bc[:, state:].astype(BF16)
    j = lax.broadcasted_iota(jnp.int32, (length, length), 0)
    i = lax.broadcasted_iota(jnp.int32, (length, length), 1)
    within = (i >= j) & (segc_ref[:, :1] == segr_ref[:1, :])
    st_ref[...] = jnp.where(within, dot_nt(keys, queries), 0.0)

    def write_low(at, value):
        low = value.astype(BF16)
        dlow_ref[:, at] = low
        dlowt_ref[at, :] = jnp.transpose(low)

    def conv_back(start, d_conv):
        at = cols(start)
        d_total = d_conv * slope_ref[:, at]
        s = stream_ref[:, at].astype(F32)
        dcb_ref[:, at] = jnp.sum(d_total, axis=0, keepdims=True)
        dcw_ref[pl.ds(taps - 1, 1), at] = jnp.sum(d_total * s, axis=0, keepdims=True)
        d_stream = d_total * cw_ref[pl.ds(taps - 1, 1), at]
        for lag in range(1, taps):
            back = pltpu.roll(d_total * twice(mask_ref[lag - 1]), length - lag, 0)
            dcw_ref[pl.ds(taps - 1 - lag, 1), at] = jnp.sum(back * s, axis=0, keepdims=True)
            d_stream = d_stream + back * cw_ref[pl.ds(taps - 1 - lag, 1), at]
        write_low(cols(inner + start), d_stream)

    def second_step(q, _):
        at = cols(q * WIDE)
        x = x_ref[:, at]
        y = y_ref[:, at]
        dm = dm_ref[:, at]
        z = gate_ref[:, at].astype(F32)
        sig = sigmoid(z)
        zs = z * sig
        yf = y + sk_ref[:, at] * x
        gated = yf * zs
        scaled = dm * scale2
        dgg_ref[:, at] = jnp.sum(scaled * gated, axis=0, keepdims=True)
        d_gated = scaled * gg_ref[:, at] - gated * back2
        dy = d_gated * zs
        write_low(at, d_gated * yf * (sig + zs * (1.0 - sig)))
        dsk_ref[:, at] = jnp.sum(dy * x, axis=0, keepdims=True)
        dy_low = dy.astype(BF16)
        cum_q = head_lanes(cum_ref[...], q, per)
        step_q = head_lanes(step_ref[...], q, per)
        lane = lax.broadcasted_iota(jnp.int32, (length, LANES), 1)
        dst_top = jnp.zeros((half, length), F32)
        dst_low = jnp.zeros((half, half), F32)
        xdts, dxdts, steps = [], [], []
        for pair in range(per // 2):
            part = slice(pair * LANES, (pair + 1) * LANES)
            step_p = spread(step_q, 2 * pair, head_dim)
            xdt = (x[:, part] * step_p).astype(BF16)
            dyp = dy_low[:, part]
            got = []
            for k in range(2):
                h = 2 * pair + k
                mine = (lane < head_dim) if k == 0 else (lane >= head_dim)
                xm = jnp.where(mine, xdt.astype(F32), 0.0).astype(BF16)
                col = cum_q[:, h : h + 1]
                row = cumt_ref[pl.ds(per * q + h, 1), :]
                decay_top = jnp.exp2(jnp.minimum(row - col[:half], 0.0))
                decay_low = jnp.exp2(jnp.minimum(row[:, half:] - col[half:], 0.0))
                top = (decay_top * st_ref[:half, :]).astype(BF16)
                low = (decay_low * st_ref[half:, half:]).astype(BF16)
                got.append(jnp.concatenate([dot(top, dyp), dot(low, dyp[half:])], axis=0))
                dm_top = dot_nt(xm[:half], dyp)
                dm_low = dot_nt(xm[half:], dyp[half:])
                dst_top = dst_top + dm_top * decay_top
                dst_low = dst_low + dm_low * decay_low
                sums = jnp.sum(dm_top * top.astype(F32), axis=0, keepdims=True)
                more = jnp.sum(dm_low * low.astype(F32), axis=0, keepdims=True)
                rows_ref[pl.ds(per * q + h, 1), :] = jnp.concatenate([sums[:, :half], sums[:, half:] + more], axis=1)
            xdts.append(xdt.astype(F32))
            steps.append(step_p)
            dxdts.append(jnp.where(lane < head_dim, got[0], got[1]))
        dst_ref[:half, :] += dst_top
        dst_ref[half:, half:] += dst_low
        xdt = jnp.concatenate(xdts, axis=1)
        dxdt = jnp.concatenate(dxdts, axis=1)
        steps = jnp.concatenate(steps, axis=1)
        pick_row = lax.broadcasted_iota(jnp.int32, (WIDE, LANES), 0)
        pick_col = lax.broadcasted_iota(jnp.int32, (WIDE, LANES), 1)
        pick = jnp.where(pick_row // head_dim + per * q == pick_col, 1.0, 0.0).astype(BF16)
        both = xdt * dxdt
        high = both.astype(BF16)
        rest = both - high.astype(F32)
        middle = rest.astype(BF16)
        low = (rest - middle.astype(F32)).astype(BF16)
        heads_ref[...] += dot(high, pick) + (dot(middle, pick) + dot(low, pick))
        direct_ref[...] += dot((dxdt * x).astype(BF16), pick)
        conv_back(q * WIDE, dxdt * steps + sk_ref[:, at] * dy)
        return 0

    lax.fori_loop(0, quads, second_step, 0)

    d_scores = jnp.where(within, dst_ref[...], 0.0).astype(BF16)
    conv_back(inner, jnp.concatenate([dot(d_scores, queries), dot_tn(d_scores, keys)], axis=1))

    upper = jnp.where(within, 1.0, 0.0)
    d_rate = lax.dot_general(
        upper, jnp.transpose(rows_ref[...]) - heads_ref[...], (((1,), (0,)), ((), ())), precision=HIGH, preferred_element_type=F32
    )
    ddl_ref[...] = jnp.sum(d_rate * rate, axis=0, keepdims=True)
    d_step = direct_ref[...] - d_rate * jnp.exp(dl_ref[...])
    d_dt = d_step / (1.0 + jnp.exp(-v))
    ddtb_ref[...] = jnp.sum(d_dt, axis=0, keepdims=True)
    d_dt_low = d_dt[:, :heads].astype(BF16)
    dlowt_ref[inner + conv : proj, :] = jnp.transpose(d_dt)[:heads].astype(BF16)

    wait(in_copy)
    u = u_ref[...].astype(F32)
    scale = lax.rsqrt(jnp.mean(u * u, axis=-1, keepdims=True) + EPS)

    def normed_step(n, _):
        at = cols(n * WIDE)
        dn_ref[:, at] = dot(dlow_ref[...], w[: inner + conv, at]) + dot(d_dt_low, w[inner + conv : proj, at])
        return 0

    lax.fori_loop(0, width // WIDE, normed_step, 0)
    dn = dn_ref[...]
    dng_ref[...] = jnp.sum(dn * u * scale, axis=0, keepdims=True)
    dn = dn * ng_ref[...]
    back = jnp.mean(dn * u, axis=-1, keepdims=True) * scale * scale * scale
    gin_ref[...] = g_ref[...].astype(F32) + dn * scale - u * back


def backward(u, g, seg_col, seg_row, small, kept, w, ow):
    length, width = u.shape
    ng, cw, cb, dtb, dl, sk, gg, heads = small
    inner, conv, taps = gg.shape[1], cb.shape[1], cw.shape[0]
    proj = w.shape[1]
    blocks = w.shape[0]
    quads = inner // WIDE
    gate, stream, dt, y = kept
    shape = jax.ShapeDtypeStruct
    return pl.pallas_call(
        functools.partial(backward_body, (length, width, inner, conv, heads, taps)),
        out_shape=(
            shape((proj, length), BF16),
            shape((length, width), F32),
            shape((1, width), F32),
            shape((taps, conv), F32),
            shape((1, conv), F32),
            shape((1, LANES), F32),
            shape((1, LANES), F32),
            shape((1, inner), F32),
            shape((1, inner), F32),
        ),
        in_specs=[vmem()] * 15 + [hbm()] * 2,
        out_specs=[vmem()] * 9,
        scratch_shapes=[
            pltpu.VMEM((proj, width), BF16),
            pltpu.VMEM((inner, width), BF16),
            pltpu.VMEM((taps - 1, length, LANES), F32),
            pltpu.VMEM((length, conv), F32),
            pltpu.VMEM((length, conv), F32),
            pltpu.VMEM((length, inner), F32),
            pltpu.VMEM((length, length), F32),
            pltpu.VMEM((length, length), F32),
            pltpu.VMEM((length, LANES), F32),
            pltpu.VMEM((length, LANES), F32),
            pltpu.VMEM((LANES, length), F32),
            pltpu.VMEM((length, LANES), F32),
            pltpu.VMEM((length, LANES), F32),
            pltpu.VMEM((LANES, length), F32),
            pltpu.VMEM((length, width), F32),
            pltpu.VMEM((length, inner + conv), BF16),
            pltpu.SemaphoreType.DMA((1, blocks)),
            pltpu.SemaphoreType.DMA((quads,)),
        ],
        compiler_params=pltpu.CompilerParams(vmem_limit_bytes=VMEM_BYTES),
        cost_estimate=pl.CostEstimate(
            flops=2 * length * (width * proj + inner * width + 4 * length * inner),
            bytes_accessed=2 * (width * proj + inner * width) + 8 * length * proj,
            transcendentals=length * (length * heads + 4 * inner),
        ),
        name="layer_backward",
    )(u, g, seg_col, seg_row, ng, cw, cb, dtb, dl, sk, gg, gate, stream, dt, y, w, ow)


def flip(value, axis, distance):
    pairs = [(source, source ^ distance) for source in range(lax.axis_size(axis))]
    return lax.ppermute(value, axis, pairs)


def rotate(value, axis):
    count = lax.axis_size(axis)
    return lax.ppermute(value, axis, [(source, (source + 1) % count) for source in range(count)])


def distances(axis):
    found, d = [], 1
    while d < lax.axis_size(axis):
        found.append(d)
        d *= 2
    return found


def after(value, *others):
    return lax.optimization_barrier((value,) + others)[0]


def blank(shape, dtype):
    return pl.pallas_call(
        lambda out: None, out_shape=jax.ShapeDtypeStruct(shape, dtype), out_specs=hbm(), name="blank"
    )()


def gather_blocks(own):
    ring, share = lax.axis_size("fsdp"), lax.axis_size("dp")
    z, q = lax.axis_index("fsdp"), lax.axis_index("dp")
    travelling = lax.dynamic_index_in_dim(own, q, 0, keepdims=False)
    whole = lax.dynamic_update_slice(blank((ring,) + own.shape, own.dtype), own[None], (z, 0, 0, 0))
    for step in range(1, ring):
        travelling = rotate(travelling, "fsdp")
        source = lax.rem(z - step + ring, ring)
        parts = {0: travelling}
        for d in reversed(distances("dp")):
            parts.update({m | d: flip(v, "dp", d) for m, v in list(parts.items())})
        for m, v in parts.items():
            whole = lax.dynamic_update_slice(whole, v[None, None], (source, q ^ m, 0, 0))
    return whole


def gather_small(row):
    ring, z = lax.axis_size("fsdp"), lax.axis_index("fsdp")
    rows = [row]
    for _ in range(1, ring):
        rows.append(rotate(rows[-1], "fsdp"))
    place = jnp.arange(ring)
    chosen = (lax.rem(z - place[:, None] + ring, ring) == place[None, :]).astype(row.dtype)
    return jnp.dot(chosen, jnp.concatenate(rows, axis=0), preferred_element_type=F32)


def ring_places():
    ring, z = lax.axis_size("fsdp"), lax.axis_index("fsdp")
    return [lax.rem(z + 2 * ring - 1 - s, ring) for s in range(ring)]


def add(a, b):
    return a.astype(F32) + b.astype(F32)


def sum_far(near, level, mask):
    if level == 0:
        return near[mask]
    d = distances("dp")[level]
    arrived = [flip(v, "dp", d) for v in sum_far(near, level - 1, mask | d)]
    return [add(a, b).astype(BF16) for a, b in zip(sum_far(near, level - 1, mask), arrived)]


def sum_ring(parts):
    value = parts[0]
    for s in range(1, len(parts)):
        value = add(rotate(value, "fsdp"), parts[s]).astype(BF16)
    return value


def share_out(value):
    q = lax.axis_index("dp")
    owned = {0: value}
    for d in reversed(distances("dp")):
        owned.update({m | d: flip(v, "dp", d) for m, v in list(owned.items())})
    whole = blank((lax.axis_size("dp"),) + value.shape, F32)
    for m, v in owned.items():
        whole = lax.dynamic_update_slice(whole, v.astype(F32)[None], (q ^ m, 0, 0))
    return whole.reshape(-1, value.shape[1])


def far_masks():
    return range(0, lax.axis_size("dp"), 2)


def rows_near(left, right):
    ring, _, rows, depth = left.shape
    q, order = lax.axis_index("dp"), ring_places()

    def together(mask):
        mine = lax.dynamic_index_in_dim(left, q ^ mask, 1, keepdims=False)
        mine = jnp.concatenate([lax.dynamic_index_in_dim(mine, at, 0) for at in order], axis=0)
        product = jnp.dot(mine.reshape(ring * rows, depth), right, preferred_element_type=F32)
        return product.astype(BF16).reshape(ring, rows, -1)

    near = {}
    for mask in reversed(far_masks()):
        arrived = flip(together(mask | 1), "dp", 1)
        both = add(together(mask), arrived).astype(BF16)
        near[mask] = [both[s] for s in range(ring)]
    return near


def columns_near(lefts, right):
    ring, depth = lax.axis_size("fsdp"), right.shape[0]
    q, order = lax.axis_index("dp"), ring_places()
    block = right.shape[1] // ring
    rights = [lax.dynamic_slice(right, (0, at * block), (depth, block)) for at in order]
    every = jnp.concatenate(rights, axis=1)

    def left(mask):
        return jnp.concatenate([lax.dynamic_index_in_dim(one, q ^ mask, 0, keepdims=False) for one in lefts], axis=1)

    near = {}
    for mask in reversed(far_masks()):
        away = jnp.dot(left(mask | 1), every, preferred_element_type=F32).astype(BF16)
        arrived = flip(away, "dp", 1)
        here = left(mask)
        near[mask] = [
            add(jnp.dot(here, rights[s], preferred_element_type=F32), arrived[:, s * block : (s + 1) * block]).astype(BF16)
            for s in range(ring)
        ]
    return near


def finish(near):
    return share_out(sum_ring(sum_far(near, len(distances("dp")) - 1, 0)))


def sum_small(rows):
    for d in distances("dp"):
        rows = rows + flip(rows, "dp", d)
    parts = [lax.dynamic_index_in_dim(rows, at, 0) for at in ring_places()]
    value = parts[0]
    for part in parts[1:]:
        value = rotate(value, "fsdp") + part
    return value


def shards(
    inputs,
    cotangent,
    segments,
    norm_gain,
    in_weight,
    conv_weight,
    conv_bias,
    dt_bias,
    decay_log,
    skip_gain,
    gate_gain,
    out_weight,
):
    first = lax.axis_index("section") == 0
    z = lax.axis_index("fsdp")
    ring, share = lax.axis_size("fsdp"), lax.axis_size("dp")
    length, width = inputs.shape[2], inputs.shape[3]
    taps = conv_weight.shape[1]
    heads = dt_bias.shape[1] * ring
    inner = gate_gain.shape[1] * ring
    head_dim = inner // heads

    pieces = (norm_gain[0], conv_bias[0], dt_bias[0], decay_log[0], skip_gain[0], gate_gain[0], conv_weight[0].reshape(-1))
    sizes = [piece.shape[0] for piece in pieces]
    packed = gather_small(jnp.concatenate(pieces)[None])
    fields, start = [], 0
    for size in sizes:
        fields.append(packed[:, start : start + size])
        start += size
    taps_w = fields[6].reshape(ring, taps, -1).transpose(1, 0, 2).reshape(taps, -1)
    rows = [field.reshape(1, -1) for field in fields[:6]]

    def lanes(row):
        return jnp.pad(row, ((0, 0), (0, LANES - heads)))

    small = (
        rows[0],
        taps_w,
        rows[1],
        lanes(rows[2]),
        lanes(rows[3]),
        jnp.repeat(rows[4], head_dim, axis=1),
        rows[5],
        heads,
    )
    proj = in_weight.shape[2]
    w = gather_blocks(in_weight[0].T.reshape(share, proj // share, -1)).reshape(ring, proj, -1)
    ow = gather_blocks(out_weight[0].reshape(share, -1, width)).reshape(inner, width)

    seg = segments[:, 0].astype(F32)
    seg_cols = [jnp.broadcast_to(seg[m][:, None], (length, LANES)) for m in range(2)]
    seg_rows = [jnp.broadcast_to(seg[m][None], (8, length)) for m in range(2)]
    pick = functools.partial(jnp.where, first)

    def to_second(value):
        return lax.ppermute(value, "section", [(0, 1)])

    def to_first(value):
        return lax.ppermute(value, "section", [(1, 0)])

    u_a, u_b = inputs[0, 0], inputs[1, 0]
    g_a, g_b = cotangent[0, 0], cotangent[1, 0]

    out0 = forward(u_a, seg_cols[0], seg_rows[0], small, w, ow, keep=False)[0]
    u1 = pick(u_b, to_second(out0))
    seg1 = pick(seg_cols[1], seg_cols[0]), pick(seg_rows[1], seg_rows[0])
    out1, gate1, stream1, dt1, y1, normed1, mixed1 = forward(u1, *seg1, small, w, ow)
    stream_b = to_second(out1)
    kept1 = (gate1, stream1, dt1, y1)
    back2 = backward(u1, g_a, *seg1, small, kept1, w, ow)
    grad_a = to_first(back2[1].astype(BF16))
    u3 = pick(u_a, stream_b)
    seg3 = pick(seg_cols[0], seg_cols[1]), pick(seg_rows[0], seg_rows[1])
    out3, gate3, stream3, dt3, y3, normed3, mixed3 = forward(u3, *seg3, small, w, ow)
    g4 = pick(grad_a, g_b)
    back4 = backward(u3, g4, *seg3, small, (gate3, stream3, dt3, y3), w, ow)
    grad_b = to_first(back4[1].astype(BF16))

    mixed_t = jnp.concatenate([mixed3, mixed1], axis=0).T.reshape(ring, share, -1, 2 * length)
    near_out = rows_near(mixed_t, jnp.concatenate([g4, pick(grad_b, g_a)], axis=0))
    ahead = [v for parts in near_out.values() for v in parts]
    back5 = backward(after(u1, *ahead), grad_b, *seg1, small, kept1, w, ow)

    output = pick(to_first(out1), out3)
    input_grad = pick(back4[1], to_second(back5[1].astype(BF16)).astype(F32))
    normed = jnp.concatenate([normed3, normed1], axis=0)
    lefts = [back4[0], pick(back5[0], back2[0])]
    near_in = columns_near([left.reshape(share, -1, length) for left in lefts], normed)
    in_grad = finish(near_in).T[None]
    out_grad = finish(near_out)[None]

    def added(k):
        return back4[k] + pick(back5[k], back2[k])

    grads = (
        added(2),
        added(4),
        added(5)[:, :heads],
        added(6)[:, :heads],
        jnp.sum(added(7).reshape(heads, head_dim), axis=1)[None],
        added(8),
    )
    taps_grad = added(3).reshape(taps, ring, -1).transpose(1, 0, 2).reshape(ring, -1)
    packed = jnp.concatenate([grad.reshape(ring, -1) for grad in grads] + [taps_grad], axis=1)
    packed = sum_small(packed)
    fields, start = [], 0
    for size in sizes:
        fields.append(packed[:, start : start + size])
        start += size
    return (
        output[None, None],
        input_grad[None, None],
        fields[0],
        in_grad,
        fields[6].reshape(1, taps, -1),
        fields[1],
        fields[2],
        fields[3],
        fields[4],
        fields[5],
        out_grad,
    )


def solution(mesh):
    spread_over = ("fsdp", "dp")
    row = P("section", "fsdp")
    matrix = P("section", "fsdp", None)
    tap = P("section", None, "fsdp")
    activation = P(None, spread_over, None, None)
    result = P("section", spread_over, None, None)
    return jax.shard_map(
        shards,
        mesh=mesh,
        in_specs=(activation, activation, P(None, spread_over, None), row, matrix, tap, row, row, row, row, row, matrix),
        out_specs=(result, result, row, matrix, tap, row, row, row, row, row, matrix),
        check_vma=False,
    )
```

```python
import functools

import jax
import jax.numpy as jnp
from jax import lax
from jax.experimental import pallas as pl
from jax.experimental.pallas import tpu as pltpu
from jax.sharding import PartitionSpec as P

EPS = 1e-05
LOG2E = 1.4426950408889634
HIGH = lax.Precision.HIGHEST
F32 = jnp.float32
BF16 = jnp.bfloat16
LANES = 128
WIDE = 256
VMEM_BYTES = 56 * 1024 * 1024


def sigmoid(v):
    return 0.5 * jnp.tanh(0.5 * v) + 0.5


def dot(a, b):
    return lax.dot_general(a, b, (((1,), (0,)), ((), ())), preferred_element_type=F32)


def dot_nt(a, b):
    return lax.dot_general(a, b, (((1,), (1,)), ((), ())), preferred_element_type=F32)


def dot_tn(a, b):
    return lax.dot_general(a, b, (((0,), (0,)), ((), ())), preferred_element_type=F32)


def twice(v):
    return jnp.concatenate([v, v], axis=1)


def fold(v):
    return v[:, :LANES] + v[:, LANES:]


def cols(start, width=WIDE):
    return pl.ds(pl.multiple_of(start, LANES), width)


def weight_copies(source, target, rows, sem, k):
    blocks, _, width = source.shape
    return [
        pltpu.make_async_copy(
            source.at[b, rows, :], target.at[rows, b * width : (b + 1) * width], sem.at[k, b]
        )
        for b in range(blocks)
    ]


def start(copies):
    for copy in copies:
        copy.start()


def wait(copies):
    for copy in copies:
        copy.wait()


def small_rows(small_ref, width, inner, conv, taps):
    row = lambda k, size: small_ref.at[taps + k : taps + k + 1, :size]
    return (
        row(0, width),
        small_ref.at[:taps],
        row(1, conv),
        row(2, LANES),
        row(3, LANES),
        row(4, inner),
        row(5, inner),
    )


def column_of(segr_ref):
    row = jnp.broadcast_to(segr_ref[:1, :], (LANES, segr_ref.shape[1]))
    return jnp.transpose(row)


def write_masks(segc_ref, mask_ref, taps):
    seg = segc_ref[...]
    row = lax.broadcasted_iota(jnp.int32, seg.shape, 0)
    for lag in range(1, taps):
        same = (pltpu.roll(seg, lag, 0) == seg) & (row >= lag)
        mask_ref[lag - 1] = jnp.where(same, 1.0, 0.0)


def conv_chunk(s, start, cw_ref, cb_ref, mask_ref, taps):
    at = cols(start)
    total = cb_ref[:, at] + s * cw_ref[pl.ds(taps - 1, 1), at]
    for lag in range(1, taps):
        shifted = pltpu.roll(s, lag, 0) * twice(mask_ref[lag - 1])
        total = total + shifted * cw_ref[pl.ds(taps - 1 - lag, 1), at]
    return total


def step_sizes(dt, dtb_ref, dl_ref, heads):
    length = dt.shape[0]
    pad = jnp.zeros((length, LANES - heads), F32)
    v = jnp.concatenate([dt, pad], axis=1) + dtb_ref[...]
    step = jnp.maximum(v, 0.0) + jnp.log1p(jnp.exp(-jnp.abs(v)))
    rate = -jnp.exp(dl_ref[...]) * step
    i = lax.broadcasted_iota(jnp.int32, (length, length), 0)
    j = lax.broadcasted_iota(jnp.int32, (length, length), 1)
    lower = jnp.where(i >= j, 1.0, 0.0)
    scaled = rate * LOG2E
    cumul = lax.dot_general(lower, scaled, (((1,), (0,)), ((), ())), precision=HIGH, preferred_element_type=F32)
    return v, step, rate, cumul


def head_lanes(v, quad, per):
    return pltpu.roll(v, lax.rem(LANES - per * quad, LANES), 1)


def spread(v, i0, head_dim):
    length = v.shape[0]
    lane = lax.broadcasted_iota(jnp.int32, (length, LANES), 1)
    a = jnp.broadcast_to(v[:, i0 : i0 + 1], (length, LANES))
    b = jnp.broadcast_to(v[:, i0 + 1 : i0 + 2], (length, LANES))
    return jnp.where(lane < head_dim, a, b)


def forward_body(
    sizes, keep, u_ref, segr_ref, small_ref, w_hbm, ow_hbm, *refs
):
    length, width, inner, conv, heads, taps = sizes
    ng_ref, cw_ref, cb_ref, dtb_ref, dl_ref, sk_ref, gg_ref = small_rows(small_ref, width, inner, conv, taps)
    outs, refs = refs[: 7 if keep else 1], refs[7 if keep else 1 :]
    held, refs = refs[:7], refs[7:]
    out_ref, gate_ref, stream_ref, dt_ref, y_ref, normed_ref, mixed_ref = held
    w, ow, segc_ref, mask_ref, s_ref, gated_ref, cum_ref, step_ref, cumt_ref, sem, osem, wsem = refs
    state = (conv - inner) // 2
    head_dim = inner // heads
    per = WIDE // head_dim
    quads = inner // WIDE
    half = length // 2
    proj = w.shape[0]
    tail = 2 * inner

    def written(k, at, j):
        if k < len(outs):
            return [pltpu.make_async_copy(held[k].at[:, at], outs[k].at[:, at], wsem.at[k, j])]
        return []


    def copies(at, k):
        return weight_copies(w_hbm, w, at, sem, k)

    def stream_copy(q):
        return copies(cols(inner + q * WIDE), 1 + 2 * q)

    def gate_copy(q):
        return copies(cols(q * WIDE), 2 + 2 * q)

    tail_copy = copies(pl.ds(tail, proj - tail), 0)
    start(tail_copy)
    for q in range(quads):
        start(stream_copy(q))
        start(gate_copy(q))
    out_copy = pltpu.make_async_copy(ow_hbm, ow, osem)
    out_copy.start()

    u = u_ref[...].astype(F32)
    scale = lax.rsqrt(jnp.mean(u * u, axis=-1, keepdims=True) + EPS)
    normed_ref[...] = (u * scale * ng_ref[...]).astype(BF16)
    start(written(5, pl.ds(0, width), 0))
    segc_ref[...] = column_of(segr_ref)
    write_masks(segc_ref, mask_ref, taps)

    wait(tail_copy)
    dt = dot_nt(normed_ref[...], w[inner + conv : proj, :])
    dt_ref[...] = dt
    start(written(3, pl.ds(0, heads), 0))
    _, step, _, cumul = step_sizes(dt, dtb_ref, dl_ref, heads)
    step_ref[...] = step
    cum_ref[...] = cumul
    cumt_ref[...] = jnp.transpose(cumul)

    def conv_of(start, s):
        low = s.astype(BF16)
        stream_ref[:, cols(start)] = low
        total = conv_chunk(low.astype(F32), start, cw_ref, cb_ref, mask_ref, taps)
        return total * sigmoid(total)

    bc = conv_of(inner, dot_nt(normed_ref[...], w[tail : tail + 2 * state, :]))
    start(written(2, cols(inner), quads))
    keys = bc[:, :state].astype(BF16)
    queries = bc[:, state:].astype(BF16)
    i = lax.broadcasted_iota(jnp.int32, (length, length), 0)
    j = lax.broadcasted_iota(jnp.int32, (length, length), 1)
    within = (i >= j) & (segc_ref[:, :1] == segr_ref[:1, :])
    s_ref[...] = jnp.where(within, dot_nt(queries, keys), 0.0)

    def quad_step(q, squares):
        at = cols(q * WIDE)
        wait(stream_copy(q))
        wait(gate_copy(q))
        x = conv_of(q * WIDE, dot_nt(normed_ref[...], w[cols(inner + q * WIDE), :]))
        z = dot_nt(normed_ref[...], w[at, :]).astype(BF16)
        gate_ref[:, at] = z
        z = z.astype(F32)
        cum_q = head_lanes(cum_ref[...], q, per)
        step_q = head_lanes(step_ref[...], q, per)
        ys = []
        for pair in range(per // 2):
            part = slice(pair * LANES, (pair + 1) * LANES)
            xdt = (x[:, part] * spread(step_q, 2 * pair, head_dim)).astype(BF16)
            got = []
            for k in range(2):
                h = 2 * pair + k
                col = cum_q[:, h : h + 1]
                row = cumt_ref[pl.ds(per * q + h, 1), :]
                top = jnp.exp2(jnp.minimum(col[:half] - row[:, :half], 0.0)) * s_ref[:half, :half]
                low = jnp.exp2(jnp.minimum(col[half:] - row, 0.0)) * s_ref[half:, :]
                got.append(
                    jnp.concatenate(
                        [dot(top.astype(BF16), xdt[:half]), dot(low.astype(BF16), xdt)], axis=0
                    )
                )
            lane = lax.broadcasted_iota(jnp.int32, (length, LANES), 1)
            ys.append(jnp.where(lane < head_dim, got[0], got[1]))
        y = jnp.concatenate(ys, axis=1)
        y_ref[:, at] = y
        start(written(1, at, q) + written(2, at, q) + written(4, at, q))
        gated = (y + sk_ref[:, at] * x) * (z * sigmoid(z))
        gated_ref[:, at] = gated
        return squares + fold(gated * gated)

    squares = lax.fori_loop(0, quads, quad_step, jnp.zeros((length, LANES), F32))
    scale2 = lax.rsqrt(jnp.sum(squares, axis=-1, keepdims=True) * (1.0 / inner) + EPS)

    def mixed_step(q, _):
        at = cols(q * WIDE)
        mixed_ref[:, at] = (gated_ref[:, at] * scale2 * gg_ref[:, at]).astype(BF16)
        start(written(6, at, q))
        return 0

    lax.fori_loop(0, quads, mixed_step, 0)
    out_copy.wait()

    def out_step(n, _):
        at = cols(n * WIDE)
        out_ref[:, at] = (u_ref[:, at].astype(F32) + dot(mixed_ref[...], ow[:, at])).astype(BF16)
        start(written(0, at, n))
        return 0

    lax.fori_loop(0, width // WIDE, out_step, 0)
    for n in range(width // WIDE):
        wait(written(0, cols(n * WIDE), n))
    wait(written(3, pl.ds(0, heads), 0) + written(5, pl.ds(0, width), 0) + written(2, cols(inner), quads))
    for q in range(quads):
        at = cols(q * WIDE)
        wait(written(1, at, q) + written(2, at, q) + written(4, at, q) + written(6, at, q))


def vmem():
    return pl.BlockSpec(memory_space=pltpu.VMEM)


def hbm():
    return pl.BlockSpec(memory_space=pl.ANY)


def forward(u, seg_row, small, sizes, w, ow, keep=True):
    length, width, inner, conv, heads, taps = sizes
    blocks, proj = w.shape[:2]
    quads = inner // WIDE
    held = (
        ((length, width), BF16),
        ((length, inner), BF16),
        ((length, conv), BF16),
        ((length, heads), F32),
        ((length, inner), F32),
        ((length, width), BF16),
        ((length, inner), BF16),
    )
    outs = held if keep else held[:1]
    return pl.pallas_call(
        functools.partial(forward_body, sizes, keep),
        out_shape=tuple(jax.ShapeDtypeStruct(*out) for out in outs),
        in_specs=[vmem()] * 3 + [hbm()] * 2,
        out_specs=[hbm()] * len(outs),
        scratch_shapes=[pltpu.VMEM(*one) for one in held]
        + [
            pltpu.VMEM((proj, width), BF16),
            pltpu.VMEM((inner, width), BF16),
            pltpu.VMEM((length, LANES), F32),
            pltpu.VMEM((taps - 1, length, LANES), F32),
            pltpu.VMEM((length, length), F32),
            pltpu.VMEM((length, inner), F32),
            pltpu.VMEM((length, LANES), F32),
            pltpu.VMEM((length, LANES), F32),
            pltpu.VMEM((LANES, length), F32),
            pltpu.SemaphoreType.DMA((1 + 2 * quads, blocks)),
            pltpu.SemaphoreType.DMA,
            pltpu.SemaphoreType.DMA((7, quads + 1)),
        ],
        compiler_params=pltpu.CompilerParams(vmem_limit_bytes=VMEM_BYTES),
        cost_estimate=pl.CostEstimate(
            flops=2 * length * (width * proj + inner * width + 2 * length * inner),
            bytes_accessed=2 * (width * proj + inner * width),
            transcendentals=length * (length * heads + 2 * inner),
        ),
        name="layer_forward",
    )(u, seg_row, small, w, ow)


def backward_body(
    sizes, full, u_ref, g_ref, segr_ref, small_ref, gate_hbm, stream_hbm, dt_ref, y_hbm, w_hbm, ow_hbm,
    dlowt_hbm, low_ref, dsmall_ref, *refs,
):
    length, width, inner, conv, heads, taps = sizes
    ng_ref, cw_ref, cb_ref, dtb_ref, dl_ref, sk_ref, gg_ref = small_rows(small_ref, width, inner, conv, taps)
    dng_ref, dcw_ref, dcb_ref, ddtb_ref, ddl_ref, dsk_ref, dgg_ref = small_rows(
        dsmall_ref, width, inner, conv, taps
    )
    gin_ref = refs[0] if full else None
    (
        w, ow, gate_ref, stream_ref, y_ref, dlowt_ref, segc_ref, mask_ref, x_ref, slope_ref, dm_ref, st_ref, dst_ref,
        cum_ref, step_ref, cumt_ref, heads_ref, direct_ref, rows_ref, dn_ref, dlow_ref, sem, osem, rsem, wsem,
    ) = refs[1 if full else 0 :]
    state = (conv - inner) // 2
    head_dim = inner // heads
    per = WIDE // head_dim
    quads = inner // WIDE
    half = length // 2
    proj = w.shape[0]

    def read(q):
        at = pl.ds(pl.multiple_of(q * WIDE, WIDE), WIDE)
        return [
            pltpu.make_async_copy(ow_hbm.at[at, :], ow.at[at, :], osem.at[q]),
            pltpu.make_async_copy(stream_hbm.at[:, at], stream_ref.at[:, at], rsem.at[0, q]),
            pltpu.make_async_copy(gate_hbm.at[:, at], gate_ref.at[:, at], rsem.at[1, q]),
            pltpu.make_async_copy(y_hbm.at[:, at], y_ref.at[:, at], rsem.at[2, q]),
        ]

    last = pl.ds(inner, conv - inner)
    read_last = [pltpu.make_async_copy(stream_hbm.at[:, last], stream_ref.at[:, last], rsem.at[0, quads])]
    for q in range(quads):
        start(read(q))
    start(read_last)
    in_copy = weight_copies(w_hbm, w, pl.ds(0, proj), sem, 0)
    start(in_copy)

    def written(first, size, j):
        rows = pl.ds(pl.multiple_of(first, 32), size)
        return [pltpu.make_async_copy(dlowt_ref.at[rows, :], dlowt_hbm.at[rows, :], wsem.at[j])]

    dsmall_ref[...] = jnp.zeros_like(dsmall_ref)
    segc_ref[...] = column_of(segr_ref)
    write_masks(segc_ref, mask_ref, taps)
    v, step, rate, cumul = step_sizes(dt_ref[...], dtb_ref, dl_ref, heads)
    step_ref[...] = step
    cum_ref[...] = cumul
    cumt_ref[...] = jnp.transpose(cumul)
    heads_ref[...] = jnp.zeros_like(heads_ref)
    direct_ref[...] = jnp.zeros_like(direct_ref)
    dst_ref[...] = jnp.zeros_like(dst_ref)
    rows_ref[...] = jnp.zeros_like(rows_ref)

    def conv_of(start):
        at = cols(start)
        total = conv_chunk(stream_ref[:, at].astype(F32), start, cw_ref, cb_ref, mask_ref, taps)
        sig = sigmoid(total)
        x = total * sig
        x_ref[:, at] = x
        slope_ref[:, at] = sig + x * (1.0 - sig)
        return x

    def first_step(q, carry):
        squares, cross = carry
        at = cols(q * WIDE)
        wait(read(q))
        dm = dot_nt(g_ref[...], ow[pl.ds(pl.multiple_of(q * WIDE, WIDE), WIDE), :])
        x = conv_of(q * WIDE)
        z = gate_ref[:, at].astype(F32)
        gated = (y_ref[:, at] + sk_ref[:, at] * x) * (z * sigmoid(z))
        dm_ref[:, at] = dm
        return squares + fold(gated * gated), cross + fold(gated * (dm * gg_ref[:, at]))

    zero = jnp.zeros((length, LANES), F32)
    squares, cross = lax.fori_loop(0, quads, first_step, (zero, zero))
    scale2 = lax.rsqrt(jnp.sum(squares, axis=-1, keepdims=True) * (1.0 / inner) + EPS)
    back2 = jnp.sum(cross, axis=-1, keepdims=True) * scale2 * scale2 * scale2 * (1.0 / inner)

    wait(read_last)
    bc = conv_of(inner)
    keys = bc[:, :state].astype(BF16)
    queries = bc[:, state:].astype(BF16)
    j = lax.broadcasted_iota(jnp.int32, (length, length), 0)
    i = lax.broadcasted_iota(jnp.int32, (length, length), 1)
    within = (i >= j) & (segc_ref[:, :1] == segr_ref[:1, :])
    st_ref[...] = jnp.where(within, dot_nt(keys, queries), 0.0)

    def write_low(at, value):
        low = value.astype(BF16)
        dlow_ref[:, at] = low
        dlowt_ref[at, :] = jnp.transpose(low)

    def conv_back(start, d_conv):
        at = cols(start)
        d_total = d_conv * slope_ref[:, at]
        s = stream_ref[:, at].astype(F32)
        dcb_ref[:, at] = jnp.sum(d_total, axis=0, keepdims=True)
        dcw_ref[pl.ds(taps - 1, 1), at] = jnp.sum(d_total * s, axis=0, keepdims=True)
        d_stream = d_total * cw_ref[pl.ds(taps - 1, 1), at]
        for lag in range(1, taps):
            back = pltpu.roll(d_total * twice(mask_ref[lag - 1]), length - lag, 0)
            dcw_ref[pl.ds(taps - 1 - lag, 1), at] = jnp.sum(back * s, axis=0, keepdims=True)
            d_stream = d_stream + back * cw_ref[pl.ds(taps - 1 - lag, 1), at]
        write_low(cols(inner + start), d_stream)

    def second_step(q, _):
        at = cols(q * WIDE)
        x = x_ref[:, at]
        y = y_ref[:, at]
        dm = dm_ref[:, at]
        z = gate_ref[:, at].astype(F32)
        sig = sigmoid(z)
        zs = z * sig
        yf = y + sk_ref[:, at] * x
        gated = yf * zs
        scaled = dm * scale2
        dgg_ref[:, at] = jnp.sum(scaled * gated, axis=0, keepdims=True)
        d_gated = scaled * gg_ref[:, at] - gated * back2
        dy = d_gated * zs
        write_low(at, d_gated * yf * (sig + zs * (1.0 - sig)))
        dsk_ref[:, at] = jnp.sum(dy * x, axis=0, keepdims=True)
        dy_low = dy.astype(BF16)
        cum_q = head_lanes(cum_ref[...], q, per)
        step_q = head_lanes(step_ref[...], q, per)
        lane = lax.broadcasted_iota(jnp.int32, (length, LANES), 1)
        dst_top = jnp.zeros((half, length), F32)
        dst_low = jnp.zeros((half, half), F32)
        xdts, dxdts, steps = [], [], []
        for pair in range(per // 2):
            part = slice(pair * LANES, (pair + 1) * LANES)
            step_p = spread(step_q, 2 * pair, head_dim)
            xdt = (x[:, part] * step_p).astype(BF16)
            dyp = dy_low[:, part]
            got = []
            for k in range(2):
                h = 2 * pair + k
                mine = (lane < head_dim) if k == 0 else (lane >= head_dim)
                xm = jnp.where(mine, xdt.astype(F32), 0.0).astype(BF16)
                col = cum_q[:, h : h + 1]
                row = cumt_ref[pl.ds(per * q + h, 1), :]
                decay_top = jnp.exp2(jnp.minimum(row - col[:half], 0.0))
                decay_low = jnp.exp2(jnp.minimum(row[:, half:] - col[half:], 0.0))
                top = (decay_top * st_ref[:half, :]).astype(BF16)
                low = (decay_low * st_ref[half:, half:]).astype(BF16)
                got.append(jnp.concatenate([dot(top, dyp), dot(low, dyp[half:])], axis=0))
                dm_top = dot_nt(xm[:half], dyp)
                dm_low = dot_nt(xm[half:], dyp[half:])
                dst_top = dst_top + dm_top * decay_top
                dst_low = dst_low + dm_low * decay_low
                sums = jnp.sum(dm_top * top.astype(F32), axis=0, keepdims=True)
                more = jnp.sum(dm_low * low.astype(F32), axis=0, keepdims=True)
                rows_ref[pl.ds(per * q + h, 1), :] = jnp.concatenate([sums[:, :half], sums[:, half:] + more], axis=1)
            xdts.append(xdt.astype(F32))
            steps.append(step_p)
            dxdts.append(jnp.where(lane < head_dim, got[0], got[1]))
        dst_ref[:half, :] += dst_top
        dst_ref[half:, half:] += dst_low
        xdt = jnp.concatenate(xdts, axis=1)
        dxdt = jnp.concatenate(dxdts, axis=1)
        steps = jnp.concatenate(steps, axis=1)
        pick_row = lax.broadcasted_iota(jnp.int32, (WIDE, LANES), 0)
        pick_col = lax.broadcasted_iota(jnp.int32, (WIDE, LANES), 1)
        pick = jnp.where(pick_row // head_dim + per * q == pick_col, 1.0, 0.0).astype(BF16)
        both = xdt * dxdt
        high = both.astype(BF16)
        rest = both - high.astype(F32)
        middle = rest.astype(BF16)
        low = (rest - middle.astype(F32)).astype(BF16)
        heads_ref[...] += dot(high, pick) + (dot(middle, pick) + dot(low, pick))
        direct_ref[...] += dot((dxdt * x).astype(BF16), pick)
        conv_back(q * WIDE, dxdt * steps + sk_ref[:, at] * dy)
        start(written(q * WIDE, WIDE, q) + written(inner + q * WIDE, WIDE, quads + q))
        return 0

    lax.fori_loop(0, quads, second_step, 0)

    d_scores = jnp.where(within, dst_ref[...], 0.0).astype(BF16)
    conv_back(inner, jnp.concatenate([dot(d_scores, queries), dot_tn(d_scores, keys)], axis=1))

    upper = jnp.where(within, 1.0, 0.0)
    d_rate = lax.dot_general(
        upper, jnp.transpose(rows_ref[...]) - heads_ref[...], (((1,), (0,)), ((), ())), precision=HIGH, preferred_element_type=F32
    )
    ddl_ref[...] = jnp.sum(d_rate * rate, axis=0, keepdims=True)
    d_step = direct_ref[...] - d_rate * jnp.exp(dl_ref[...])
    d_dt = d_step / (1.0 + jnp.exp(-v))
    ddtb_ref[...] = jnp.sum(d_dt, axis=0, keepdims=True)
    d_dt_low = d_dt[:, :heads].astype(BF16)
    dlowt_ref[inner + conv : proj, :] = jnp.transpose(d_dt)[:heads].astype(BF16)
    start(written(2 * inner, proj - 2 * inner, 2 * quads))

    wait(in_copy)
    u = u_ref[...].astype(F32)
    scale = lax.rsqrt(jnp.mean(u * u, axis=-1, keepdims=True) + EPS)

    def normed_step(n, _):
        at = cols(n * WIDE)
        dn_ref[:, at] = dot(dlow_ref[...], w[: inner + conv, at]) + dot(d_dt_low, w[inner + conv : proj, at])
        return 0

    lax.fori_loop(0, width // WIDE, normed_step, 0)
    dn = dn_ref[...]
    dng_ref[...] = jnp.sum(dn * u * scale, axis=0, keepdims=True)
    dn = dn * ng_ref[...]
    back = jnp.mean(dn * u, axis=-1, keepdims=True) * scale * scale * scale
    gin = g_ref[...].astype(F32) + dn * scale - u * back
    if full:
        gin_ref[...] = gin
    low_ref[...] = gin.astype(BF16)
    for q in range(quads):
        wait(written(q * WIDE, WIDE, q) + written(inner + q * WIDE, WIDE, quads + q))
    wait(written(2 * inner, proj - 2 * inner, 2 * quads))


def backward(u, g, seg_row, small, sizes, kept, w, ow, full=False):
    length, width, inner, conv, heads, taps = sizes
    blocks, proj = w.shape[:2]
    quads = inner // WIDE
    shape = jax.ShapeDtypeStruct
    outs = (shape((proj, length), BF16), shape((length, width), BF16), shape(small.shape, F32))
    outs += (shape((length, width), F32),) if full else ()
    gate, stream, dt, y = kept
    return pl.pallas_call(
        functools.partial(backward_body, sizes, full),
        out_shape=outs,
        in_specs=[vmem()] * 4 + [hbm()] * 2 + [vmem()] + [hbm()] * 3,
        out_specs=[hbm()] + [vmem()] * (len(outs) - 1),
        scratch_shapes=[
            pltpu.VMEM((proj, width), BF16),
            pltpu.VMEM((inner, width), BF16),
            pltpu.VMEM((length, inner), BF16),
            pltpu.VMEM((length, conv), BF16),
            pltpu.VMEM((length, inner), F32),
            pltpu.VMEM((proj, length), BF16),
            pltpu.VMEM((length, LANES), F32),
            pltpu.VMEM((taps - 1, length, LANES), F32),
            pltpu.VMEM((length, conv), F32),
            pltpu.VMEM((length, conv), F32),
            pltpu.VMEM((length, inner), F32),
            pltpu.VMEM((length, length), F32),
            pltpu.VMEM((length, length), F32),
            pltpu.VMEM((length, LANES), F32),
            pltpu.VMEM((length, LANES), F32),
            pltpu.VMEM((LANES, length), F32),
            pltpu.VMEM((length, LANES), F32),
            pltpu.VMEM((length, LANES), F32),
            pltpu.VMEM((LANES, length), F32),
            pltpu.VMEM((length, width), F32),
            pltpu.VMEM((length, inner + conv), BF16),
            pltpu.SemaphoreType.DMA((1, blocks)),
            pltpu.SemaphoreType.DMA((quads,)),
            pltpu.SemaphoreType.DMA((3, quads + 1)),
            pltpu.SemaphoreType.DMA((2 * quads + 1,)),
        ],
        compiler_params=pltpu.CompilerParams(vmem_limit_bytes=VMEM_BYTES),
        cost_estimate=pl.CostEstimate(
            flops=2 * length * (width * proj + inner * width + 4 * length * inner),
            bytes_accessed=2 * (width * proj + inner * width) + 8 * length * proj,
            transcendentals=length * (length * heads + 4 * inner),
        ),
        name="layer_backward",
    )(u, g, seg_row, small, gate, stream, dt, y, w, ow)


def flip(value, axis, distance):
    pairs = [(source, source ^ distance) for source in range(lax.axis_size(axis))]
    return lax.ppermute(value, axis, pairs)


def rotate(value, axis):
    count = lax.axis_size(axis)
    return lax.ppermute(value, axis, [(source, (source + 1) % count) for source in range(count)])


def distances(axis):
    found, d = [], 1
    while d < lax.axis_size(axis):
        found.append(d)
        d *= 2
    return found


def after(value, *others):
    return lax.optimization_barrier((value,) + others)[0]


def blank(shape, dtype):
    return pl.pallas_call(
        lambda out: None,
        out_shape=jax.ShapeDtypeStruct(shape, dtype),
        out_specs=hbm(),
        compiler_params=pltpu.CompilerParams(vmem_limit_bytes=1024 * 1024),
        name="blank",
    )()


class Line:
    def __init__(self):
        self.last = None

    def take(self, value):
        if self.last is not None:
            value, _ = lax.optimization_barrier((value, self.last))
        self.last = value
        return value


def gather_all(large, little, row):
    ring, share = lax.axis_size("fsdp"), lax.axis_size("dp")
    z, q = lax.axis_index("fsdp"), lax.axis_index("dp")
    far, near = distances("dp")[-1], list(reversed(distances("dp")[:-1]))
    line = Line()

    def begin(own):
        whole = lax.dynamic_update_slice(blank((ring,) + own.shape, own.dtype), own[None], (z, 0, 0, 0))
        return whole, lax.dynamic_index_in_dim(own, q, 0, keepdims=False)

    def place(whole, step, here, arrived):
        parts = {0: here, far: arrived}
        for d in near:
            parts.update({m | d: flip(v, "dp", d) for m, v in list(parts.items())})
        source = lax.rem(z - step + ring, ring)
        for m, v in parts.items():
            whole = lax.dynamic_update_slice(whole, v[None, None], (source, q ^ m, 0, 0))
        return whole

    large_all, travelling = begin(large)
    large_next = rotate(travelling, "fsdp")
    little_all, travelling = begin(little)
    little_next = rotate(travelling, "fsdp")
    rows = [after(row, travelling)]
    row_next = rotate(rows[0], "fsdp")
    waiting = None
    for step in range(1, ring):
        more = step + 1 < ring
        little_here = line.take(little_next)
        if more:
            little_next = rotate(little_here, "fsdp")
        little_far = flip(little_here, "dp", far)
        large_here = line.take(large_next)
        if more:
            large_next = rotate(large_here, "fsdp")
        if waiting is not None:
            large_all = place(large_all, step - 1, waiting[0], line.take(waiting[1]))
        waiting = (large_here, flip(large_here, "dp", far))
        rows.append(line.take(row_next))
        if more:
            row_next = rotate(rows[-1], "fsdp")
        little_all = place(little_all, step, little_here, line.take(little_far))
    large_all = place(large_all, ring - 1, waiting[0], line.take(waiting[1]))
    at = jnp.arange(ring)
    chosen = (lax.rem(z - at[:, None] + ring, ring) == at[None, :]).astype(row.dtype)
    row_all = jnp.dot(chosen, jnp.concatenate(rows, axis=0), preferred_element_type=F32)
    return large_all, little_all, row_all


def ring_places():
    ring, z = lax.axis_size("fsdp"), lax.axis_index("fsdp")
    return [lax.rem(z + 2 * ring - 1 - s, ring) for s in range(ring)]


def add(a, b):
    return a.astype(F32) + b.astype(F32)


def sum_far(near, level, mask):
    if level == 0:
        return near[mask]
    d = distances("dp")[level]
    away = [flip(v, "dp", d) for v in sum_far(near, level - 1, mask | d)]
    line = Line()
    return [add(a, line.take(b)).astype(BF16) for a, b in zip(sum_far(near, level - 1, mask), away)]


def sum_rings(near, early, rows):
    ring, levels = lax.axis_size("fsdp"), len(distances("dp")) - 1
    d = distances("dp")[-1]
    order = Line()
    away = [flip(order.take(v), "dp", d) for v in sum_far(near, levels - 1, d)]
    here = [order.take(v) for v in sum_far(near, levels - 1, 0)]
    line = Line()
    value, value_next = None, None
    early_value, early_next = early[0], rotate(early[0], "fsdp")
    small, small_next = None, None
    for s in range(ring):
        part = add(here[s], line.take(away[s])).astype(BF16)
        value = part if s == 0 else add(line.take(value_next), part).astype(BF16)
        if s == 0:
            rows = after(rows, value)
            rows = rows + flip(rows, "dp", distances("dp")[0])
            small = [lax.dynamic_index_in_dim(rows, at, 0) for at in ring_places()]
            small_value, small_next = small[0], rotate(small[0], "fsdp")
        if s + 1 < ring:
            value_next = rotate(value, "fsdp")
            early_value = add(line.take(early_next), early[s + 1]).astype(BF16)
            if s + 2 < ring:
                early_next = rotate(early_value, "fsdp")
        if s > 0:
            small_value = line.take(small_next) + small[s]
            if s + 1 < ring:
                small_next = rotate(small_value, "fsdp")
    small_value = after(small_value, value)
    for d in distances("dp")[1:]:
        small_value = small_value + flip(small_value, "dp", d)
    return value, early_value, small_value


def share_out(value):
    q = lax.axis_index("dp")
    owned = {0: value}
    for d in reversed(distances("dp")):
        owned.update({m | d: flip(v, "dp", d) for m, v in list(owned.items())})
    whole = blank((lax.axis_size("dp"),) + value.shape, F32)
    for m, v in owned.items():
        whole = lax.dynamic_update_slice(whole, v.astype(F32)[None], (q ^ m, 0, 0))
    return whole.reshape(-1, value.shape[1])


def far_masks():
    return range(0, lax.axis_size("dp"), 2)


def rows_near(left, right):
    ring, _, rows, depth = left.shape
    q, order = lax.axis_index("dp"), ring_places()

    def together(mask):
        mine = lax.dynamic_index_in_dim(left, q ^ mask, 1, keepdims=False)
        mine = jnp.concatenate([lax.dynamic_index_in_dim(mine, at, 0) for at in order], axis=0)
        product = jnp.dot(mine.reshape(ring * rows, depth), right, preferred_element_type=F32)
        return product.astype(BF16).reshape(ring, rows, -1)

    near = {}
    for mask in reversed(far_masks()):
        arrived = flip(together(mask | 1), "dp", 1)
        both = add(together(mask), arrived).astype(BF16)
        near[mask] = [both[s] for s in range(ring)]
    return near


def columns_near(left, right):
    ring, depth = lax.axis_size("fsdp"), right.shape[0]
    order = ring_places()
    block = right.shape[1] // ring
    rights = [lax.dynamic_slice(right, (0, at * block), (depth, block)) for at in order]
    every = jnp.concatenate(rights, axis=1)
    near = {}
    for mask in reversed(far_masks()):
        away = jnp.dot(left(mask | 1), every, preferred_element_type=F32).astype(BF16)
        arrived = flip(away, "dp", 1)
        here = left(mask)
        near[mask] = [
            add(jnp.dot(here, rights[s], preferred_element_type=F32), arrived[:, s * block : (s + 1) * block]).astype(BF16)
            for s in range(ring)
        ]
    return near


def shards(
    inputs,
    cotangent,
    segments,
    norm_gain,
    in_weight,
    conv_weight,
    conv_bias,
    dt_bias,
    decay_log,
    skip_gain,
    gate_gain,
    out_weight,
):
    first = lax.axis_index("section") == 0
    z = lax.axis_index("fsdp")
    ring, share = lax.axis_size("fsdp"), lax.axis_size("dp")
    length, width = inputs.shape[2], inputs.shape[3]
    taps = conv_weight.shape[1]
    heads = dt_bias.shape[1] * ring
    inner = gate_gain.shape[1] * ring
    head_dim = inner // heads

    pieces = (norm_gain[0], conv_bias[0], dt_bias[0], decay_log[0], skip_gain[0], gate_gain[0], conv_weight[0].reshape(-1))
    sizes = [piece.shape[0] for piece in pieces]
    proj = in_weight.shape[2]
    w, ow, packed = gather_all(
        in_weight[0].T.reshape(share, proj // share, -1),
        out_weight[0].reshape(share, -1, width),
        jnp.concatenate(pieces)[None],
    )
    w = w.reshape(ring, proj, -1)
    ow = ow.reshape(inner, width)
    fields, start = [], 0
    for size in sizes:
        fields.append(packed[:, start : start + size])
        start += size
    taps_w = fields[6].reshape(ring, taps, -1).transpose(1, 0, 2).reshape(taps, -1)
    rows = [field.reshape(1, -1) for field in fields[:6]]

    conv_width = conv_bias.shape[1] * ring

    def padded(row):
        return jnp.pad(row, ((0, 0), (0, conv_width - row.shape[1])))

    wide_rows = [rows[0], rows[1], rows[2], rows[3], jnp.repeat(rows[4], head_dim, axis=1), rows[5]]
    filler = jnp.zeros((-(taps + len(wide_rows)) % 8, conv_width), F32)
    small = jnp.concatenate([taps_w] + [padded(row) for row in wide_rows] + [filler], axis=0)
    sizes_of = (length, width, inner, conv_width, heads, taps)
    seg = segments[:, 0].astype(F32)
    seg_rows = [jnp.broadcast_to(seg[m][None], (8, length)) for m in range(2)]
    pick = functools.partial(jnp.where, first)

    def to_second(value):
        return lax.ppermute(value, "section", [(0, 1)])

    def to_first(value):
        return lax.ppermute(value, "section", [(1, 0)])

    u_a, u_b = inputs[0, 0], inputs[1, 0]
    g_a, g_b = cotangent[0, 0], cotangent[1, 0]

    out0 = forward(u_a, seg_rows[0], small, sizes_of, w, ow, keep=False)[0]
    u1 = pick(u_b, to_second(out0))
    seg1 = pick(seg_rows[1], seg_rows[0])
    out1, gate1, stream1, dt1, y1, normed1, mixed1 = forward(u1, seg1, small, sizes_of, w, ow)
    stream_b = to_second(out1)
    kept1 = (gate1, stream1, dt1, y1)
    back2 = backward(u1, g_a, seg1, small, sizes_of, kept1, w, ow)
    grad_a = to_first(back2[1])
    u3 = pick(u_a, stream_b)
    seg3 = pick(seg_rows[0], seg_rows[1])
    out3, gate3, stream3, dt3, y3, normed3, mixed3 = forward(u3, seg3, small, sizes_of, w, ow)
    g4 = pick(grad_a, g_b)
    back4 = backward(u3, g4, seg3, small, sizes_of, (gate3, stream3, dt3, y3), w, ow, full=True)
    grad_b = to_first(back4[1])

    mixed_t = jnp.concatenate([mixed3, mixed1], axis=0).T.reshape(ring, share, -1, 2 * length)
    near_out = rows_near(mixed_t, jnp.concatenate([g4, pick(grad_b, g_a)], axis=0))
    ahead = [v for parts in near_out.values() for v in parts]
    back5 = backward(after(u1, *ahead), grad_b, seg1, small, sizes_of, kept1, w, ow)

    levels = len(distances("dp")) - 1
    far_out = sum_far(near_out, levels, 0)
    normed = jnp.concatenate([normed3, normed1], axis=0)
    q = lax.axis_index("dp")
    back5_t = after(back5[0], *far_out)

    def left(mask):
        def part(value):
            return lax.dynamic_index_in_dim(value.reshape(share, -1, length), q ^ mask, 0, keepdims=False)

        return jnp.concatenate([part(back4[0]), pick(part(back5_t), part(back2[0]))], axis=1)

    near_in = columns_near(left, normed)
    grad = back4[2] + pick(back5[2], back2[2])

    def field(k, size):
        return grad[taps + k, :size].reshape(ring, -1)

    packed = jnp.concatenate(
        [
            field(0, width),
            field(1, conv_width),
            field(2, heads),
            field(3, heads),
            jnp.sum(grad[taps + 4, :inner].reshape(heads, head_dim), axis=1).reshape(ring, -1),
            field(5, inner),
            grad[:taps].reshape(taps, ring, -1).transpose(1, 0, 2).reshape(ring, -1),
        ],
        axis=1,
    )
    own_in, own_out, packed = sum_rings(near_in, far_out, packed)
    in_grad = share_out(own_in).T[None]
    out_grad = share_out(own_out)[None]
    begun = near_in[0][0]
    output = pick(after(to_first(after(out1, begun)), own_in), out3)
    input_grad = pick(back4[3], after(to_second(after(back5[1], begun)), own_in).astype(F32))
    fields, start = [], 0
    for size in sizes:
        fields.append(packed[:, start : start + size])
        start += size
    return (
        output[None, None],
        input_grad[None, None],
        fields[0],
        in_grad,
        fields[6].reshape(1, taps, -1),
        fields[1],
        fields[2],
        fields[3],
        fields[4],
        fields[5],
        out_grad,
    )


def solution(mesh):
    spread_over = ("fsdp", "dp")
    row = P("section", "fsdp")
    matrix = P("section", "fsdp", None)
    tap = P("section", None, "fsdp")
    activation = P(None, spread_over, None, None)
    result = P("section", spread_over, None, None)
    return jax.shard_map(
        shards,
        mesh=mesh,
        in_specs=(activation, activation, P(None, spread_over, None), row, matrix, tap, row, row, row, row, row, matrix),
        out_specs=(result, result, row, matrix, tap, row, row, row, row, row, matrix),
        check_vma=False,
    )
```

```python
import functools

import jax
import jax.numpy as jnp
from jax import lax
from jax.experimental import pallas as pl
from jax.experimental.pallas import tpu as pltpu
from jax.sharding import PartitionSpec as P

EPS = 1e-05
LOG2E = 1.4426950408889634
HIGH = lax.Precision.HIGHEST
F32 = jnp.float32
BF16 = jnp.bfloat16
LANES = 128
WIDE = 256
VMEM_BYTES = 56 * 1024 * 1024


def sigmoid(v):
    return 0.5 * jnp.tanh(0.5 * v) + 0.5


def dot(a, b):
    return lax.dot_general(a, b, (((1,), (0,)), ((), ())), preferred_element_type=F32)


def dot_nt(a, b):
    return lax.dot_general(a, b, (((1,), (1,)), ((), ())), preferred_element_type=F32)


def dot_tn(a, b):
    return lax.dot_general(a, b, (((0,), (0,)), ((), ())), preferred_element_type=F32)


def twice(v):
    return jnp.concatenate([v, v], axis=1)


def fold(v):
    return v[:, :LANES] + v[:, LANES:]


def cols(start, width=WIDE):
    return pl.ds(pl.multiple_of(start, LANES), width)


def weight_copies(source, target, rows, sem, k):
    blocks, _, width = source.shape
    return [
        pltpu.make_async_copy(
            source.at[b, rows, :], target.at[rows, b * width : (b + 1) * width], sem.at[k, b]
        )
        for b in range(blocks)
    ]


def start(copies):
    for copy in copies:
        copy.start()


def wait(copies):
    for copy in copies:
        copy.wait()


def small_rows(small_ref, width, inner, conv, taps):
    row = lambda k, size: small_ref.at[taps + k : taps + k + 1, :size]
    return (
        row(0, width),
        small_ref.at[:taps],
        row(1, conv),
        row(2, LANES),
        row(3, LANES),
        row(4, inner),
        row(5, inner),
    )


def column_of(segr_ref):
    row = jnp.broadcast_to(segr_ref[:1, :], (LANES, segr_ref.shape[1]))
    return jnp.transpose(row)


def write_masks(segc_ref, mask_ref, taps):
    seg = segc_ref[...]
    row = lax.broadcasted_iota(jnp.int32, seg.shape, 0)
    for lag in range(1, taps):
        same = (pltpu.roll(seg, lag, 0) == seg) & (row >= lag)
        mask_ref[lag - 1] = jnp.where(same, 1.0, 0.0)


def conv_chunk(s, start, cw_ref, cb_ref, mask_ref, taps):
    at = cols(start)
    total = cb_ref[:, at] + s * cw_ref[pl.ds(taps - 1, 1), at]
    for lag in range(1, taps):
        shifted = pltpu.roll(s, lag, 0) * twice(mask_ref[lag - 1])
        total = total + shifted * cw_ref[pl.ds(taps - 1 - lag, 1), at]
    return total


def step_sizes(dt, dtb_ref, dl_ref, heads):
    length = dt.shape[0]
    pad = jnp.zeros((length, LANES - heads), F32)
    v = jnp.concatenate([dt, pad], axis=1) + dtb_ref[...]
    step = jnp.maximum(v, 0.0) + jnp.log1p(jnp.exp(-jnp.abs(v)))
    rate = -jnp.exp(dl_ref[...]) * step
    i = lax.broadcasted_iota(jnp.int32, (length, length), 0)
    j = lax.broadcasted_iota(jnp.int32, (length, length), 1)
    lower = jnp.where(i >= j, 1.0, 0.0)
    scaled = rate * LOG2E
    cumul = lax.dot_general(lower, scaled, (((1,), (0,)), ((), ())), precision=HIGH, preferred_element_type=F32)
    return v, step, rate, cumul


def head_lanes(v, quad, per):
    return pltpu.roll(v, lax.rem(LANES - per * quad, LANES), 1)


def spread(v, i0, head_dim):
    length = v.shape[0]
    lane = lax.broadcasted_iota(jnp.int32, (length, LANES), 1)
    a = jnp.broadcast_to(v[:, i0 : i0 + 1], (length, LANES))
    b = jnp.broadcast_to(v[:, i0 + 1 : i0 + 2], (length, LANES))
    return jnp.where(lane < head_dim, a, b)


def forward_body(
    sizes, keep, u_ref, segr_ref, small_ref, w_hbm, ow_hbm, *refs
):
    length, width, inner, conv, heads, taps = sizes
    ng_ref, cw_ref, cb_ref, dtb_ref, dl_ref, sk_ref, gg_ref = small_rows(small_ref, width, inner, conv, taps)
    count = 10 if keep else 1
    outs, held, refs = refs[:count], refs[count : count + 10], refs[count + 10 :]
    out_ref, zs_ref, zslope_ref, yf_ref, x_ref, slope_ref, stream_ref, dt_ref, normed_ref, mixed_ref = held
    w, ow, segc_ref, mask_ref, s_ref, gated_ref, gate_ref, cum_ref, step_ref, cumt_ref, sem, osem, wsem = refs
    state = (conv - inner) // 2
    head_dim = inner // heads
    per = WIDE // head_dim
    quads = inner // WIDE
    half = length // 2
    proj = w.shape[0]
    tail = 2 * inner

    def written(k, at, j):
        if k < len(outs):
            return [pltpu.make_async_copy(held[k].at[:, at], outs[k].at[:, at], wsem.at[k, j])]
        return []


    def copies(at, k):
        return weight_copies(w_hbm, w, at, sem, k)

    def stream_copy(q):
        return copies(cols(inner + q * WIDE), 1 + 2 * q)

    def gate_copy(q):
        return copies(cols(q * WIDE), 2 + 2 * q)

    tail_copy = copies(pl.ds(tail, proj - tail), 0)
    start(tail_copy)
    ahead = min(3, quads)
    for q in range(ahead):
        start(stream_copy(q))
        start(gate_copy(q))
    out_copy = pltpu.make_async_copy(ow_hbm, ow, osem)

    u = u_ref[...].astype(F32)
    scale = lax.rsqrt(jnp.mean(u * u, axis=-1, keepdims=True) + EPS)
    normed_ref[...] = (u * scale * ng_ref[...]).astype(BF16)
    start(written(8, pl.ds(0, width), 0))
    segc_ref[...] = column_of(segr_ref)
    write_masks(segc_ref, mask_ref, taps)

    def project(q):
        rows = cols(inner + q * WIDE)
        stream_ref[:, cols(q * WIDE)] = dot_nt(normed_ref[...], w[rows, :]).astype(BF16)
        gate_ref[:, cols(q * WIDE)] = dot_nt(normed_ref[...], w[cols(q * WIDE), :])

    wait(tail_copy)
    dt = dot_nt(normed_ref[...], w[inner + conv : proj, :])
    dt_ref[...] = dt
    start(written(7, pl.ds(0, heads), 0))
    stream_ref[:, cols(inner)] = dot_nt(normed_ref[...], w[tail : tail + 2 * state, :]).astype(BF16)
    _, step, _, cumul = step_sizes(dt, dtb_ref, dl_ref, heads)
    step_ref[...] = step
    cum_ref[...] = cumul
    cumt_ref[...] = jnp.transpose(cumul)
    wait(stream_copy(0))
    wait(gate_copy(0))
    project(0)

    def conv_of(first):
        at = cols(first)
        total = conv_chunk(stream_ref[:, at].astype(F32), first, cw_ref, cb_ref, mask_ref, taps)
        sig = sigmoid(total)
        x = total * sig
        if keep:
            x_ref[:, at] = x.astype(BF16)
            slope_ref[:, at] = (sig + x * (1.0 - sig)).astype(BF16)
        return x

    bc = conv_of(inner)
    start(written(4, cols(inner), quads) + written(5, cols(inner), quads) + written(6, cols(inner), quads))
    keys = bc[:, :state].astype(BF16)
    queries = bc[:, state:].astype(BF16)
    i = lax.broadcasted_iota(jnp.int32, (length, length), 0)
    j = lax.broadcasted_iota(jnp.int32, (length, length), 1)
    within = (i >= j) & (segc_ref[:, :1] == segr_ref[:1, :])
    s_ref[...] = jnp.where(within, dot_nt(queries, keys), 0.0)

    def quad_step(q, squares, more=True):
        at = cols(q * WIDE)
        if more:

            @pl.when(q + ahead < quads)
            def _():
                start(stream_copy(q + ahead))
                start(gate_copy(q + ahead))

            @pl.when(q + ahead == quads)
            def _():
                out_copy.start()

            wait(stream_copy(q + 1))
            wait(gate_copy(q + 1))
        x = conv_of(q * WIDE)
        z = gate_ref[:, at]
        sig = sigmoid(z)
        zs = z * sig
        if keep:
            zs_ref[:, at] = zs.astype(BF16)
            zslope_ref[:, at] = (sig + zs * (1.0 - sig)).astype(BF16)
        if more:
            project(q + 1)
        cum_q = head_lanes(cum_ref[...], q, per)
        step_q = head_lanes(step_ref[...], q, per)
        ys = []
        for pair in range(per // 2):
            part = slice(pair * LANES, (pair + 1) * LANES)
            xdt = (x[:, part] * spread(step_q, 2 * pair, head_dim)).astype(BF16)
            got = []
            for k in range(2):
                h = 2 * pair + k
                col = cum_q[:, h : h + 1]
                row = cumt_ref[pl.ds(per * q + h, 1), :]
                top = jnp.exp2(jnp.minimum(col[:half] - row[:, :half], 0.0)) * s_ref[:half, :half]
                low = jnp.exp2(jnp.minimum(col[half:] - row, 0.0)) * s_ref[half:, :]
                got.append(
                    jnp.concatenate(
                        [dot(top.astype(BF16), xdt[:half]), dot(low.astype(BF16), xdt)], axis=0
                    )
                )
            lane = lax.broadcasted_iota(jnp.int32, (length, LANES), 1)
            ys.append(jnp.where(lane < head_dim, got[0], got[1]))
        yf = jnp.concatenate(ys, axis=1) + sk_ref[:, at] * x
        gated = yf * zs
        if keep:
            yf_ref[:, at] = yf.astype(BF16)
        gated_ref[:, at] = gated
        for k in range(1, 7):
            start(written(k, at, q))
        return squares + fold(gated * gated)

    squares = lax.fori_loop(0, quads - 1, quad_step, jnp.zeros((length, LANES), F32))
    squares = quad_step(quads - 1, squares, more=False)
    scale2 = lax.rsqrt(jnp.sum(squares, axis=-1, keepdims=True) * (1.0 / inner) + EPS)

    for q in range(quads):
        at = cols(q * WIDE)
        mixed_ref[:, at] = (gated_ref[:, at] * scale2 * gg_ref[:, at]).astype(BF16)
        start(written(9, at, q))
    out_copy.wait()
    for n in range(width // WIDE):
        at = cols(n * WIDE)
        out_ref[:, at] = (u_ref[:, at].astype(F32) + dot(mixed_ref[...], ow[:, at])).astype(BF16)
        start(written(0, at, n))
    for n in range(width // WIDE):
        wait(written(0, cols(n * WIDE), n))
    wait(written(7, pl.ds(0, heads), 0) + written(8, pl.ds(0, width), 0))
    wait(written(4, cols(inner), quads) + written(5, cols(inner), quads) + written(6, cols(inner), quads))
    for q in range(quads):
        for k in (1, 2, 3, 4, 5, 6, 9):
            wait(written(k, cols(q * WIDE), q))


def vmem():
    return pl.BlockSpec(memory_space=pltpu.VMEM)


def hbm():
    return pl.BlockSpec(memory_space=pl.ANY)


def forward(u, seg_row, small, sizes, w, ow, keep=True):
    length, width, inner, conv, heads, taps = sizes
    blocks, proj = w.shape[:2]
    quads = inner // WIDE
    held = (
        ((length, width), BF16),
        ((length, inner), BF16),
        ((length, inner), BF16),
        ((length, inner), BF16),
        ((length, conv), BF16),
        ((length, conv), BF16),
        ((length, conv), BF16),
        ((length, heads), F32),
        ((length, width), BF16),
        ((length, inner), BF16),
    )
    outs = held if keep else held[:1]
    return pl.pallas_call(
        functools.partial(forward_body, sizes, keep),
        out_shape=tuple(jax.ShapeDtypeStruct(*out) for out in outs),
        in_specs=[vmem()] * 3 + [hbm()] * 2,
        out_specs=[hbm()] * len(outs),
        scratch_shapes=[pltpu.VMEM(*one) for one in held]
        + [
            pltpu.VMEM((proj, width), BF16),
            pltpu.VMEM((inner, width), BF16),
            pltpu.VMEM((length, LANES), F32),
            pltpu.VMEM((taps - 1, length, LANES), F32),
            pltpu.VMEM((length, length), F32),
            pltpu.VMEM((length, inner), F32),
            pltpu.VMEM((length, inner), F32),
            pltpu.VMEM((length, LANES), F32),
            pltpu.VMEM((length, LANES), F32),
            pltpu.VMEM((LANES, length), F32),
            pltpu.SemaphoreType.DMA((1 + 2 * quads, blocks)),
            pltpu.SemaphoreType.DMA,
            pltpu.SemaphoreType.DMA((10, quads + 1)),
        ],
        compiler_params=pltpu.CompilerParams(vmem_limit_bytes=VMEM_BYTES),
        cost_estimate=pl.CostEstimate(
            flops=2 * length * (width * proj + inner * width + 2 * length * inner),
            bytes_accessed=2 * (width * proj + inner * width),
            transcendentals=length * (length * heads + 2 * inner),
        ),
        name="layer_forward",
    )(u, seg_row, small, w, ow)


def backward_body(
    sizes, full, u_ref, g_ref, segr_ref, small_ref, zs_hbm, zslope_hbm, yf_hbm, x_hbm, slope_hbm, stream_hbm, dt_ref, w_hbm, ow_hbm,
    dlowt_hbm, low_ref, dsmall_ref, *refs,
):
    length, width, inner, conv, heads, taps = sizes
    ng_ref, cw_ref, cb_ref, dtb_ref, dl_ref, sk_ref, gg_ref = small_rows(small_ref, width, inner, conv, taps)
    dng_ref, dcw_ref, dcb_ref, ddtb_ref, ddl_ref, dsk_ref, dgg_ref = small_rows(
        dsmall_ref, width, inner, conv, taps
    )
    gin_ref = refs[0] if full else None
    (
        w, ow, zs_ref, zslope_ref, yf_ref, x_ref, slope_ref, stream_ref, dlowt_ref, segc_ref, mask_ref, dm_ref, st_ref, dst_ref,
        cum_ref, step_ref, cumt_ref, heads_ref, direct_ref, rows_ref, dn_ref, dlow_ref, sem, osem, rsem, wsem,
    ) = refs[1 if full else 0 :]
    state = (conv - inner) // 2
    head_dim = inner // heads
    per = WIDE // head_dim
    quads = inner // WIDE
    half = length // 2
    proj = w.shape[0]

    def fetch(k, source, target, at, j):
        return pltpu.make_async_copy(source.at[:, at], target.at[:, at], rsem.at[k, j])

    def read(q):
        at = pl.ds(pl.multiple_of(q * WIDE, WIDE), WIDE)
        return [
            pltpu.make_async_copy(ow_hbm.at[at, :], ow.at[at, :], osem.at[q]),
            fetch(0, zs_hbm, zs_ref, at, q),
            fetch(1, yf_hbm, yf_ref, at, q),
        ]

    def read_later(q):
        at = pl.ds(pl.multiple_of(q * WIDE, WIDE), WIDE)
        return [
            fetch(2, x_hbm, x_ref, at, q),
            fetch(3, slope_hbm, slope_ref, at, q),
            fetch(4, stream_hbm, stream_ref, at, q),
            fetch(5, zslope_hbm, zslope_ref, at, q),
        ]

    last = pl.ds(inner, conv - inner)
    read_last = [
        fetch(2, x_hbm, x_ref, last, quads),
        fetch(3, slope_hbm, slope_ref, last, quads),
        fetch(4, stream_hbm, stream_ref, last, quads),
    ]
    for q in range(quads):
        start(read(q))
    start(read_last)
    in_copy = weight_copies(w_hbm, w, pl.ds(0, proj), sem, 0)

    def written(first, size, j):
        rows = pl.ds(pl.multiple_of(first, 32), size)
        return [pltpu.make_async_copy(dlowt_ref.at[rows, :], dlowt_hbm.at[rows, :], wsem.at[j])]

    dsmall_ref[...] = jnp.zeros_like(dsmall_ref)
    segc_ref[...] = column_of(segr_ref)
    write_masks(segc_ref, mask_ref, taps)
    v, step, rate, cumul = step_sizes(dt_ref[...], dtb_ref, dl_ref, heads)
    step_ref[...] = step
    cum_ref[...] = cumul
    cumt_ref[...] = jnp.transpose(cumul)
    heads_ref[...] = jnp.zeros_like(heads_ref)
    direct_ref[...] = jnp.zeros_like(direct_ref)
    dst_ref[...] = jnp.zeros_like(dst_ref)
    rows_ref[...] = jnp.zeros_like(rows_ref)

    def first_step(q, carry):
        squares, cross = carry
        at = cols(q * WIDE)
        wait(read(q))
        start(read_later(q))
        dm = dot_nt(g_ref[...], ow[pl.ds(pl.multiple_of(q * WIDE, WIDE), WIDE), :])
        gated = yf_ref[:, at].astype(F32) * zs_ref[:, at].astype(F32)
        dm_ref[:, at] = dm
        return squares + fold(gated * gated), cross + fold(gated * (dm * gg_ref[:, at]))

    zero = jnp.zeros((length, LANES), F32)
    squares, cross = lax.fori_loop(0, quads, first_step, (zero, zero))
    scale2 = lax.rsqrt(jnp.sum(squares, axis=-1, keepdims=True) * (1.0 / inner) + EPS)
    back2 = jnp.sum(cross, axis=-1, keepdims=True) * scale2 * scale2 * scale2 * (1.0 / inner)

    start(in_copy)
    wait(read_last)
    keys = x_ref[:, inner : inner + state]
    queries = x_ref[:, inner + state : inner + 2 * state]
    j = lax.broadcasted_iota(jnp.int32, (length, length), 0)
    i = lax.broadcasted_iota(jnp.int32, (length, length), 1)
    within = (i >= j) & (segc_ref[:, :1] == segr_ref[:1, :])
    st_ref[...] = jnp.where(within, dot_nt(keys, queries), 0.0)

    def write_low(at, value):
        low = value.astype(BF16)
        dlow_ref[:, at] = low
        dlowt_ref[at, :] = jnp.transpose(low)

    def conv_back(start, d_conv):
        at = cols(start)
        d_total = d_conv * slope_ref[:, at].astype(F32)
        s = stream_ref[:, at].astype(F32)
        dcb_ref[:, at] = jnp.sum(d_total, axis=0, keepdims=True)
        dcw_ref[pl.ds(taps - 1, 1), at] = jnp.sum(d_total * s, axis=0, keepdims=True)
        d_stream = d_total * cw_ref[pl.ds(taps - 1, 1), at]
        for lag in range(1, taps):
            back = pltpu.roll(d_total * twice(mask_ref[lag - 1]), length - lag, 0)
            dcw_ref[pl.ds(taps - 1 - lag, 1), at] = jnp.sum(back * s, axis=0, keepdims=True)
            d_stream = d_stream + back * cw_ref[pl.ds(taps - 1 - lag, 1), at]
        write_low(cols(inner + start), d_stream)

    def second_step(q, _):
        at = cols(q * WIDE)
        wait(read_later(q))
        x = x_ref[:, at].astype(F32)
        zs = zs_ref[:, at].astype(F32)
        yf = yf_ref[:, at].astype(F32)
        gated = yf * zs
        scaled = dm_ref[:, at] * scale2
        dgg_ref[:, at] = jnp.sum(scaled * gated, axis=0, keepdims=True)
        d_gated = scaled * gg_ref[:, at] - gated * back2
        dy = d_gated * zs
        write_low(at, d_gated * yf * zslope_ref[:, at].astype(F32))
        dsk_ref[:, at] = jnp.sum(dy * x, axis=0, keepdims=True)
        dy_low = dy.astype(BF16)
        cum_q = head_lanes(cum_ref[...], q, per)
        step_q = head_lanes(step_ref[...], q, per)
        lane = lax.broadcasted_iota(jnp.int32, (length, LANES), 1)
        dst_top = jnp.zeros((half, length), F32)
        dst_low = jnp.zeros((half, half), F32)
        xdts, dxdts, steps = [], [], []
        for pair in range(per // 2):
            part = slice(pair * LANES, (pair + 1) * LANES)
            step_p = spread(step_q, 2 * pair, head_dim)
            xdt = (x[:, part] * step_p).astype(BF16)
            dyp = dy_low[:, part]
            got = []
            for k in range(2):
                h = 2 * pair + k
                mine = (lane < head_dim) if k == 0 else (lane >= head_dim)
                xm = jnp.where(mine, xdt.astype(F32), 0.0).astype(BF16)
                col = cum_q[:, h : h + 1]
                row = cumt_ref[pl.ds(per * q + h, 1), :]
                decay_top = jnp.exp2(jnp.minimum(row - col[:half], 0.0))
                decay_low = jnp.exp2(jnp.minimum(row[:, half:] - col[half:], 0.0))
                top = (decay_top * st_ref[:half, :]).astype(BF16)
                low = (decay_low * st_ref[half:, half:]).astype(BF16)
                got.append(jnp.concatenate([dot(top, dyp), dot(low, dyp[half:])], axis=0))
                dm_top = dot_nt(xm[:half], dyp)
                dm_low = dot_nt(xm[half:], dyp[half:])
                dst_top = dst_top + dm_top * decay_top
                dst_low = dst_low + dm_low * decay_low
                sums = jnp.sum(dm_top * top.astype(F32), axis=0, keepdims=True)
                more = jnp.sum(dm_low * low.astype(F32), axis=0, keepdims=True)
                rows_ref[pl.ds(per * q + h, 1), :] = jnp.concatenate([sums[:, :half], sums[:, half:] + more], axis=1)
            xdts.append(xdt.astype(F32))
            steps.append(step_p)
            dxdts.append(jnp.where(lane < head_dim, got[0], got[1]))
        dst_ref[:half, :] += dst_top
        dst_ref[half:, half:] += dst_low
        xdt = jnp.concatenate(xdts, axis=1)
        dxdt = jnp.concatenate(dxdts, axis=1)
        steps = jnp.concatenate(steps, axis=1)
        pick_row = lax.broadcasted_iota(jnp.int32, (WIDE, LANES), 0)
        pick_col = lax.broadcasted_iota(jnp.int32, (WIDE, LANES), 1)
        pick = jnp.where(pick_row // head_dim + per * q == pick_col, 1.0, 0.0).astype(BF16)
        both = xdt * dxdt
        high = both.astype(BF16)
        rest = (both - high.astype(F32)).astype(BF16)
        heads_ref[...] += dot(high, pick) + dot(rest, pick)
        direct_ref[...] += dot((dxdt * x).astype(BF16), pick)
        conv_back(q * WIDE, dxdt * steps + sk_ref[:, at] * dy)
        start(written(q * WIDE, WIDE, q) + written(inner + q * WIDE, WIDE, quads + q))
        return 0

    lax.fori_loop(0, quads, second_step, 0)

    d_scores = jnp.where(within, dst_ref[...], 0.0).astype(BF16)
    conv_back(inner, jnp.concatenate([dot(d_scores, queries), dot_tn(d_scores, keys)], axis=1))

    upper = jnp.where(within, 1.0, 0.0)
    d_rate = lax.dot_general(
        upper, jnp.transpose(rows_ref[...]) - heads_ref[...], (((1,), (0,)), ((), ())), precision=HIGH, preferred_element_type=F32
    )
    ddl_ref[...] = jnp.sum(d_rate * rate, axis=0, keepdims=True)
    d_step = direct_ref[...] - d_rate * jnp.exp(dl_ref[...])
    d_dt = d_step / (1.0 + jnp.exp(-v))
    ddtb_ref[...] = jnp.sum(d_dt, axis=0, keepdims=True)
    d_dt_low = d_dt[:, :heads].astype(BF16)
    dlowt_ref[inner + conv : proj, :] = jnp.transpose(d_dt)[:heads].astype(BF16)
    start(written(2 * inner, proj - 2 * inner, 2 * quads))

    wait(in_copy)
    u = u_ref[...].astype(F32)
    scale = lax.rsqrt(jnp.mean(u * u, axis=-1, keepdims=True) + EPS)

    def normed_step(n, _):
        at = cols(n * WIDE)
        dn_ref[:, at] = dot(dlow_ref[...], w[: inner + conv, at]) + dot(d_dt_low, w[inner + conv : proj, at])
        return 0

    lax.fori_loop(0, width // WIDE, normed_step, 0)
    dn = dn_ref[...]
    dng_ref[...] = jnp.sum(dn * u * scale, axis=0, keepdims=True)
    dn = dn * ng_ref[...]
    back = jnp.mean(dn * u, axis=-1, keepdims=True) * scale * scale * scale
    gin = g_ref[...].astype(F32) + dn * scale - u * back
    if full:
        gin_ref[...] = gin
    low_ref[...] = gin.astype(BF16)
    for q in range(quads):
        wait(written(q * WIDE, WIDE, q) + written(inner + q * WIDE, WIDE, quads + q))
    wait(written(2 * inner, proj - 2 * inner, 2 * quads))


def backward(u, g, seg_row, small, sizes, kept, w, ow, full=False):
    length, width, inner, conv, heads, taps = sizes
    blocks, proj = w.shape[:2]
    quads = inner // WIDE
    shape = jax.ShapeDtypeStruct
    outs = (shape((proj, length), BF16), shape((length, width), BF16), shape(small.shape, F32))
    outs += (shape((length, width), F32),) if full else ()
    zs, zslope, yf, x, slope, stream, dt = kept
    return pl.pallas_call(
        functools.partial(backward_body, sizes, full),
        out_shape=outs,
        in_specs=[vmem()] * 4 + [hbm()] * 6 + [vmem()] + [hbm()] * 2,
        out_specs=[hbm()] + [vmem()] * (len(outs) - 1),
        scratch_shapes=[
            pltpu.VMEM((proj, width), BF16),
            pltpu.VMEM((inner, width), BF16),
            pltpu.VMEM((length, inner), BF16),
            pltpu.VMEM((length, inner), BF16),
            pltpu.VMEM((length, inner), BF16),
            pltpu.VMEM((length, conv), BF16),
            pltpu.VMEM((length, conv), BF16),
            pltpu.VMEM((length, conv), BF16),
            pltpu.VMEM((proj, length), BF16),
            pltpu.VMEM((length, LANES), F32),
            pltpu.VMEM((taps - 1, length, LANES), F32),
            pltpu.VMEM((length, inner), F32),
            pltpu.VMEM((length, length), F32),
            pltpu.VMEM((length, length), F32),
            pltpu.VMEM((length, LANES), F32),
            pltpu.VMEM((length, LANES), F32),
            pltpu.VMEM((LANES, length), F32),
            pltpu.VMEM((length, LANES), F32),
            pltpu.VMEM((length, LANES), F32),
            pltpu.VMEM((LANES, length), F32),
            pltpu.VMEM((length, width), F32),
            pltpu.VMEM((length, inner + conv), BF16),
            pltpu.SemaphoreType.DMA((1, blocks)),
            pltpu.SemaphoreType.DMA((quads,)),
            pltpu.SemaphoreType.DMA((6, quads + 1)),
            pltpu.SemaphoreType.DMA((2 * quads + 1,)),
        ],
        compiler_params=pltpu.CompilerParams(vmem_limit_bytes=VMEM_BYTES),
        cost_estimate=pl.CostEstimate(
            flops=2 * length * (width * proj + inner * width + 4 * length * inner),
            bytes_accessed=2 * (width * proj + inner * width) + 8 * length * proj,
            transcendentals=length * (length * heads + 4 * inner),
        ),
        name="layer_backward",
    )(u, g, seg_row, small, zs, zslope, yf, x, slope, stream, dt, w, ow)


def flip(value, axis, distance):
    pairs = [(source, source ^ distance) for source in range(lax.axis_size(axis))]
    return lax.ppermute(value, axis, pairs)


def rotate(value, axis):
    count = lax.axis_size(axis)
    return lax.ppermute(value, axis, [(source, (source + 1) % count) for source in range(count)])


def distances(axis):
    found, d = [], 1
    while d < lax.axis_size(axis):
        found.append(d)
        d *= 2
    return found


def after(value, *others):
    return lax.optimization_barrier((value,) + others)[0]


def blank(shape, dtype):
    return pl.pallas_call(
        lambda out: None,
        out_shape=jax.ShapeDtypeStruct(shape, dtype),
        out_specs=hbm(),
        compiler_params=pltpu.CompilerParams(vmem_limit_bytes=1024 * 1024),
        name="blank",
    )()


class Line:
    def __init__(self):
        self.last = None

    def take(self, value):
        if self.last is not None:
            value, _ = lax.optimization_barrier((value, self.last))
        self.last = value
        return value


def gather_all(large, little, row):
    ring, share = lax.axis_size("fsdp"), lax.axis_size("dp")
    z, q = lax.axis_index("fsdp"), lax.axis_index("dp")
    far, near = distances("dp")[-1], list(reversed(distances("dp")[:-1]))
    line = Line()

    def begin(own):
        whole = lax.dynamic_update_slice(blank((ring,) + own.shape, own.dtype), own[None], (z, 0, 0, 0))
        return whole, lax.dynamic_index_in_dim(own, q, 0, keepdims=False)

    def place(whole, step, here, arrived):
        parts = {0: here, far: arrived}
        for d in near:
            parts.update({m | d: flip(v, "dp", d) for m, v in list(parts.items())})
        source = lax.rem(z - step + ring, ring)
        for m, v in parts.items():
            whole = lax.dynamic_update_slice(whole, v[None, None], (source, q ^ m, 0, 0))
        return whole

    large_all, travelling = begin(large)
    large_next = rotate(travelling, "fsdp")
    little_all, travelling = begin(little)
    little_next = rotate(travelling, "fsdp")
    rows = [after(row, travelling)]
    row_next = rotate(rows[0], "fsdp")
    waiting = None
    for step in range(1, ring):
        more = step + 1 < ring
        little_here = line.take(little_next)
        if more:
            little_next = rotate(little_here, "fsdp")
        little_far = flip(little_here, "dp", far)
        large_here = line.take(large_next)
        if more:
            large_next = rotate(large_here, "fsdp")
        if waiting is not None:
            large_all = place(large_all, step - 1, waiting[0], line.take(waiting[1]))
        waiting = (large_here, flip(large_here, "dp", far))
        rows.append(line.take(row_next))
        if more:
            row_next = rotate(rows[-1], "fsdp")
        little_all = place(little_all, step, little_here, line.take(little_far))
    large_all = place(large_all, ring - 1, waiting[0], line.take(waiting[1]))
    at = jnp.arange(ring)
    chosen = (lax.rem(z - at[:, None] + ring, ring) == at[None, :]).astype(row.dtype)
    row_all = jnp.dot(chosen, jnp.concatenate(rows, axis=0), preferred_element_type=F32)
    return large_all, little_all, row_all


def ring_places():
    ring, z = lax.axis_size("fsdp"), lax.axis_index("fsdp")
    return [lax.rem(z + 2 * ring - 1 - s, ring) for s in range(ring)]


def add(a, b):
    return a.astype(F32) + b.astype(F32)


def sum_far(near, level, mask):
    if level == 0:
        return near[mask]
    d = distances("dp")[level]
    away = [flip(v, "dp", d) for v in sum_far(near, level - 1, mask | d)]
    line = Line()
    return [add(a, line.take(b)).astype(BF16) for a, b in zip(sum_far(near, level - 1, mask), away)]


def sum_rings(near, early, rows):
    ring, levels = lax.axis_size("fsdp"), len(distances("dp")) - 1
    d = distances("dp")[-1]
    order = Line()
    ready = [order.take(v) for v in sum_far(near, levels - 1, d)]
    away = [flip(v, "dp", d) for v in ready]
    here = [order.take(v) for v in sum_far(near, levels - 1, 0)]
    line = Line()
    value, value_next = None, None
    early_value, early_at = early[0], 0
    early_next = rotate(early[0], "fsdp")

    def early_step(value, arrived, at):
        value = add(arrived, early[at + 1]).astype(BF16)
        return value, (rotate(value, "fsdp") if at + 2 < ring else None), at + 1

    early_value, early_next, early_at = early_step(early_value, after(early_next, ready[-1]), early_at)
    if early_next is not None:
        early_value, early_next, early_at = early_step(early_value, after(early_next, here[-1]), early_at)
    small, small_next = None, None
    for s in range(ring):
        part = add(here[s], line.take(away[s])).astype(BF16)
        value = part if s == 0 else add(line.take(value_next), part).astype(BF16)
        if s == 0:
            rows = after(rows, value)
            rows = rows + flip(rows, "dp", distances("dp")[0])
            small = [lax.dynamic_index_in_dim(rows, at, 0) for at in ring_places()]
            small_value, small_next = small[0], rotate(small[0], "fsdp")
        if s + 1 < ring:
            value_next = rotate(value, "fsdp")
        if early_next is not None:
            early_value, early_next, early_at = early_step(early_value, line.take(early_next), early_at)
        if s > 0:
            small_value = line.take(small_next) + small[s]
            if s + 1 < ring:
                small_next = rotate(small_value, "fsdp")
    small_value = after(small_value, value)
    for d in distances("dp")[1:]:
        small_value = small_value + flip(small_value, "dp", d)
    return value, early_value, small_value


def share_out(value, *behind):
    q = lax.axis_index("dp")
    owned = {0: value}
    for d in reversed(distances("dp")):
        arrived = {m | d: flip(v, "dp", d) for m, v in owned.items()}
        owned.update({m: after(v, *behind) if behind else v for m, v in arrived.items()})
    whole = blank((lax.axis_size("dp"),) + value.shape, F32)
    for m, v in owned.items():
        whole = lax.dynamic_update_slice(whole, v.astype(F32)[None], (q ^ m, 0, 0))
    return whole.reshape(-1, value.shape[1])


def far_masks():
    return range(0, lax.axis_size("dp"), 2)


def rows_near(left, right):
    ring, _, rows, depth = left.shape
    q, order = lax.axis_index("dp"), ring_places()

    def together(mask):
        mine = lax.dynamic_index_in_dim(left, q ^ mask, 1, keepdims=False)
        mine = jnp.concatenate([lax.dynamic_index_in_dim(mine, at, 0) for at in order], axis=0)
        product = jnp.dot(mine.reshape(ring * rows, depth), right, preferred_element_type=F32)
        return product.astype(BF16).reshape(ring, rows, -1)

    near = {}
    for mask in reversed(far_masks()):
        arrived = flip(together(mask | 1), "dp", 1)
        both = add(together(mask), arrived).astype(BF16)
        near[mask] = [both[s] for s in range(ring)]
    return near


def columns_near(left, right):
    ring, depth = lax.axis_size("fsdp"), right.shape[0]
    order = ring_places()
    block = right.shape[1] // ring
    rights = [lax.dynamic_slice(right, (0, at * block), (depth, block)) for at in order]
    every = jnp.concatenate(rights, axis=1)
    near = {}
    for mask in reversed(far_masks()):
        away = jnp.dot(left(mask | 1), every, preferred_element_type=F32).astype(BF16)
        arrived = flip(away, "dp", 1)
        here = left(mask)
        near[mask] = [
            add(jnp.dot(here, rights[s], preferred_element_type=F32), arrived[:, s * block : (s + 1) * block]).astype(BF16)
            for s in range(ring)
        ]
    return near


def shards(
    inputs,
    cotangent,
    segments,
    norm_gain,
    in_weight,
    conv_weight,
    conv_bias,
    dt_bias,
    decay_log,
    skip_gain,
    gate_gain,
    out_weight,
):
    first = lax.axis_index("section") == 0
    z = lax.axis_index("fsdp")
    ring, share = lax.axis_size("fsdp"), lax.axis_size("dp")
    length, width = inputs.shape[2], inputs.shape[3]
    taps = conv_weight.shape[1]
    heads = dt_bias.shape[1] * ring
    inner = gate_gain.shape[1] * ring
    head_dim = inner // heads

    pieces = (norm_gain[0], conv_bias[0], dt_bias[0], decay_log[0], skip_gain[0], gate_gain[0], conv_weight[0].reshape(-1))
    sizes = [piece.shape[0] for piece in pieces]
    proj = in_weight.shape[2]
    w, ow, packed = gather_all(
        in_weight[0].T.reshape(share, proj // share, -1),
        out_weight[0].reshape(share, -1, width),
        jnp.concatenate(pieces)[None],
    )
    w = w.reshape(ring, proj, -1)
    ow = ow.reshape(inner, width)
    fields, start = [], 0
    for size in sizes:
        fields.append(packed[:, start : start + size])
        start += size
    taps_w = fields[6].reshape(ring, taps, -1).transpose(1, 0, 2).reshape(taps, -1)
    rows = [field.reshape(1, -1) for field in fields[:6]]

    conv_width = conv_bias.shape[1] * ring

    def padded(row):
        return jnp.pad(row, ((0, 0), (0, conv_width - row.shape[1])))

    wide_rows = [rows[0], rows[1], rows[2], rows[3], jnp.repeat(rows[4], head_dim, axis=1), rows[5]]
    filler = jnp.zeros((-(taps + len(wide_rows)) % 8, conv_width), F32)
    small = jnp.concatenate([taps_w] + [padded(row) for row in wide_rows] + [filler], axis=0)
    sizes_of = (length, width, inner, conv_width, heads, taps)
    seg = segments[:, 0].astype(F32)
    seg_rows = [jnp.broadcast_to(seg[m][None], (8, length)) for m in range(2)]
    pick = functools.partial(jnp.where, first)

    def to_second(value):
        return lax.ppermute(value, "section", [(0, 1)])

    def to_first(value):
        return lax.ppermute(value, "section", [(1, 0)])

    u_a, u_b = inputs[0, 0], inputs[1, 0]
    g_a, g_b = cotangent[0, 0], cotangent[1, 0]

    seg1, seg3 = pick(seg_rows[1], seg_rows[0]), pick(seg_rows[0], seg_rows[1])
    w, small, u_a, u_b, g_a, g_b, seg1, seg3, seg0 = lax.optimization_barrier(
        (w, small, u_a, u_b, g_a, g_b, seg1, seg3, seg_rows[0])
    )
    out0 = forward(u_a, seg0, small, sizes_of, w, ow, keep=False)[0]
    u1 = pick(u_b, to_second(out0))
    out1, *kept1, normed1, mixed1 = forward(u1, seg1, small, sizes_of, w, ow)
    stream_b = to_second(out1)
    back2 = backward(u1, g_a, seg1, small, sizes_of, kept1, w, ow)
    grad_a = to_first(back2[1])
    u3 = pick(u_a, stream_b)
    out3, *kept3, normed3, mixed3 = forward(u3, seg3, small, sizes_of, w, ow)
    g4 = pick(grad_a, g_b)
    back4 = backward(u3, g4, seg3, small, sizes_of, kept3, w, ow, full=True)
    grad_b = to_first(back4[1])

    mixed_both = after(jnp.concatenate([mixed3, mixed1], axis=0), back4[1])
    mixed_t = mixed_both.T.reshape(ring, share, -1, 2 * length)
    near_out = rows_near(mixed_t, jnp.concatenate([g4, pick(grad_b, g_a)], axis=0))
    ahead = [v for parts in near_out.values() for v in parts]
    back5 = backward(after(u1, *ahead), grad_b, seg1, small, sizes_of, kept1, w, ow)

    levels = len(distances("dp")) - 1
    far_out = sum_far(near_out, levels, 0)
    normed = jnp.concatenate([normed3, normed1], axis=0)
    q = lax.axis_index("dp")
    back5_t = after(back5[0], *far_out)

    def left(mask):
        def part(value):
            return lax.dynamic_index_in_dim(value.reshape(share, -1, length), q ^ mask, 0, keepdims=False)

        return jnp.concatenate([part(back4[0]), pick(part(back5_t), part(back2[0]))], axis=1)

    near_in = columns_near(left, normed)
    grad = back4[2] + pick(back5[2], back2[2])

    def field(k, size):
        return grad[taps + k, :size].reshape(ring, -1)

    packed = jnp.concatenate(
        [
            field(0, width),
            field(1, conv_width),
            field(2, heads),
            field(3, heads),
            jnp.sum(grad[taps + 4, :inner].reshape(heads, head_dim), axis=1).reshape(ring, -1),
            field(5, inner),
            grad[:taps].reshape(taps, ring, -1).transpose(1, 0, 2).reshape(ring, -1),
        ],
        axis=1,
    )
    own_in, own_out, packed = sum_rings(near_in, far_out, packed)
    in_grad = share_out(own_in).T[None]
    out_grad = share_out(own_out, own_in)[None]
    begun = near_in[0][0]
    output = pick(after(to_first(after(out1, begun)), own_in), out3)
    input_grad = pick(back4[3], after(to_second(after(back5[1], begun)), own_in).astype(F32))
    fields, start = [], 0
    for size in sizes:
        fields.append(packed[:, start : start + size])
        start += size
    return (
        output[None, None],
        input_grad[None, None],
        fields[0],
        in_grad,
        fields[6].reshape(1, taps, -1),
        fields[1],
        fields[2],
        fields[3],
        fields[4],
        fields[5],
        out_grad,
    )


def solution(mesh):
    spread_over = ("fsdp", "dp")
    row = P("section", "fsdp")
    matrix = P("section", "fsdp", None)
    tap = P("section", None, "fsdp")
    activation = P(None, spread_over, None, None)
    result = P("section", spread_over, None, None)
    return jax.shard_map(
        shards,
        mesh=mesh,
        in_specs=(activation, activation, P(None, spread_over, None), row, matrix, tap, row, row, row, row, row, matrix),
        out_specs=(result, result, row, matrix, tap, row, row, row, row, row, matrix),
        check_vma=False,
    )
```

```python
import functools

import jax
import jax.numpy as jnp
from jax import lax
from jax.experimental import pallas as pl
from jax.experimental.pallas import tpu as pltpu
from jax.sharding import PartitionSpec as P

EPS = 1e-05
LOG2E = 1.4426950408889634
HIGH = lax.Precision.HIGHEST
F32 = jnp.float32
BF16 = jnp.bfloat16
LANES = 128
WIDE = 256
VMEM_BYTES = 56 * 1024 * 1024


def sigmoid(v):
    return 0.5 * jnp.tanh(0.5 * v) + 0.5


def dot(a, b):
    return lax.dot_general(a, b, (((1,), (0,)), ((), ())), preferred_element_type=F32)


def dot_nt(a, b):
    return lax.dot_general(a, b, (((1,), (1,)), ((), ())), preferred_element_type=F32)


def dot_tn(a, b):
    return lax.dot_general(a, b, (((0,), (0,)), ((), ())), preferred_element_type=F32)


def twice(v):
    return jnp.concatenate([v, v], axis=1)


def fold(v):
    return v[:, :LANES] + v[:, LANES:]


def cols(start, width=WIDE):
    return pl.ds(pl.multiple_of(start, LANES), width)


def weight_copies(source, target, rows, sem, k):
    blocks, _, width = source.shape
    return [
        pltpu.make_async_copy(
            source.at[b, rows, :], target.at[rows, b * width : (b + 1) * width], sem.at[k, b]
        )
        for b in range(blocks)
    ]


def start(copies):
    for copy in copies:
        copy.start()


def wait(copies):
    for copy in copies:
        copy.wait()


def small_rows(small_ref, width, inner, conv, taps):
    row = lambda k, size: small_ref.at[taps + k : taps + k + 1, :size]
    return (
        row(0, width),
        small_ref.at[:taps],
        row(1, conv),
        row(2, LANES),
        row(3, LANES),
        row(4, inner),
        row(5, inner),
    )


def column_of(segr_ref):
    row = jnp.broadcast_to(segr_ref[:1, :], (LANES, segr_ref.shape[1]))
    return jnp.transpose(row)


def write_masks(segc_ref, mask_ref, taps):
    seg = segc_ref[...]
    row = lax.broadcasted_iota(jnp.int32, seg.shape, 0)
    for lag in range(1, taps):
        same = (pltpu.roll(seg, lag, 0) == seg) & (row >= lag)
        mask_ref[lag - 1] = jnp.where(same, 1.0, 0.0)


def conv_chunk(s, start, cw_ref, cb_ref, mask_ref, taps):
    at = cols(start)
    total = cb_ref[:, at] + s * cw_ref[pl.ds(taps - 1, 1), at]
    for lag in range(1, taps):
        shifted = pltpu.roll(s, lag, 0) * twice(mask_ref[lag - 1])
        total = total + shifted * cw_ref[pl.ds(taps - 1 - lag, 1), at]
    return total


def step_sizes(dt, dtb_ref, dl_ref, heads):
    length = dt.shape[0]
    pad = jnp.zeros((length, LANES - heads), F32)
    v = jnp.concatenate([dt, pad], axis=1) + dtb_ref[...]
    step = jnp.maximum(v, 0.0) + jnp.log1p(jnp.exp(-jnp.abs(v)))
    rate = -jnp.exp(dl_ref[...]) * step
    i = lax.broadcasted_iota(jnp.int32, (length, length), 0)
    j = lax.broadcasted_iota(jnp.int32, (length, length), 1)
    lower = jnp.where(i >= j, 1.0, 0.0)
    scaled = rate * LOG2E
    cumul = lax.dot_general(lower, scaled, (((1,), (0,)), ((), ())), precision=HIGH, preferred_element_type=F32)
    return v, step, rate, cumul


def head_lanes(v, quad, per):
    return pltpu.roll(v, lax.rem(LANES - per * quad, LANES), 1)


def spread(v, i0, head_dim):
    length = v.shape[0]
    lane = lax.broadcasted_iota(jnp.int32, (length, LANES), 1)
    a = jnp.broadcast_to(v[:, i0 : i0 + 1], (length, LANES))
    b = jnp.broadcast_to(v[:, i0 + 1 : i0 + 2], (length, LANES))
    return jnp.where(lane < head_dim, a, b)


def forward_body(
    sizes, keep, u_ref, segr_ref, small_ref, w_hbm, *refs
):
    length, width, inner, conv, heads, taps = sizes
    ng_ref, cw_ref, cb_ref, dtb_ref, dl_ref, sk_ref, gg_ref = small_rows(small_ref, width, inner, conv, taps)
    ow_hbm, refs = (refs[0], refs[1:]) if keep else (None, refs)
    count = 10 if keep else 1
    outs, held, refs = refs[:count], refs[count : count + 10], refs[count + 10 :]
    out_ref, zs_ref, zslope_ref, yf_ref, x_ref, slope_ref, stream_ref, dt_ref, normed_ref, mixed_ref = held
    w, ow, segc_ref, mask_ref, s_ref, gated_ref, gate_ref, cum_ref, step_ref, cumt_ref, sem, osem, wsem = refs
    state = (conv - inner) // 2
    head_dim = inner // heads
    per = WIDE // head_dim
    quads = inner // WIDE
    half = length // 2
    proj = w.shape[0]
    tail = 2 * inner

    def written(k, at, j):
        if keep or k == 9:
            return [pltpu.make_async_copy(held[k].at[:, at], outs[k if keep else 0].at[:, at], wsem.at[k, j])]
        return []


    def copies(at, k):
        return weight_copies(w_hbm, w, at, sem, k)

    def stream_copy(q):
        return copies(cols(inner + q * WIDE), 1 + 2 * q)

    def gate_copy(q):
        return copies(cols(q * WIDE), 2 + 2 * q)

    tail_copy = copies(pl.ds(tail, proj - tail), 0)
    start(tail_copy)
    ahead = min(3, quads)
    for q in range(ahead):
        start(stream_copy(q))
        start(gate_copy(q))
    out_copy = pltpu.make_async_copy(ow_hbm, ow, osem) if keep else None

    u = u_ref[...].astype(F32)
    scale = lax.rsqrt(jnp.mean(u * u, axis=-1, keepdims=True) + EPS)
    normed_ref[...] = (u * scale * ng_ref[...]).astype(BF16)
    start(written(8, pl.ds(0, width), 0))
    segc_ref[...] = column_of(segr_ref)
    write_masks(segc_ref, mask_ref, taps)

    def project(q):
        rows = cols(inner + q * WIDE)
        stream_ref[:, cols(q * WIDE)] = dot_nt(normed_ref[...], w[rows, :]).astype(BF16)
        gate_ref[:, cols(q * WIDE)] = dot_nt(normed_ref[...], w[cols(q * WIDE), :])

    wait(tail_copy)
    dt = dot_nt(normed_ref[...], w[inner + conv : proj, :])
    dt_ref[...] = dt
    start(written(7, pl.ds(0, heads), 0))
    stream_ref[:, cols(inner)] = dot_nt(normed_ref[...], w[tail : tail + 2 * state, :]).astype(BF16)
    _, step, _, cumul = step_sizes(dt, dtb_ref, dl_ref, heads)
    step_ref[...] = step
    cum_ref[...] = cumul
    cumt_ref[...] = jnp.transpose(cumul)
    wait(stream_copy(0))
    wait(gate_copy(0))
    project(0)

    def conv_of(first):
        at = cols(first)
        total = conv_chunk(stream_ref[:, at].astype(F32), first, cw_ref, cb_ref, mask_ref, taps)
        sig = sigmoid(total)
        x = total * sig
        if keep:
            x_ref[:, at] = x.astype(BF16)
            slope_ref[:, at] = (sig + x * (1.0 - sig)).astype(BF16)
        return x

    bc = conv_of(inner)
    start(written(4, cols(inner), quads) + written(5, cols(inner), quads) + written(6, cols(inner), quads))
    keys = bc[:, :state].astype(BF16)
    queries = bc[:, state:].astype(BF16)
    i = lax.broadcasted_iota(jnp.int32, (length, length), 0)
    j = lax.broadcasted_iota(jnp.int32, (length, length), 1)
    within = (i >= j) & (segc_ref[:, :1] == segr_ref[:1, :])
    s_ref[...] = jnp.where(within, dot_nt(queries, keys), 0.0)

    def quad_step(q, squares, more=True):
        at = cols(q * WIDE)
        if more:

            @pl.when(q + ahead < quads)
            def _():
                start(stream_copy(q + ahead))
                start(gate_copy(q + ahead))

            if keep:

                @pl.when(q + ahead == quads)
                def _():
                    out_copy.start()

            wait(stream_copy(q + 1))
            wait(gate_copy(q + 1))
        x = conv_of(q * WIDE)
        z = gate_ref[:, at]
        sig = sigmoid(z)
        zs = z * sig
        if keep:
            zs_ref[:, at] = zs.astype(BF16)
            zslope_ref[:, at] = (sig + zs * (1.0 - sig)).astype(BF16)
        if more:
            project(q + 1)
        cum_q = head_lanes(cum_ref[...], q, per)
        step_q = head_lanes(step_ref[...], q, per)
        ys = []
        for pair in range(per // 2):
            part = slice(pair * LANES, (pair + 1) * LANES)
            xdt = (x[:, part] * spread(step_q, 2 * pair, head_dim)).astype(BF16)
            got = []
            for k in range(2):
                h = 2 * pair + k
                col = cum_q[:, h : h + 1]
                row = cumt_ref[pl.ds(per * q + h, 1), :]
                top = jnp.exp2(jnp.minimum(col[:half] - row[:, :half], 0.0)) * s_ref[:half, :half]
                low = jnp.exp2(jnp.minimum(col[half:] - row, 0.0)) * s_ref[half:, :]
                got.append(
                    jnp.concatenate(
                        [dot(top.astype(BF16), xdt[:half]), dot(low.astype(BF16), xdt)], axis=0
                    )
                )
            lane = lax.broadcasted_iota(jnp.int32, (length, LANES), 1)
            ys.append(jnp.where(lane < head_dim, got[0], got[1]))
        yf = jnp.concatenate(ys, axis=1) + sk_ref[:, at] * x
        gated = yf * zs
        if keep:
            yf_ref[:, at] = yf.astype(BF16)
        gated_ref[:, at] = gated
        for k in range(1, 7):
            start(written(k, at, q))
        return squares + fold(gated * gated)

    squares = lax.fori_loop(0, quads - 1, quad_step, jnp.zeros((length, LANES), F32))
    squares = quad_step(quads - 1, squares, more=False)
    scale2 = lax.rsqrt(jnp.sum(squares, axis=-1, keepdims=True) * (1.0 / inner) + EPS)

    for q in range(quads):
        at = cols(q * WIDE)
        mixed_ref[:, at] = (gated_ref[:, at] * scale2 * gg_ref[:, at]).astype(BF16)
        start(written(9, at, q))
    if keep:
        out_copy.wait()
    for n in range(width // WIDE if keep else 0):
        at = cols(n * WIDE)
        out_ref[:, at] = (u_ref[:, at].astype(F32) + dot(mixed_ref[...], ow[:, at])).astype(BF16)
        start(written(0, at, n))
    for n in range(width // WIDE if keep else 0):
        wait(written(0, cols(n * WIDE), n))
    wait(written(7, pl.ds(0, heads), 0) + written(8, pl.ds(0, width), 0))
    wait(written(4, cols(inner), quads) + written(5, cols(inner), quads) + written(6, cols(inner), quads))
    for q in range(quads):
        for k in (1, 2, 3, 4, 5, 6, 9):
            wait(written(k, cols(q * WIDE), q))


def vmem():
    return pl.BlockSpec(memory_space=pltpu.VMEM)


def hbm():
    return pl.BlockSpec(memory_space=pl.ANY)


def forward(u, seg_row, small, sizes, w, ow=None):
    keep = ow is not None
    length, width, inner, conv, heads, taps = sizes
    blocks, proj = w.shape[:2]
    quads = inner // WIDE
    held = (
        ((length, width), BF16),
        ((length, inner), BF16),
        ((length, inner), BF16),
        ((length, inner), BF16),
        ((length, conv), BF16),
        ((length, conv), BF16),
        ((length, conv), BF16),
        ((length, heads), F32),
        ((length, width), BF16),
        ((length, inner), BF16),
    )
    outs = held if keep else held[9:]
    weights = (w, ow) if keep else (w,)
    return pl.pallas_call(
        functools.partial(forward_body, sizes, keep),
        out_shape=tuple(jax.ShapeDtypeStruct(*out) for out in outs),
        in_specs=[vmem()] * 3 + [hbm()] * len(weights),
        out_specs=[hbm()] * len(outs),
        scratch_shapes=[pltpu.VMEM(*one) for one in held]
        + [
            pltpu.VMEM((proj, width), BF16),
            pltpu.VMEM((inner, width), BF16),
            pltpu.VMEM((length, LANES), F32),
            pltpu.VMEM((taps - 1, length, LANES), F32),
            pltpu.VMEM((length, length), F32),
            pltpu.VMEM((length, inner), F32),
            pltpu.VMEM((length, inner), F32),
            pltpu.VMEM((length, LANES), F32),
            pltpu.VMEM((length, LANES), F32),
            pltpu.VMEM((LANES, length), F32),
            pltpu.SemaphoreType.DMA((1 + 2 * quads, blocks)),
            pltpu.SemaphoreType.DMA,
            pltpu.SemaphoreType.DMA((10, quads + 1)),
        ],
        compiler_params=pltpu.CompilerParams(vmem_limit_bytes=VMEM_BYTES),
        cost_estimate=pl.CostEstimate(
            flops=2 * length * (width * proj + inner * width + 2 * length * inner),
            bytes_accessed=2 * (width * proj + inner * width),
            transcendentals=length * (length * heads + 2 * inner),
        ),
        name="layer_forward",
    )(u, seg_row, small, *weights)


def backward_body(
    sizes, full, u_ref, g_ref, segr_ref, small_ref, zs_hbm, zslope_hbm, yf_hbm, x_hbm, slope_hbm, stream_hbm, dt_ref, w_hbm, ow_hbm,
    dlowt_hbm, low_ref, dsmall_ref, *refs,
):
    length, width, inner, conv, heads, taps = sizes
    ng_ref, cw_ref, cb_ref, dtb_ref, dl_ref, sk_ref, gg_ref = small_rows(small_ref, width, inner, conv, taps)
    dng_ref, dcw_ref, dcb_ref, ddtb_ref, ddl_ref, dsk_ref, dgg_ref = small_rows(
        dsmall_ref, width, inner, conv, taps
    )
    gin_ref = refs[0] if full else None
    (
        w, ow, zs_ref, zslope_ref, yf_ref, x_ref, slope_ref, stream_ref, dlowt_ref, segc_ref, mask_ref, dm_ref, st_ref, dst_ref,
        cum_ref, step_ref, cumt_ref, heads_ref, direct_ref, rows_ref, dn_ref, dlow_ref, sem, osem, rsem, wsem,
    ) = refs[1 if full else 0 :]
    state = (conv - inner) // 2
    head_dim = inner // heads
    per = WIDE // head_dim
    quads = inner // WIDE
    half = length // 2
    proj = w.shape[0]

    def fetch(k, source, target, at, j):
        return pltpu.make_async_copy(source.at[:, at], target.at[:, at], rsem.at[k, j])

    def read(q):
        at = pl.ds(pl.multiple_of(q * WIDE, WIDE), WIDE)
        return [
            pltpu.make_async_copy(ow_hbm.at[at, :], ow.at[at, :], osem.at[q]),
            fetch(0, zs_hbm, zs_ref, at, q),
            fetch(1, yf_hbm, yf_ref, at, q),
        ]

    def read_later(q):
        at = pl.ds(pl.multiple_of(q * WIDE, WIDE), WIDE)
        return [
            fetch(2, x_hbm, x_ref, at, q),
            fetch(3, slope_hbm, slope_ref, at, q),
            fetch(4, stream_hbm, stream_ref, at, q),
            fetch(5, zslope_hbm, zslope_ref, at, q),
        ]

    last = pl.ds(inner, conv - inner)
    read_last = [
        fetch(2, x_hbm, x_ref, last, quads),
        fetch(3, slope_hbm, slope_ref, last, quads),
        fetch(4, stream_hbm, stream_ref, last, quads),
    ]
    for q in range(quads):
        start(read(q))
    start(read_last)
    in_copy = weight_copies(w_hbm, w, pl.ds(0, proj), sem, 0)

    def written(first, size, j):
        rows = pl.ds(pl.multiple_of(first, 32), size)
        return [pltpu.make_async_copy(dlowt_ref.at[rows, :], dlowt_hbm.at[rows, :], wsem.at[j])]

    dsmall_ref[...] = jnp.zeros_like(dsmall_ref)
    segc_ref[...] = column_of(segr_ref)
    write_masks(segc_ref, mask_ref, taps)
    v, step, rate, cumul = step_sizes(dt_ref[...], dtb_ref, dl_ref, heads)
    step_ref[...] = step
    cum_ref[...] = cumul
    cumt_ref[...] = jnp.transpose(cumul)
    heads_ref[...] = jnp.zeros_like(heads_ref)
    direct_ref[...] = jnp.zeros_like(direct_ref)
    dst_ref[...] = jnp.zeros_like(dst_ref)
    rows_ref[...] = jnp.zeros_like(rows_ref)

    def first_step(q, carry):
        squares, cross = carry
        at = cols(q * WIDE)
        wait(read(q))
        start(read_later(q))
        dm = dot_nt(g_ref[...], ow[pl.ds(pl.multiple_of(q * WIDE, WIDE), WIDE), :])
        gated = yf_ref[:, at].astype(F32) * zs_ref[:, at].astype(F32)
        dm_ref[:, at] = dm
        return squares + fold(gated * gated), cross + fold(gated * (dm * gg_ref[:, at]))

    zero = jnp.zeros((length, LANES), F32)
    squares, cross = lax.fori_loop(0, quads, first_step, (zero, zero))
    scale2 = lax.rsqrt(jnp.sum(squares, axis=-1, keepdims=True) * (1.0 / inner) + EPS)
    back2 = jnp.sum(cross, axis=-1, keepdims=True) * scale2 * scale2 * scale2 * (1.0 / inner)

    start(in_copy)
    wait(read_last)
    keys = x_ref[:, inner : inner + state]
    queries = x_ref[:, inner + state : inner + 2 * state]
    j = lax.broadcasted_iota(jnp.int32, (length, length), 0)
    i = lax.broadcasted_iota(jnp.int32, (length, length), 1)
    within = (i >= j) & (segc_ref[:, :1] == segr_ref[:1, :])
    st_ref[...] = jnp.where(within, dot_nt(keys, queries), 0.0)

    def write_low(at, value):
        low = value.astype(BF16)
        dlow_ref[:, at] = low
        dlowt_ref[at, :] = jnp.transpose(low)

    def conv_back(start, d_conv):
        at = cols(start)
        d_total = d_conv * slope_ref[:, at].astype(F32)
        s = stream_ref[:, at].astype(F32)
        dcb_ref[:, at] = jnp.sum(d_total, axis=0, keepdims=True)
        dcw_ref[pl.ds(taps - 1, 1), at] = jnp.sum(d_total * s, axis=0, keepdims=True)
        d_stream = d_total * cw_ref[pl.ds(taps - 1, 1), at]
        for lag in range(1, taps):
            back = pltpu.roll(d_total * twice(mask_ref[lag - 1]), length - lag, 0)
            dcw_ref[pl.ds(taps - 1 - lag, 1), at] = jnp.sum(back * s, axis=0, keepdims=True)
            d_stream = d_stream + back * cw_ref[pl.ds(taps - 1 - lag, 1), at]
        write_low(cols(inner + start), d_stream)

    def second_step(q, _):
        at = cols(q * WIDE)
        wait(read_later(q))
        x = x_ref[:, at].astype(F32)
        zs = zs_ref[:, at].astype(F32)
        yf = yf_ref[:, at].astype(F32)
        gated = yf * zs
        scaled = dm_ref[:, at] * scale2
        dgg_ref[:, at] = jnp.sum(scaled * gated, axis=0, keepdims=True)
        d_gated = scaled * gg_ref[:, at] - gated * back2
        dy = d_gated * zs
        write_low(at, d_gated * yf * zslope_ref[:, at].astype(F32))
        dsk_ref[:, at] = jnp.sum(dy * x, axis=0, keepdims=True)
        dy_low = dy.astype(BF16)
        cum_q = head_lanes(cum_ref[...], q, per)
        step_q = head_lanes(step_ref[...], q, per)
        lane = lax.broadcasted_iota(jnp.int32, (length, LANES), 1)
        dst_top = jnp.zeros((half, length), F32)
        dst_low = jnp.zeros((half, half), F32)
        xdts, dxdts, steps = [], [], []
        for pair in range(per // 2):
            part = slice(pair * LANES, (pair + 1) * LANES)
            step_p = spread(step_q, 2 * pair, head_dim)
            xdt = (x[:, part] * step_p).astype(BF16)
            dyp = dy_low[:, part]
            got = []
            for k in range(2):
                h = 2 * pair + k
                mine = (lane < head_dim) if k == 0 else (lane >= head_dim)
                xm = jnp.where(mine, xdt.astype(F32), 0.0).astype(BF16)
                col = cum_q[:, h : h + 1]
                row = cumt_ref[pl.ds(per * q + h, 1), :]
                decay_top = jnp.exp2(jnp.minimum(row - col[:half], 0.0))
                decay_low = jnp.exp2(jnp.minimum(row[:, half:] - col[half:], 0.0))
                top = (decay_top * st_ref[:half, :]).astype(BF16)
                low = (decay_low * st_ref[half:, half:]).astype(BF16)
                got.append(jnp.concatenate([dot(top, dyp), dot(low, dyp[half:])], axis=0))
                dm_top = dot_nt(xm[:half], dyp)
                dm_low = dot_nt(xm[half:], dyp[half:])
                dst_top = dst_top + dm_top * decay_top
                dst_low = dst_low + dm_low * decay_low
                sums = jnp.sum(dm_top * top.astype(F32), axis=0, keepdims=True)
                more = jnp.sum(dm_low * low.astype(F32), axis=0, keepdims=True)
                rows_ref[pl.ds(per * q + h, 1), :] = jnp.concatenate([sums[:, :half], sums[:, half:] + more], axis=1)
            xdts.append(xdt.astype(F32))
            steps.append(step_p)
            dxdts.append(jnp.where(lane < head_dim, got[0], got[1]))
        dst_ref[:half, :] += dst_top
        dst_ref[half:, half:] += dst_low
        xdt = jnp.concatenate(xdts, axis=1)
        dxdt = jnp.concatenate(dxdts, axis=1)
        steps = jnp.concatenate(steps, axis=1)
        pick_row = lax.broadcasted_iota(jnp.int32, (WIDE, LANES), 0)
        pick_col = lax.broadcasted_iota(jnp.int32, (WIDE, LANES), 1)
        pick = jnp.where(pick_row // head_dim + per * q == pick_col, 1.0, 0.0).astype(BF16)
        both = xdt * dxdt
        high = both.astype(BF16)
        rest = (both - high.astype(F32)).astype(BF16)
        heads_ref[...] += dot(high, pick) + dot(rest, pick)
        direct_ref[...] += dot((dxdt * x).astype(BF16), pick)
        conv_back(q * WIDE, dxdt * steps + sk_ref[:, at] * dy)
        start(written(q * WIDE, WIDE, q) + written(inner + q * WIDE, WIDE, quads + q))
        return 0

    lax.fori_loop(0, quads, second_step, 0)

    d_scores = jnp.where(within, dst_ref[...], 0.0).astype(BF16)
    conv_back(inner, jnp.concatenate([dot(d_scores, queries), dot_tn(d_scores, keys)], axis=1))

    upper = jnp.where(within, 1.0, 0.0)
    d_rate = lax.dot_general(
        upper, jnp.transpose(rows_ref[...]) - heads_ref[...], (((1,), (0,)), ((), ())), precision=HIGH, preferred_element_type=F32
    )
    ddl_ref[...] = jnp.sum(d_rate * rate, axis=0, keepdims=True)
    d_step = direct_ref[...] - d_rate * jnp.exp(dl_ref[...])
    d_dt = d_step / (1.0 + jnp.exp(-v))
    ddtb_ref[...] = jnp.sum(d_dt, axis=0, keepdims=True)
    d_dt_low = d_dt[:, :heads].astype(BF16)
    dlowt_ref[inner + conv : proj, :] = jnp.transpose(d_dt)[:heads].astype(BF16)
    start(written(2 * inner, proj - 2 * inner, 2 * quads))

    wait(in_copy)
    u = u_ref[...].astype(F32)
    scale = lax.rsqrt(jnp.mean(u * u, axis=-1, keepdims=True) + EPS)

    def normed_step(n, _):
        at = cols(n * WIDE)
        dn_ref[:, at] = dot(dlow_ref[...], w[: inner + conv, at]) + dot(d_dt_low, w[inner + conv : proj, at])
        return 0

    lax.fori_loop(0, width // WIDE, normed_step, 0)
    dn = dn_ref[...]
    dng_ref[...] = jnp.sum(dn * u * scale, axis=0, keepdims=True)
    dn = dn * ng_ref[...]
    back = jnp.mean(dn * u, axis=-1, keepdims=True) * scale * scale * scale
    gin = g_ref[...].astype(F32) + dn * scale - u * back
    if full:
        gin_ref[...] = gin
    low_ref[...] = gin.astype(BF16)
    for q in range(quads):
        wait(written(q * WIDE, WIDE, q) + written(inner + q * WIDE, WIDE, quads + q))
    wait(written(2 * inner, proj - 2 * inner, 2 * quads))


def backward(u, g, seg_row, small, sizes, kept, w, ow, full=False):
    length, width, inner, conv, heads, taps = sizes
    blocks, proj = w.shape[:2]
    quads = inner // WIDE
    shape = jax.ShapeDtypeStruct
    outs = (shape((proj, length), BF16), shape((length, width), BF16), shape(small.shape, F32))
    outs += (shape((length, width), F32),) if full else ()
    zs, zslope, yf, x, slope, stream, dt = kept
    return pl.pallas_call(
        functools.partial(backward_body, sizes, full),
        out_shape=outs,
        in_specs=[vmem()] * 4 + [hbm()] * 6 + [vmem()] + [hbm()] * 2,
        out_specs=[hbm()] + [vmem()] * (len(outs) - 1),
        scratch_shapes=[
            pltpu.VMEM((proj, width), BF16),
            pltpu.VMEM((inner, width), BF16),
            pltpu.VMEM((length, inner), BF16),
            pltpu.VMEM((length, inner), BF16),
            pltpu.VMEM((length, inner), BF16),
            pltpu.VMEM((length, conv), BF16),
            pltpu.VMEM((length, conv), BF16),
            pltpu.VMEM((length, conv), BF16),
            pltpu.VMEM((proj, length), BF16),
            pltpu.VMEM((length, LANES), F32),
            pltpu.VMEM((taps - 1, length, LANES), F32),
            pltpu.VMEM((length, inner), F32),
            pltpu.VMEM((length, length), F32),
            pltpu.VMEM((length, length), F32),
            pltpu.VMEM((length, LANES), F32),
            pltpu.VMEM((length, LANES), F32),
            pltpu.VMEM((LANES, length), F32),
            pltpu.VMEM((length, LANES), F32),
            pltpu.VMEM((length, LANES), F32),
            pltpu.VMEM((LANES, length), F32),
            pltpu.VMEM((length, width), F32),
            pltpu.VMEM((length, inner + conv), BF16),
            pltpu.SemaphoreType.DMA((1, blocks)),
            pltpu.SemaphoreType.DMA((quads,)),
            pltpu.SemaphoreType.DMA((6, quads + 1)),
            pltpu.SemaphoreType.DMA((2 * quads + 1,)),
        ],
        compiler_params=pltpu.CompilerParams(vmem_limit_bytes=VMEM_BYTES),
        cost_estimate=pl.CostEstimate(
            flops=2 * length * (width * proj + inner * width + 4 * length * inner),
            bytes_accessed=2 * (width * proj + inner * width) + 8 * length * proj,
            transcendentals=length * (length * heads + 4 * inner),
        ),
        name="layer_backward",
    )(u, g, seg_row, small, zs, zslope, yf, x, slope, stream, dt, w, ow)


def flip(value, axis, distance):
    pairs = [(source, source ^ distance) for source in range(lax.axis_size(axis))]
    return lax.ppermute(value, axis, pairs)


def rotate(value, axis):
    count = lax.axis_size(axis)
    return lax.ppermute(value, axis, [(source, (source + 1) % count) for source in range(count)])


def distances(axis):
    found, d = [], 1
    while d < lax.axis_size(axis):
        found.append(d)
        d *= 2
    return found


def after(value, *others):
    return lax.optimization_barrier((value,) + others)[0]


def blank(shape, dtype):
    return pl.pallas_call(
        lambda out: None,
        out_shape=jax.ShapeDtypeStruct(shape, dtype),
        out_specs=hbm(),
        compiler_params=pltpu.CompilerParams(vmem_limit_bytes=1024 * 1024),
        name="blank",
    )()


class Line:
    def __init__(self):
        self.last = None

    def take(self, value):
        if self.last is not None:
            value, _ = lax.optimization_barrier((value, self.last))
        self.last = value
        return value


def gather_all(large, little, row, *early):
    ring, share = lax.axis_size("fsdp"), lax.axis_size("dp")
    z, q = lax.axis_index("fsdp"), lax.axis_index("dp")
    far, near = distances("dp")[-1], list(reversed(distances("dp")[:-1]))
    line = Line()

    def own_part(own):
        return lax.dynamic_index_in_dim(own, q, 0, keepdims=False)

    def begin(own):
        return lax.dynamic_update_slice(blank((ring,) + own.shape, own.dtype), own[None], (z, 0, 0, 0))

    def place(whole, step, here, arrived):
        parts = {0: here, far: arrived}
        for d in near:
            parts.update({m | d: flip(v, "dp", d) for m, v in list(parts.items())})
        source = lax.rem(z - step + ring, ring)
        for m, v in parts.items():
            whole = lax.dynamic_update_slice(whole, v[None, None], (source, q ^ m, 0, 0))
        return whole

    travelling = own_part(large)
    arriving = rotate(travelling, "fsdp")
    rows = [after(row, travelling)]
    row_next = rotate(rows[0], "fsdp")
    large_all = after(begin(large), *early)
    little_all = begin(little)
    waiting, little_next = None, None
    for step in range(1, ring):
        here = line.take(arriving)
        if step + 1 < ring:
            arriving = rotate(here, "fsdp")
        arrived = flip(here, "dp", far)
        if step + 2 >= ring and little_next is None:
            little_next = rotate(after(own_part(little), here), "fsdp")
        if waiting is not None:
            large_all = place(large_all, step - 1, waiting[0], line.take(waiting[1]))
        waiting = (here, arrived)
        rows.append(line.take(row_next))
        if step + 1 < ring:
            row_next = rotate(rows[-1], "fsdp")
    pending = []
    for step in range(1, ring):
        here = line.take(little_next)
        if step + 1 < ring:
            little_next = rotate(here, "fsdp")
        pending.append((here, flip(here, "dp", far)))
        if step + 1 == max(ring - 1, 2):
            large_all = place(large_all, ring - 1, waiting[0], line.take(waiting[1]))
    if ring < 3:
        large_all = place(large_all, ring - 1, waiting[0], line.take(waiting[1]))
    placed = large_all
    large_all = after(large_all, pending[-1][0])

    def finish(*behind):
        whole = little_all
        for step, (here, arrived) in enumerate(pending, 1):
            whole = place(whole, step, here, after(arrived, *behind) if step > 1 else after(arrived, placed))
        return whole

    at = jnp.arange(ring)
    chosen = (lax.rem(z - at[:, None] + ring, ring) == at[None, :]).astype(row.dtype)
    return large_all, finish, jnp.dot(chosen, jnp.concatenate(rows, axis=0), preferred_element_type=F32)


def ring_places():
    ring, z = lax.axis_size("fsdp"), lax.axis_index("fsdp")
    return [lax.rem(z + 2 * ring - 1 - s, ring) for s in range(ring)]


def add(a, b):
    return a.astype(F32) + b.astype(F32)


def sum_far(near, level, mask):
    if level == 0:
        return near[mask]
    d = distances("dp")[level]
    away = [flip(v, "dp", d) for v in sum_far(near, level - 1, mask | d)]
    line = Line()
    return [add(a, line.take(b)).astype(BF16) for a, b in zip(sum_far(near, level - 1, mask), away)]


def sum_rings(near, early, rows):
    ring, levels = lax.axis_size("fsdp"), len(distances("dp")) - 1
    d = distances("dp")[-1]
    order = Line()
    ready = [order.take(v) for v in sum_far(near, levels - 1, d)]
    away = [flip(v, "dp", d) for v in ready]
    here = [order.take(v) for v in sum_far(near, levels - 1, 0)]
    line = Line()
    value, value_next = None, None
    early_value, early_at = early[0], 0
    early_next = rotate(early[0], "fsdp")

    def early_step(value, arrived, at):
        value = add(arrived, early[at + 1]).astype(BF16)
        return value, (rotate(value, "fsdp") if at + 2 < ring else None), at + 1

    early_value, early_next, early_at = early_step(early_value, after(early_next, ready[-1]), early_at)
    if early_next is not None:
        early_value, early_next, early_at = early_step(early_value, after(early_next, here[-1]), early_at)
    small, small_next = None, None
    for s in range(ring):
        part = add(here[s], line.take(away[s])).astype(BF16)
        value = part if s == 0 else add(line.take(value_next), part).astype(BF16)
        if s == 0:
            rows = after(rows, value)
            rows = rows + flip(rows, "dp", distances("dp")[0])
            small = [lax.dynamic_index_in_dim(rows, at, 0) for at in ring_places()]
            small_value, small_next = small[0], rotate(small[0], "fsdp")
        if s + 1 < ring:
            value_next = rotate(value, "fsdp")
        if early_next is not None:
            early_value, early_next, early_at = early_step(early_value, line.take(early_next), early_at)
        if s > 0:
            small_value = line.take(small_next) + small[s]
            if s + 1 < ring:
                small_next = rotate(small_value, "fsdp")
    small_value = after(small_value, value)
    for d in distances("dp")[1:]:
        small_value = small_value + flip(small_value, "dp", d)
    return value, early_value, small_value


def share_out(value, *behind):
    q = lax.axis_index("dp")
    owned = {0: value}
    for d in reversed(distances("dp")):
        arrived = {m | d: flip(v, "dp", d) for m, v in owned.items()}
        owned.update({m: after(v, *behind) if behind else v for m, v in arrived.items()})
    whole = blank((lax.axis_size("dp"),) + value.shape, F32)
    for m, v in owned.items():
        whole = lax.dynamic_update_slice(whole, v.astype(F32)[None], (q ^ m, 0, 0))
    return whole.reshape(-1, value.shape[1])


def far_masks():
    return range(0, lax.axis_size("dp"), 2)


def rows_far(left, right):
    ring, _, rows, depth = left.shape
    q, order = lax.axis_index("dp"), ring_places()

    def products(masks):
        chosen = [lax.dynamic_index_in_dim(left, q ^ mask, 1, keepdims=False) for mask in masks]
        chosen = [lax.dynamic_index_in_dim(one, at, 0) for one in chosen for at in order]
        product = jnp.dot(jnp.concatenate(chosen).reshape(-1, depth), right, preferred_element_type=F32)
        return product.astype(BF16).reshape(len(masks), ring, rows, -1)

    steps = distances("dp")
    masks = list(far_masks())
    arrived = flip(products([mask | 1 for mask in masks]), "dp", 1)
    both = sent = add(products(masks), arrived).astype(BF16)
    for d in steps[1:]:
        here = [k for k, mask in enumerate(masks) if not mask & d]
        away = [masks.index(masks[k] | d) for k in here]
        arrived = flip(jnp.stack([both[k] for k in away]), "dp", d)
        both = add(jnp.stack([both[k] for k in here]), arrived).astype(BF16)
        masks = [masks[k] for k in here]
    return [both[0, s] for s in range(ring)], sent


def columns_near(left, right):
    ring, depth = lax.axis_size("fsdp"), right.shape[0]
    order = ring_places()
    block = right.shape[1] // ring
    rights = [lax.dynamic_slice(right, (0, at * block), (depth, block)) for at in order]
    every = jnp.concatenate(rights, axis=1)
    near = {}
    for mask in reversed(far_masks()):
        away = jnp.dot(left(mask | 1), every, preferred_element_type=F32).astype(BF16)
        arrived = flip(away, "dp", 1)
        here = left(mask)
        near[mask] = [
            add(jnp.dot(here, rights[s], preferred_element_type=F32), arrived[:, s * block : (s + 1) * block]).astype(BF16)
            for s in range(ring)
        ]
    return near


def shards(
    inputs,
    cotangent,
    segments,
    norm_gain,
    in_weight,
    conv_weight,
    conv_bias,
    dt_bias,
    decay_log,
    skip_gain,
    gate_gain,
    out_weight,
):
    first = lax.axis_index("section") == 0
    z = lax.axis_index("fsdp")
    ring, share = lax.axis_size("fsdp"), lax.axis_size("dp")
    length, width = inputs.shape[2], inputs.shape[3]
    taps = conv_weight.shape[1]
    heads = dt_bias.shape[1] * ring
    inner = gate_gain.shape[1] * ring
    head_dim = inner // heads

    seg = segments[:, 0].astype(F32)
    seg_rows = [jnp.broadcast_to(seg[m][None], (8, length)) for m in range(2)]
    pick = functools.partial(jnp.where, first)

    seg1, seg3 = pick(seg_rows[1], seg_rows[0]), pick(seg_rows[0], seg_rows[1])
    pieces = (norm_gain[0], conv_bias[0], dt_bias[0], decay_log[0], skip_gain[0], gate_gain[0], conv_weight[0].reshape(-1))
    sizes = [piece.shape[0] for piece in pieces]
    proj = in_weight.shape[2]
    w, finish, packed = gather_all(
        in_weight[0].T.reshape(share, proj // share, -1),
        out_weight[0].reshape(share, -1, width),
        jnp.concatenate(pieces)[None],
        *seg_rows,
        seg1,
        seg3,
    )
    w = w.reshape(ring, proj, -1)
    fields, start = [], 0
    for size in sizes:
        fields.append(packed[:, start : start + size])
        start += size
    taps_w = fields[6].reshape(ring, taps, -1).transpose(1, 0, 2).reshape(taps, -1)
    rows = [field.reshape(1, -1) for field in fields[:6]]

    conv_width = conv_bias.shape[1] * ring

    def padded(row):
        return jnp.pad(row, ((0, 0), (0, conv_width - row.shape[1])))

    wide_rows = [rows[0], rows[1], rows[2], rows[3], jnp.repeat(rows[4], head_dim, axis=1), rows[5]]
    filler = jnp.zeros((-(taps + len(wide_rows)) % 8, conv_width), F32)
    small = jnp.concatenate([taps_w] + [padded(row) for row in wide_rows] + [filler], axis=0)
    sizes_of = (length, width, inner, conv_width, heads, taps)
    def to_second(value):
        return lax.ppermute(value, "section", [(0, 1)])

    def to_first(value):
        return lax.ppermute(value, "section", [(1, 0)])

    u_a, u_b = inputs[0, 0], inputs[1, 0]
    g_a, g_b = cotangent[0, 0], cotangent[1, 0]

    w, small, u_a, u_b, g_a, g_b, seg1, seg3, seg0 = lax.optimization_barrier(
        (w, small, u_a, u_b, g_a, g_b, seg1, seg3, seg_rows[0])
    )
    mixed0 = forward(u_a, seg0, small, sizes_of, w)[0]
    ow = finish(mixed0).reshape(inner, width)
    out0 = (u_a.astype(F32) + jnp.dot(mixed0, ow, preferred_element_type=F32)).astype(BF16)
    u1 = pick(u_b, to_second(out0))
    out1, *kept1, normed1, mixed1 = forward(u1, seg1, small, sizes_of, w, ow)
    stream_b = to_second(out1)
    back2 = backward(u1, g_a, seg1, small, sizes_of, kept1, w, ow)
    grad_a = to_first(back2[1])
    u3 = pick(u_a, stream_b)
    out3, *kept3, normed3, mixed3 = forward(u3, seg3, small, sizes_of, w, ow)
    g4 = pick(grad_a, g_b)
    back4 = backward(u3, g4, seg3, small, sizes_of, kept3, w, ow, full=True)
    grad_b = to_first(back4[1])

    mixed_both = after(jnp.concatenate([mixed3, mixed1], axis=0), back4[1])
    mixed_t = mixed_both.T.reshape(ring, share, -1, 2 * length)
    far_out, sent = rows_far(mixed_t, jnp.concatenate([g4, pick(grad_b, g_a)], axis=0))
    back5 = backward(after(u1, sent), grad_b, seg1, small, sizes_of, kept1, w, ow)

    normed = jnp.concatenate([normed3, normed1], axis=0)
    q = lax.axis_index("dp")
    back5_t = after(back5[0], *far_out)

    def left(mask):
        def part(value):
            return lax.dynamic_index_in_dim(value.reshape(share, -1, length), q ^ mask, 0, keepdims=False)

        return jnp.concatenate([part(back4[0]), pick(part(back5_t), part(back2[0]))], axis=1)

    near_in = columns_near(left, normed)
    grad = back4[2] + pick(back5[2], back2[2])

    def field(k, size):
        return grad[taps + k, :size].reshape(ring, -1)

    packed = jnp.concatenate(
        [
            field(0, width),
            field(1, conv_width),
            field(2, heads),
            field(3, heads),
            jnp.sum(grad[taps + 4, :inner].reshape(heads, head_dim), axis=1).reshape(ring, -1),
            field(5, inner),
            grad[:taps].reshape(taps, ring, -1).transpose(1, 0, 2).reshape(ring, -1),
        ],
        axis=1,
    )
    own_in, own_out, packed = sum_rings(near_in, far_out, packed)
    in_grad = share_out(own_in).T[None]
    out_grad = share_out(own_out, own_in)[None]
    begun = near_in[0][0]
    output = pick(after(to_first(after(out1, begun)), own_in), out3)
    input_grad = pick(back4[3], after(to_second(after(back5[1], begun)), own_in).astype(F32))
    fields, start = [], 0
    for size in sizes:
        fields.append(packed[:, start : start + size])
        start += size
    return (
        output[None, None],
        input_grad[None, None],
        fields[0],
        in_grad,
        fields[6].reshape(1, taps, -1),
        fields[1],
        fields[2],
        fields[3],
        fields[4],
        fields[5],
        out_grad,
    )


def solution(mesh):
    spread_over = ("fsdp", "dp")
    row = P("section", "fsdp")
    matrix = P("section", "fsdp", None)
    tap = P("section", None, "fsdp")
    activation = P(None, spread_over, None, None)
    result = P("section", spread_over, None, None)
    return jax.shard_map(
        shards,
        mesh=mesh,
        in_specs=(activation, activation, P(None, spread_over, None), row, matrix, tap, row, row, row, row, row, matrix),
        out_specs=(result, result, row, matrix, tap, row, row, row, row, row, matrix),
        check_vma=False,
    )
```

```python
import functools

import jax
import jax.numpy as jnp
from jax import lax
from jax.experimental import pallas as pl
from jax.experimental.pallas import tpu as pltpu
from jax.sharding import PartitionSpec as P

EPS = 1e-05
LOG2E = 1.4426950408889634
HIGH = lax.Precision.HIGHEST
F32 = jnp.float32
BF16 = jnp.bfloat16
LANES = 128
WIDE = 256
VMEM_BYTES = 56 * 1024 * 1024


def sigmoid(v):
    return 0.5 * jnp.tanh(0.5 * v) + 0.5


def dot(a, b):
    return lax.dot_general(a, b, (((1,), (0,)), ((), ())), preferred_element_type=F32)


def dot_nt(a, b):
    return lax.dot_general(a, b, (((1,), (1,)), ((), ())), preferred_element_type=F32)


def dot_tn(a, b):
    return lax.dot_general(a, b, (((0,), (0,)), ((), ())), preferred_element_type=F32)


def twice(v):
    return jnp.concatenate([v, v], axis=1)


def fold(v):
    return v[:, :LANES] + v[:, LANES:]


def cols(start, width=WIDE):
    return pl.ds(pl.multiple_of(start, LANES), width)


def weight_copies(source, target, rows, sem, k):
    blocks, _, width = source.shape
    return [
        pltpu.make_async_copy(
            source.at[b, rows, :], target.at[rows, b * width : (b + 1) * width], sem.at[k, b]
        )
        for b in range(blocks)
    ]


def start(copies):
    for copy in copies:
        copy.start()


def wait(copies):
    for copy in copies:
        copy.wait()


def small_rows(small_ref, width, inner, conv, taps):
    row = lambda k, size: small_ref.at[taps + k : taps + k + 1, :size]
    return (
        row(0, width),
        small_ref.at[:taps],
        row(1, conv),
        row(2, LANES),
        row(3, LANES),
        row(4, inner),
        row(5, inner),
    )


def column_of(segr_ref):
    row = jnp.broadcast_to(segr_ref[:1, :], (LANES, segr_ref.shape[1]))
    return jnp.transpose(row)


def write_masks(segc_ref, mask_ref, taps):
    seg = segc_ref[...]
    row = lax.broadcasted_iota(jnp.int32, seg.shape, 0)
    for lag in range(1, taps):
        same = (pltpu.roll(seg, lag, 0) == seg) & (row >= lag)
        mask_ref[lag - 1] = jnp.where(same, 1.0, 0.0)


def conv_chunk(s, start, cw_ref, cb_ref, mask_ref, taps):
    at = cols(start)
    total = cb_ref[:, at] + s * cw_ref[pl.ds(taps - 1, 1), at]
    for lag in range(1, taps):
        shifted = pltpu.roll(s, lag, 0) * twice(mask_ref[lag - 1])
        total = total + shifted * cw_ref[pl.ds(taps - 1 - lag, 1), at]
    return total


def step_sizes(dt, dtb_ref, dl_ref, heads):
    length = dt.shape[0]
    pad = jnp.zeros((length, LANES - heads), F32)
    v = jnp.concatenate([dt, pad], axis=1) + dtb_ref[...]
    step = jnp.maximum(v, 0.0) + jnp.log1p(jnp.exp(-jnp.abs(v)))
    rate = -jnp.exp(dl_ref[...]) * step
    i = lax.broadcasted_iota(jnp.int32, (length, length), 0)
    j = lax.broadcasted_iota(jnp.int32, (length, length), 1)
    lower = jnp.where(i >= j, 1.0, 0.0)
    scaled = rate * LOG2E
    cumul = lax.dot_general(lower, scaled, (((1,), (0,)), ((), ())), precision=HIGH, preferred_element_type=F32)
    return v, step, rate, cumul


def head_lanes(v, quad, per):
    return pltpu.roll(v, lax.rem(LANES - per * quad, LANES), 1)


def spread(v, i0, head_dim):
    length = v.shape[0]
    lane = lax.broadcasted_iota(jnp.int32, (length, LANES), 1)
    a = jnp.broadcast_to(v[:, i0 : i0 + 1], (length, LANES))
    b = jnp.broadcast_to(v[:, i0 + 1 : i0 + 2], (length, LANES))
    return jnp.where(lane < head_dim, a, b)


def forward_body(
    sizes, keep, u_ref, segr_ref, small_ref, w_hbm, *refs
):
    length, width, inner, conv, heads, taps = sizes
    ng_ref, cw_ref, cb_ref, dtb_ref, dl_ref, sk_ref, gg_ref = small_rows(small_ref, width, inner, conv, taps)
    ow_hbm, refs = (refs[0], refs[1:]) if keep else (None, refs)
    count = 10 if keep else 1
    outs, held, refs = refs[:count], refs[count : count + 10], refs[count + 10 :]
    out_ref, zs_ref, zslope_ref, yf_ref, x_ref, slope_ref, stream_ref, dt_ref, normed_ref, mixed_ref = held
    w, ow, segc_ref, mask_ref, s_ref, gated_ref, gate_ref, cum_ref, step_ref, cumt_ref, sem, osem, wsem = refs
    state = (conv - inner) // 2
    head_dim = inner // heads
    per = WIDE // head_dim
    quads = inner // WIDE
    half = length // 2
    proj = w.shape[0]
    tail = 2 * inner

    def written(k, at, j):
        if keep or k == 9:
            return [pltpu.make_async_copy(held[k].at[:, at], outs[k if keep else 0].at[:, at], wsem.at[k, j])]
        return []


    def copies(at, k):
        return weight_copies(w_hbm, w, at, sem, k)

    def stream_copy(q):
        return copies(cols(inner + q * WIDE), 1 + 2 * q)

    def gate_copy(q):
        return copies(cols(q * WIDE), 2 + 2 * q)

    tail_copy = copies(pl.ds(tail, proj - tail), 0)
    start(tail_copy)
    ahead = min(3, quads)
    for q in range(ahead):
        start(stream_copy(q))
        start(gate_copy(q))
    out_copy = pltpu.make_async_copy(ow_hbm, ow, osem) if keep else None

    u = u_ref[...].astype(F32)
    scale = lax.rsqrt(jnp.mean(u * u, axis=-1, keepdims=True) + EPS)
    normed_ref[...] = (u * scale * ng_ref[...]).astype(BF16)
    start(written(8, pl.ds(0, width), 0))
    segc_ref[...] = column_of(segr_ref)
    write_masks(segc_ref, mask_ref, taps)

    def project(q):
        rows = cols(inner + q * WIDE)
        stream_ref[:, cols(q * WIDE)] = dot_nt(normed_ref[...], w[rows, :]).astype(BF16)
        gate_ref[:, cols(q * WIDE)] = dot_nt(normed_ref[...], w[cols(q * WIDE), :])

    wait(tail_copy)
    dt = dot_nt(normed_ref[...], w[inner + conv : proj, :])
    dt_ref[...] = dt
    start(written(7, pl.ds(0, heads), 0))
    stream_ref[:, cols(inner)] = dot_nt(normed_ref[...], w[tail : tail + 2 * state, :]).astype(BF16)
    _, step, _, cumul = step_sizes(dt, dtb_ref, dl_ref, heads)
    step_ref[...] = step
    cum_ref[...] = cumul
    cumt_ref[...] = jnp.transpose(cumul)
    wait(stream_copy(0))
    wait(gate_copy(0))
    project(0)

    def conv_of(first):
        at = cols(first)
        total = conv_chunk(stream_ref[:, at].astype(F32), first, cw_ref, cb_ref, mask_ref, taps)
        sig = sigmoid(total)
        x = total * sig
        if keep:
            x_ref[:, at] = x.astype(BF16)
            slope_ref[:, at] = (sig + x * (1.0 - sig)).astype(BF16)
        return x

    bc = conv_of(inner)
    start(written(4, cols(inner), quads) + written(5, cols(inner), quads) + written(6, cols(inner), quads))
    keys = bc[:, :state].astype(BF16)
    queries = bc[:, state:].astype(BF16)
    i = lax.broadcasted_iota(jnp.int32, (length, length), 0)
    j = lax.broadcasted_iota(jnp.int32, (length, length), 1)
    within = (i >= j) & (segc_ref[:, :1] == segr_ref[:1, :])
    s_ref[...] = jnp.where(within, dot_nt(queries, keys), 0.0)

    def quad_step(q, squares, more=True):
        at = cols(q * WIDE)
        if more:

            @pl.when(q + ahead < quads)
            def _():
                start(stream_copy(q + ahead))
                start(gate_copy(q + ahead))

            if keep:

                @pl.when(q + ahead == quads)
                def _():
                    out_copy.start()

            wait(stream_copy(q + 1))
            wait(gate_copy(q + 1))
        x = conv_of(q * WIDE)
        z = gate_ref[:, at]
        sig = sigmoid(z)
        zs = z * sig
        if keep:
            zs_ref[:, at] = zs.astype(BF16)
            zslope_ref[:, at] = (sig + zs * (1.0 - sig)).astype(BF16)
        if more:
            project(q + 1)
        cum_q = head_lanes(cum_ref[...], q, per)
        step_q = head_lanes(step_ref[...], q, per)
        ys = []
        for pair in range(per // 2):
            part = slice(pair * LANES, (pair + 1) * LANES)
            xdt = (x[:, part] * spread(step_q, 2 * pair, head_dim)).astype(BF16)
            got = []
            for k in range(2):
                h = 2 * pair + k
                col = cum_q[:, h : h + 1]
                row = cumt_ref[pl.ds(per * q + h, 1), :]
                top = jnp.exp2(jnp.minimum(col[:half] - row[:, :half], 0.0)) * s_ref[:half, :half]
                low = jnp.exp2(jnp.minimum(col[half:] - row, 0.0)) * s_ref[half:, :]
                got.append(
                    jnp.concatenate(
                        [dot(top.astype(BF16), xdt[:half]), dot(low.astype(BF16), xdt)], axis=0
                    )
                )
            lane = lax.broadcasted_iota(jnp.int32, (length, LANES), 1)
            ys.append(jnp.where(lane < head_dim, got[0], got[1]))
        yf = jnp.concatenate(ys, axis=1) + sk_ref[:, at] * x
        gated = yf * zs
        if keep:
            yf_ref[:, at] = yf.astype(BF16)
        gated_ref[:, at] = gated
        for k in range(1, 7):
            start(written(k, at, q))
        return squares + fold(gated * gated)

    squares = lax.fori_loop(0, quads - 1, quad_step, jnp.zeros((length, LANES), F32))
    squares = quad_step(quads - 1, squares, more=False)
    scale2 = lax.rsqrt(jnp.sum(squares, axis=-1, keepdims=True) * (1.0 / inner) + EPS)

    for q in range(quads):
        at = cols(q * WIDE)
        mixed_ref[:, at] = (gated_ref[:, at] * scale2 * gg_ref[:, at]).astype(BF16)
        start(written(9, at, q))
    if keep:
        out_copy.wait()
    for n in range(width // WIDE if keep else 0):
        at = cols(n * WIDE)
        out_ref[:, at] = (u_ref[:, at].astype(F32) + dot(mixed_ref[...], ow[:, at])).astype(BF16)
        start(written(0, at, n))
    for n in range(width // WIDE if keep else 0):
        wait(written(0, cols(n * WIDE), n))
    wait(written(7, pl.ds(0, heads), 0) + written(8, pl.ds(0, width), 0))
    wait(written(4, cols(inner), quads) + written(5, cols(inner), quads) + written(6, cols(inner), quads))
    for q in range(quads):
        for k in (1, 2, 3, 4, 5, 6, 9):
            wait(written(k, cols(q * WIDE), q))


def vmem():
    return pl.BlockSpec(memory_space=pltpu.VMEM)


def hbm():
    return pl.BlockSpec(memory_space=pl.ANY)


def forward(u, seg_row, small, sizes, w, ow=None):
    keep = ow is not None
    length, width, inner, conv, heads, taps = sizes
    blocks, proj = w.shape[:2]
    quads = inner // WIDE
    held = (
        ((length, width), BF16),
        ((length, inner), BF16),
        ((length, inner), BF16),
        ((length, inner), BF16),
        ((length, conv), BF16),
        ((length, conv), BF16),
        ((length, conv), BF16),
        ((length, heads), F32),
        ((length, width), BF16),
        ((length, inner), BF16),
    )
    outs = held if keep else held[9:]
    weights = (w, ow) if keep else (w,)
    return pl.pallas_call(
        functools.partial(forward_body, sizes, keep),
        out_shape=tuple(jax.ShapeDtypeStruct(*out) for out in outs),
        in_specs=[vmem()] * 3 + [hbm()] * len(weights),
        out_specs=[hbm()] * len(outs),
        scratch_shapes=[pltpu.VMEM(*one) for one in held]
        + [
            pltpu.VMEM((proj, width), BF16),
            pltpu.VMEM((inner, width), BF16),
            pltpu.VMEM((length, LANES), F32),
            pltpu.VMEM((taps - 1, length, LANES), F32),
            pltpu.VMEM((length, length), F32),
            pltpu.VMEM((length, inner), F32),
            pltpu.VMEM((length, inner), F32),
            pltpu.VMEM((length, LANES), F32),
            pltpu.VMEM((length, LANES), F32),
            pltpu.VMEM((LANES, length), F32),
            pltpu.SemaphoreType.DMA((1 + 2 * quads, blocks)),
            pltpu.SemaphoreType.DMA,
            pltpu.SemaphoreType.DMA((10, quads + 1)),
        ],
        compiler_params=pltpu.CompilerParams(vmem_limit_bytes=VMEM_BYTES),
        cost_estimate=pl.CostEstimate(
            flops=2 * length * (width * proj + inner * width + 2 * length * inner),
            bytes_accessed=2 * (width * proj + inner * width),
            transcendentals=length * (length * heads + 2 * inner),
        ),
        name="layer_forward",
    )(u, seg_row, small, *weights)


def backward_body(
    sizes, full, u_ref, g_ref, segr_ref, small_ref, zs_hbm, zslope_hbm, yf_hbm, x_hbm, slope_hbm, stream_hbm, dt_ref, w_hbm, ow_hbm,
    dlowt_hbm, low_ref, dsmall_ref, *refs,
):
    length, width, inner, conv, heads, taps = sizes
    ng_ref, cw_ref, cb_ref, dtb_ref, dl_ref, sk_ref, gg_ref = small_rows(small_ref, width, inner, conv, taps)
    dng_ref, dcw_ref, dcb_ref, ddtb_ref, ddl_ref, dsk_ref, dgg_ref = small_rows(
        dsmall_ref, width, inner, conv, taps
    )
    gin_ref = refs[0] if full else None
    (
        w, ow, zs_ref, zslope_ref, yf_ref, x_ref, slope_ref, stream_ref, dlowt_ref, segc_ref, mask_ref, dm_ref, st_ref, dst_ref,
        cum_ref, step_ref, cumt_ref, heads_ref, direct_ref, rows_ref, dn_ref, dlow_ref, sem, osem, rsem, wsem,
    ) = refs[1 if full else 0 :]
    state = (conv - inner) // 2
    head_dim = inner // heads
    per = WIDE // head_dim
    quads = inner // WIDE
    half = length // 2
    proj = w.shape[0]

    def fetch(k, source, target, at, j):
        return pltpu.make_async_copy(source.at[:, at], target.at[:, at], rsem.at[k, j])

    def read(q):
        at = pl.ds(pl.multiple_of(q * WIDE, WIDE), WIDE)
        return [
            pltpu.make_async_copy(ow_hbm.at[at, :], ow.at[at, :], osem.at[q]),
            fetch(0, zs_hbm, zs_ref, at, q),
            fetch(1, yf_hbm, yf_ref, at, q),
        ]

    def read_later(q):
        at = pl.ds(pl.multiple_of(q * WIDE, WIDE), WIDE)
        return [
            fetch(2, x_hbm, x_ref, at, q),
            fetch(3, slope_hbm, slope_ref, at, q),
            fetch(4, stream_hbm, stream_ref, at, q),
            fetch(5, zslope_hbm, zslope_ref, at, q),
        ]

    last = pl.ds(inner, conv - inner)
    read_last = [
        fetch(2, x_hbm, x_ref, last, quads),
        fetch(3, slope_hbm, slope_ref, last, quads),
        fetch(4, stream_hbm, stream_ref, last, quads),
    ]
    for q in range(quads):
        start(read(q))
    start(read_last)
    in_copy = weight_copies(w_hbm, w, pl.ds(0, proj), sem, 0)

    def written(first, size, j):
        rows = pl.ds(pl.multiple_of(first, 32), size)
        return [pltpu.make_async_copy(dlowt_ref.at[rows, :], dlowt_hbm.at[rows, :], wsem.at[j])]

    dsmall_ref[...] = jnp.zeros_like(dsmall_ref)
    segc_ref[...] = column_of(segr_ref)
    write_masks(segc_ref, mask_ref, taps)
    v, step, rate, cumul = step_sizes(dt_ref[...], dtb_ref, dl_ref, heads)
    step_ref[...] = step
    cum_ref[...] = cumul
    cumt_ref[...] = jnp.transpose(cumul)
    heads_ref[...] = jnp.zeros_like(heads_ref)
    direct_ref[...] = jnp.zeros_like(direct_ref)
    dst_ref[...] = jnp.zeros_like(dst_ref)
    rows_ref[...] = jnp.zeros_like(rows_ref)

    def first_step(q, carry):
        squares, cross = carry
        at = cols(q * WIDE)
        wait(read(q))
        start(read_later(q))
        dm = dot_nt(g_ref[...], ow[pl.ds(pl.multiple_of(q * WIDE, WIDE), WIDE), :])
        gated = yf_ref[:, at].astype(F32) * zs_ref[:, at].astype(F32)
        dm_ref[:, at] = dm
        return squares + fold(gated * gated), cross + fold(gated * (dm * gg_ref[:, at]))

    zero = jnp.zeros((length, LANES), F32)
    squares, cross = lax.fori_loop(0, quads, first_step, (zero, zero))
    scale2 = lax.rsqrt(jnp.sum(squares, axis=-1, keepdims=True) * (1.0 / inner) + EPS)
    back2 = jnp.sum(cross, axis=-1, keepdims=True) * scale2 * scale2 * scale2 * (1.0 / inner)

    start(in_copy)
    wait(read_last)
    keys = x_ref[:, inner : inner + state]
    queries = x_ref[:, inner + state : inner + 2 * state]
    j = lax.broadcasted_iota(jnp.int32, (length, length), 0)
    i = lax.broadcasted_iota(jnp.int32, (length, length), 1)
    within = (i >= j) & (segc_ref[:, :1] == segr_ref[:1, :])
    st_ref[...] = jnp.where(within, dot_nt(keys, queries), 0.0)

    def write_low(at, value):
        low = value.astype(BF16)
        dlow_ref[:, at] = low
        dlowt_ref[at, :] = jnp.transpose(low)

    def conv_back(start, d_conv):
        at = cols(start)
        d_total = d_conv * slope_ref[:, at].astype(F32)
        s = stream_ref[:, at].astype(F32)
        dcb_ref[:, at] = jnp.sum(d_total, axis=0, keepdims=True)
        dcw_ref[pl.ds(taps - 1, 1), at] = jnp.sum(d_total * s, axis=0, keepdims=True)
        d_stream = d_total * cw_ref[pl.ds(taps - 1, 1), at]
        for lag in range(1, taps):
            back = pltpu.roll(d_total * twice(mask_ref[lag - 1]), length - lag, 0)
            dcw_ref[pl.ds(taps - 1 - lag, 1), at] = jnp.sum(back * s, axis=0, keepdims=True)
            d_stream = d_stream + back * cw_ref[pl.ds(taps - 1 - lag, 1), at]
        write_low(cols(inner + start), d_stream)

    for q in range(quads):
        wait(read_later(q))

    def second_step(q, _):
        at = cols(q * WIDE)
        x = x_ref[:, at].astype(F32)
        zs = zs_ref[:, at].astype(F32)
        yf = yf_ref[:, at].astype(F32)
        gated = yf * zs
        scaled = dm_ref[:, at] * scale2
        dgg_ref[:, at] = jnp.sum(scaled * gated, axis=0, keepdims=True)
        d_gated = scaled * gg_ref[:, at] - gated * back2
        dy = d_gated * zs
        write_low(at, d_gated * yf * zslope_ref[:, at].astype(F32))
        dsk_ref[:, at] = jnp.sum(dy * x, axis=0, keepdims=True)
        dy_low = dy.astype(BF16)
        cum_q = head_lanes(cum_ref[...], q, per)
        step_q = head_lanes(step_ref[...], q, per)
        lane = lax.broadcasted_iota(jnp.int32, (length, LANES), 1)
        dst_top = jnp.zeros((half, length), F32)
        dst_low = jnp.zeros((half, half), F32)
        xdts, dxdts, steps = [], [], []
        for pair in range(per // 2):
            part = slice(pair * LANES, (pair + 1) * LANES)
            step_p = spread(step_q, 2 * pair, head_dim)
            xdt = (x[:, part] * step_p).astype(BF16)
            dyp = dy_low[:, part]
            got = []
            for k in range(2):
                h = 2 * pair + k
                mine = (lane < head_dim) if k == 0 else (lane >= head_dim)
                xm = jnp.where(mine, xdt.astype(F32), 0.0).astype(BF16)
                col = cum_q[:, h : h + 1]
                row = cumt_ref[pl.ds(per * q + h, 1), :]
                decay_top = jnp.exp2(jnp.minimum(row - col[:half], 0.0))
                decay_low = jnp.exp2(jnp.minimum(row[:, half:] - col[half:], 0.0))
                top = (decay_top * st_ref[:half, :]).astype(BF16)
                low = (decay_low * st_ref[half:, half:]).astype(BF16)
                got.append(jnp.concatenate([dot(top, dyp), dot(low, dyp[half:])], axis=0))
                dm_top = dot_nt(xm[:half], dyp)
                dm_low = dot_nt(xm[half:], dyp[half:])
                dst_top = dst_top + dm_top * decay_top
                dst_low = dst_low + dm_low * decay_low
                sums = jnp.sum(dm_top * top.astype(F32), axis=0, keepdims=True)
                more = jnp.sum(dm_low * low.astype(F32), axis=0, keepdims=True)
                rows_ref[pl.ds(per * q + h, 1), :] = jnp.concatenate([sums[:, :half], sums[:, half:] + more], axis=1)
            xdts.append(xdt.astype(F32))
            steps.append(step_p)
            dxdts.append(jnp.where(lane < head_dim, got[0], got[1]))
        dst_ref[:half, :] += dst_top
        dst_ref[half:, half:] += dst_low
        xdt = jnp.concatenate(xdts, axis=1)
        dxdt = jnp.concatenate(dxdts, axis=1)
        steps = jnp.concatenate(steps, axis=1)
        pick_row = lax.broadcasted_iota(jnp.int32, (WIDE, LANES), 0)
        pick_col = lax.broadcasted_iota(jnp.int32, (WIDE, LANES), 1)
        pick = jnp.where(pick_row // head_dim + per * q == pick_col, 1.0, 0.0).astype(BF16)
        both = xdt * dxdt
        high = both.astype(BF16)
        rest = (both - high.astype(F32)).astype(BF16)
        heads_ref[...] += dot(high, pick) + dot(rest, pick)
        direct_ref[...] += dot((dxdt * x).astype(BF16), pick)
        conv_back(q * WIDE, dxdt * steps + sk_ref[:, at] * dy)
        start(written(q * WIDE, WIDE, q) + written(inner + q * WIDE, WIDE, quads + q))
        return 0

    lax.fori_loop(0, quads, second_step, 0, unroll=2)

    d_scores = jnp.where(within, dst_ref[...], 0.0).astype(BF16)
    conv_back(inner, jnp.concatenate([dot(d_scores, queries), dot_tn(d_scores, keys)], axis=1))

    upper = jnp.where(within, 1.0, 0.0)
    d_rate = lax.dot_general(
        upper, jnp.transpose(rows_ref[...]) - heads_ref[...], (((1,), (0,)), ((), ())), precision=HIGH, preferred_element_type=F32
    )
    ddl_ref[...] = jnp.sum(d_rate * rate, axis=0, keepdims=True)
    d_step = direct_ref[...] - d_rate * jnp.exp(dl_ref[...])
    d_dt = d_step / (1.0 + jnp.exp(-v))
    ddtb_ref[...] = jnp.sum(d_dt, axis=0, keepdims=True)
    d_dt_low = d_dt[:, :heads].astype(BF16)
    dlowt_ref[inner + conv : proj, :] = jnp.transpose(d_dt)[:heads].astype(BF16)
    start(written(2 * inner, proj - 2 * inner, 2 * quads))

    wait(in_copy)
    u = u_ref[...].astype(F32)
    scale = lax.rsqrt(jnp.mean(u * u, axis=-1, keepdims=True) + EPS)

    def normed_step(n, _):
        at = cols(n * WIDE)
        dn_ref[:, at] = dot(dlow_ref[...], w[: inner + conv, at]) + dot(d_dt_low, w[inner + conv : proj, at])
        return 0

    lax.fori_loop(0, width // WIDE, normed_step, 0)
    dn = dn_ref[...]
    dng_ref[...] = jnp.sum(dn * u * scale, axis=0, keepdims=True)
    dn = dn * ng_ref[...]
    back = jnp.mean(dn * u, axis=-1, keepdims=True) * scale * scale * scale
    gin = g_ref[...].astype(F32) + dn * scale - u * back
    if full:
        gin_ref[...] = gin
    low_ref[...] = gin.astype(BF16)
    for q in range(quads):
        wait(written(q * WIDE, WIDE, q) + written(inner + q * WIDE, WIDE, quads + q))
    wait(written(2 * inner, proj - 2 * inner, 2 * quads))


def backward(u, g, seg_row, small, sizes, kept, w, ow, full=False):
    length, width, inner, conv, heads, taps = sizes
    blocks, proj = w.shape[:2]
    quads = inner // WIDE
    shape = jax.ShapeDtypeStruct
    outs = (shape((proj, length), BF16), shape((length, width), BF16), shape(small.shape, F32))
    outs += (shape((length, width), F32),) if full else ()
    zs, zslope, yf, x, slope, stream, dt = kept
    return pl.pallas_call(
        functools.partial(backward_body, sizes, full),
        out_shape=outs,
        in_specs=[vmem()] * 4 + [hbm()] * 6 + [vmem()] + [hbm()] * 2,
        out_specs=[hbm()] + [vmem()] * (len(outs) - 1),
        scratch_shapes=[
            pltpu.VMEM((proj, width), BF16),
            pltpu.VMEM((inner, width), BF16),
            pltpu.VMEM((length, inner), BF16),
            pltpu.VMEM((length, inner), BF16),
            pltpu.VMEM((length, inner), BF16),
            pltpu.VMEM((length, conv), BF16),
            pltpu.VMEM((length, conv), BF16),
            pltpu.VMEM((length, conv), BF16),
            pltpu.VMEM((proj, length), BF16),
            pltpu.VMEM((length, LANES), F32),
            pltpu.VMEM((taps - 1, length, LANES), F32),
            pltpu.VMEM((length, inner), F32),
            pltpu.VMEM((length, length), F32),
            pltpu.VMEM((length, length), F32),
            pltpu.VMEM((length, LANES), F32),
            pltpu.VMEM((length, LANES), F32),
            pltpu.VMEM((LANES, length), F32),
            pltpu.VMEM((length, LANES), F32),
            pltpu.VMEM((length, LANES), F32),
            pltpu.VMEM((LANES, length), F32),
            pltpu.VMEM((length, width), F32),
            pltpu.VMEM((length, inner + conv), BF16),
            pltpu.SemaphoreType.DMA((1, blocks)),
            pltpu.SemaphoreType.DMA((quads,)),
            pltpu.SemaphoreType.DMA((6, quads + 1)),
            pltpu.SemaphoreType.DMA((2 * quads + 1,)),
        ],
        compiler_params=pltpu.CompilerParams(vmem_limit_bytes=VMEM_BYTES),
        cost_estimate=pl.CostEstimate(
            flops=2 * length * (width * proj + inner * width + 4 * length * inner),
            bytes_accessed=2 * (width * proj + inner * width) + 8 * length * proj,
            transcendentals=length * (length * heads + 4 * inner),
        ),
        name="layer_backward",
    )(u, g, seg_row, small, zs, zslope, yf, x, slope, stream, dt, w, ow)


def flip(value, axis, distance):
    pairs = [(source, source ^ distance) for source in range(lax.axis_size(axis))]
    return lax.ppermute(value, axis, pairs)


def rotate(value, axis):
    count = lax.axis_size(axis)
    return lax.ppermute(value, axis, [(source, (source + 1) % count) for source in range(count)])


def distances(axis):
    found, d = [], 1
    while d < lax.axis_size(axis):
        found.append(d)
        d *= 2
    return found


def after(value, *others):
    return lax.optimization_barrier((value,) + others)[0]


def blank(shape, dtype):
    return pl.pallas_call(
        lambda out: None,
        out_shape=jax.ShapeDtypeStruct(shape, dtype),
        out_specs=hbm(),
        compiler_params=pltpu.CompilerParams(vmem_limit_bytes=1024 * 1024),
        name="blank",
    )()


class Line:
    def __init__(self):
        self.last = None

    def take(self, value):
        if self.last is not None:
            value, _ = lax.optimization_barrier((value, self.last))
        self.last = value
        return value


def gather_all(large, little, row, *early):
    ring, share = lax.axis_size("fsdp"), lax.axis_size("dp")
    z, q = lax.axis_index("fsdp"), lax.axis_index("dp")
    far, near = distances("dp")[-1], list(reversed(distances("dp")[:-1]))
    line = Line()

    def own_part(own):
        return lax.dynamic_index_in_dim(own, q, 0, keepdims=False)

    def begin(own):
        return lax.dynamic_update_slice(blank((ring,) + own.shape, own.dtype), own[None], (z, 0, 0, 0))

    def place(whole, step, here, arrived):
        parts = {0: here, far: arrived}
        for d in near:
            parts.update({m | d: flip(v, "dp", d) for m, v in list(parts.items())})
        source = lax.rem(z - step + ring, ring)
        for m, v in parts.items():
            whole = lax.dynamic_update_slice(whole, v[None, None], (source, q ^ m, 0, 0))
        return whole

    travelling = own_part(large)
    arriving = rotate(travelling, "fsdp")
    rows = [after(row, travelling)]
    row_next = rotate(rows[0], "fsdp")
    large_all = after(begin(large), *early)
    little_all = begin(little)
    waiting, little_next = None, None
    for step in range(1, ring):
        here = line.take(arriving)
        if step + 1 < ring:
            arriving = rotate(here, "fsdp")
        arrived = flip(here, "dp", far)
        if step + 2 >= ring and little_next is None:
            little_next = rotate(after(own_part(little), here), "fsdp")
        if waiting is not None:
            large_all = place(large_all, step - 1, waiting[0], line.take(waiting[1]))
        waiting = (here, arrived)
        rows.append(line.take(row_next))
        if step + 1 < ring:
            row_next = rotate(rows[-1], "fsdp")
    pending = []
    for step in range(1, ring):
        here = line.take(little_next)
        if step + 1 < ring:
            little_next = rotate(here, "fsdp")
        pending.append((here, flip(here, "dp", far)))
        if step + 1 == max(ring - 1, 2):
            large_all = place(large_all, ring - 1, waiting[0], line.take(waiting[1]))
    if ring < 3:
        large_all = place(large_all, ring - 1, waiting[0], line.take(waiting[1]))
    placed = large_all
    large_all = after(large_all, pending[-1][0])

    def finish(*behind):
        whole = little_all
        for step, (here, arrived) in enumerate(pending, 1):
            whole = place(whole, step, here, after(arrived, *behind) if step > 1 else after(arrived, placed))
        return whole

    at = jnp.arange(ring)
    chosen = (lax.rem(z - at[:, None] + ring, ring) == at[None, :]).astype(row.dtype)
    return large_all, finish, jnp.dot(chosen, jnp.concatenate(rows, axis=0), preferred_element_type=F32)


def ring_places():
    ring, z = lax.axis_size("fsdp"), lax.axis_index("fsdp")
    return [lax.rem(z + 2 * ring - 1 - s, ring) for s in range(ring)]


def add(a, b):
    return a.astype(F32) + b.astype(F32)


def sum_far(near, level, mask):
    if level == 0:
        return near[mask]
    d = distances("dp")[level]
    away = [flip(v, "dp", d) for v in sum_far(near, level - 1, mask | d)]
    line = Line()
    return [add(a, line.take(b)).astype(BF16) for a, b in zip(sum_far(near, level - 1, mask), away)]


def sum_rings(near, early, rows):
    ring, levels = lax.axis_size("fsdp"), len(distances("dp")) - 1
    d = distances("dp")[-1]
    order = Line()
    ready = [order.take(v) for v in sum_far(near, levels - 1, d)]
    away = [flip(v, "dp", d) for v in ready]
    here = [order.take(v) for v in sum_far(near, levels - 1, 0)]
    line = Line()
    value, value_next = None, None
    early_value, early_at = early[0], 0
    early_next = rotate(early[0], "fsdp")

    def early_step(value, arrived, at):
        value = add(arrived, early[at + 1]).astype(BF16)
        return value, (rotate(value, "fsdp") if at + 2 < ring else None), at + 1

    early_value, early_next, early_at = early_step(early_value, after(early_next, ready[-1]), early_at)
    if early_next is not None:
        early_value, early_next, early_at = early_step(early_value, after(early_next, here[-1]), early_at)
    rows = after(rows, ready[-1])
    rows = rows + flip(rows, "dp", distances("dp")[0])
    small = [lax.dynamic_index_in_dim(rows, at, 0) for at in ring_places()]
    small_value, small_at = small[0], 0
    small_next = rotate(small_value, "fsdp")

    def small_step(value, arrived, at):
        value = arrived + small[at + 1]
        return value, (rotate(value, "fsdp") if at + 2 < ring else None), at + 1

    small_value, small_next, small_at = small_step(small_value, after(small_next, here[-1]), small_at)
    for s in range(ring):
        part = add(here[s], line.take(away[s])).astype(BF16)
        if s > 0 and small_next is not None:
            small_value, small_next, small_at = small_step(small_value, line.take(small_next), small_at)
        value = part if s == 0 else add(line.take(value_next), part).astype(BF16)
        if s + 1 < ring:
            value_next = rotate(value, "fsdp")
        if early_next is not None:
            early_value, early_next, early_at = early_step(early_value, line.take(early_next), early_at)
        if s == 0 and small_next is not None:
            small_value, small_next, small_at = small_step(small_value, line.take(small_next), small_at)
    for d in distances("dp")[1:]:
        small_value = small_value + after(flip(small_value, "dp", d), value)
    return value, early_value, small_value


def share_out(value, *behind):
    q = lax.axis_index("dp")
    owned = {0: value}
    for d in reversed(distances("dp")):
        arrived = {m | d: flip(v, "dp", d) for m, v in owned.items()}
        owned.update({m: after(v, *behind) if behind else v for m, v in arrived.items()})
    whole = blank((lax.axis_size("dp"),) + value.shape, F32)
    for m, v in owned.items():
        whole = lax.dynamic_update_slice(whole, v.astype(F32)[None], (q ^ m, 0, 0))
    return whole.reshape(-1, value.shape[1])


def far_masks():
    return range(0, lax.axis_size("dp"), 2)


def rows_far(left, right):
    ring, _, rows, depth = left.shape
    q, order = lax.axis_index("dp"), ring_places()

    def products(masks):
        chosen = [lax.dynamic_index_in_dim(left, q ^ mask, 1, keepdims=False) for mask in masks]
        chosen = [lax.dynamic_index_in_dim(one, at, 0) for one in chosen for at in order]
        product = jnp.dot(jnp.concatenate(chosen).reshape(-1, depth), right, preferred_element_type=F32)
        return product.astype(BF16).reshape(len(masks), ring, rows, -1)

    steps = distances("dp")
    masks = list(far_masks())
    arrived = flip(products([mask | 1 for mask in masks]), "dp", 1)
    both = sent = add(products(masks), arrived).astype(BF16)
    for d in steps[1:]:
        here = [k for k, mask in enumerate(masks) if not mask & d]
        away = [masks.index(masks[k] | d) for k in here]
        arrived = flip(jnp.stack([both[k] for k in away]), "dp", d)
        both = add(jnp.stack([both[k] for k in here]), arrived).astype(BF16)
        masks = [masks[k] for k in here]
    return [both[0, s] for s in range(ring)], sent


def ring_blocks(right):
    ring, depth = lax.axis_size("fsdp"), right.shape[0]
    block = right.shape[1] // ring
    return [lax.dynamic_slice(right, (0, at * block), (depth, block)) for at in ring_places()]


def columns_near(left, rights):
    ring, block = len(rights), rights[0].shape[1]
    every = jnp.concatenate(rights, axis=1)
    near = {}
    for mask in reversed(far_masks()):
        away = jnp.dot(left(mask | 1), every, preferred_element_type=F32).astype(BF16)
        arrived = flip(away, "dp", 1)
        here = left(mask)
        near[mask] = [
            add(jnp.dot(here, rights[s], preferred_element_type=F32), arrived[:, s * block : (s + 1) * block]).astype(BF16)
            for s in range(ring)
        ]
    return near


def shards(
    inputs,
    cotangent,
    segments,
    norm_gain,
    in_weight,
    conv_weight,
    conv_bias,
    dt_bias,
    decay_log,
    skip_gain,
    gate_gain,
    out_weight,
):
    first = lax.axis_index("section") == 0
    z = lax.axis_index("fsdp")
    ring, share = lax.axis_size("fsdp"), lax.axis_size("dp")
    length, width = inputs.shape[2], inputs.shape[3]
    taps = conv_weight.shape[1]
    heads = dt_bias.shape[1] * ring
    inner = gate_gain.shape[1] * ring
    head_dim = inner // heads

    seg = segments[:, 0].astype(F32)
    seg_rows = [jnp.broadcast_to(seg[m][None], (8, length)) for m in range(2)]
    pick = functools.partial(jnp.where, first)

    seg1, seg3 = pick(seg_rows[1], seg_rows[0]), pick(seg_rows[0], seg_rows[1])
    pieces = (norm_gain[0], conv_bias[0], dt_bias[0], decay_log[0], skip_gain[0], gate_gain[0], conv_weight[0].reshape(-1))
    sizes = [piece.shape[0] for piece in pieces]
    proj = in_weight.shape[2]
    w, finish, packed = gather_all(
        in_weight[0].T.reshape(share, proj // share, -1),
        out_weight[0].reshape(share, -1, width),
        jnp.concatenate(pieces)[None],
        *seg_rows,
        seg1,
        seg3,
    )
    w = w.reshape(ring, proj, -1)
    fields, start = [], 0
    for size in sizes:
        fields.append(packed[:, start : start + size])
        start += size
    taps_w = fields[6].reshape(ring, taps, -1).transpose(1, 0, 2).reshape(taps, -1)
    rows = [field.reshape(1, -1) for field in fields[:6]]

    conv_width = conv_bias.shape[1] * ring

    def padded(row):
        return jnp.pad(row, ((0, 0), (0, conv_width - row.shape[1])))

    wide_rows = [rows[0], rows[1], rows[2], rows[3], jnp.repeat(rows[4], head_dim, axis=1), rows[5]]
    filler = jnp.zeros((-(taps + len(wide_rows)) % 8, conv_width), F32)
    small = jnp.concatenate([taps_w] + [padded(row) for row in wide_rows] + [filler], axis=0)
    sizes_of = (length, width, inner, conv_width, heads, taps)
    def to_second(value):
        return lax.ppermute(value, "section", [(0, 1)])

    def to_first(value):
        return lax.ppermute(value, "section", [(1, 0)])

    u_a, u_b = inputs[0, 0], inputs[1, 0]
    g_a, g_b = cotangent[0, 0], cotangent[1, 0]

    w, small, u_a, u_b, g_a, g_b, seg1, seg3, seg0 = lax.optimization_barrier(
        (w, small, u_a, u_b, g_a, g_b, seg1, seg3, seg_rows[0])
    )
    mixed0 = forward(u_a, seg0, small, sizes_of, w)[0]
    ow = finish(mixed0).reshape(inner, width)
    out0 = (u_a.astype(F32) + jnp.dot(mixed0, ow, preferred_element_type=F32)).astype(BF16)
    u1 = pick(u_b, to_second(out0))
    out1, *kept1, normed1, mixed1 = forward(u1, seg1, small, sizes_of, w, ow)
    stream_b = to_second(out1)
    back2 = backward(u1, g_a, seg1, small, sizes_of, kept1, w, ow)
    grad_a = to_first(back2[1])
    u3 = pick(u_a, stream_b)
    out3, *kept3, normed3, mixed3 = forward(u3, seg3, small, sizes_of, w, ow)
    g4 = pick(grad_a, g_b)
    back4 = backward(u3, g4, seg3, small, sizes_of, kept3, w, ow, full=True)
    grad_b = to_first(back4[1])

    mixed_both = after(jnp.concatenate([mixed3, mixed1], axis=0), back4[1])
    mixed_t = mixed_both.T.reshape(ring, share, -1, 2 * length)
    rights = ring_blocks(after(jnp.concatenate([normed3, normed1], axis=0), back4[1]))
    grad_b = after(grad_b, *rights)
    far_out, sent = rows_far(mixed_t, jnp.concatenate([g4, pick(grad_b, g_a)], axis=0))
    back5 = backward(after(u1, sent), grad_b, seg1, small, sizes_of, kept1, w, ow)

    q = lax.axis_index("dp")
    back5_t = after(back5[0], *far_out)

    def left(mask):
        def part(value):
            return lax.dynamic_index_in_dim(value.reshape(share, -1, length), q ^ mask, 0, keepdims=False)

        return jnp.concatenate([part(back4[0]), pick(part(back5_t), part(back2[0]))], axis=1)

    near_in = columns_near(left, rights)
    grad = back4[2] + pick(back5[2], back2[2])

    def field(k, size):
        return grad[taps + k, :size].reshape(ring, -1)

    packed = jnp.concatenate(
        [
            field(0, width),
            field(1, conv_width),
            field(2, heads),
            field(3, heads),
            jnp.sum(grad[taps + 4, :inner].reshape(heads, head_dim), axis=1).reshape(ring, -1),
            field(5, inner),
            grad[:taps].reshape(taps, ring, -1).transpose(1, 0, 2).reshape(ring, -1),
        ],
        axis=1,
    )
    own_in, own_out, packed = sum_rings(near_in, far_out, packed)
    in_grad = share_out(own_in).T[None]
    out_grad = share_out(own_out, own_in)[None]
    begun = near_in[0][0]
    output = pick(after(to_first(after(out1, begun)), own_in), out3)
    input_grad = pick(back4[3], after(to_second(after(back5[1], begun)), own_in).astype(F32))
    fields, start = [], 0
    for size in sizes:
        fields.append(packed[:, start : start + size])
        start += size
    return (
        output[None, None],
        input_grad[None, None],
        fields[0],
        in_grad,
        fields[6].reshape(1, taps, -1),
        fields[1],
        fields[2],
        fields[3],
        fields[4],
        fields[5],
        out_grad,
    )


def solution(mesh):
    spread_over = ("fsdp", "dp")
    row = P("section", "fsdp")
    matrix = P("section", "fsdp", None)
    tap = P("section", None, "fsdp")
    activation = P(None, spread_over, None, None)
    result = P("section", spread_over, None, None)
    return jax.shard_map(
        shards,
        mesh=mesh,
        in_specs=(activation, activation, P(None, spread_over, None), row, matrix, tap, row, row, row, row, row, matrix),
        out_specs=(result, result, row, matrix, tap, row, row, row, row, row, matrix),
        check_vma=False,
    )
```

```python
import functools

import jax
import jax.numpy as jnp
from jax import lax
from jax.experimental import pallas as pl
from jax.experimental.pallas import tpu as pltpu
from jax.sharding import PartitionSpec as P

EPS = 1e-05
LOG2E = 1.4426950408889634
HIGH = lax.Precision.HIGHEST
F32 = jnp.float32
BF16 = jnp.bfloat16
LANES = 128
WIDE = 256
VMEM_BYTES = 56 * 1024 * 1024


def sigmoid(v):
    return 0.5 * jnp.tanh(0.5 * v) + 0.5


def dot(a, b):
    return lax.dot_general(a, b, (((1,), (0,)), ((), ())), preferred_element_type=F32)


def dot_nt(a, b):
    return lax.dot_general(a, b, (((1,), (1,)), ((), ())), preferred_element_type=F32)


def dot_tn(a, b):
    return lax.dot_general(a, b, (((0,), (0,)), ((), ())), preferred_element_type=F32)


def twice(v):
    return jnp.concatenate([v, v], axis=1)


def fold(v):
    return v[:, :LANES] + v[:, LANES:]


def cols(start, width=WIDE):
    return pl.ds(pl.multiple_of(start, LANES), width)


def weight_copies(source, target, rows, sem, k):
    blocks, _, width = source.shape
    return [
        pltpu.make_async_copy(
            source.at[b, rows, :], target.at[rows, b * width : (b + 1) * width], sem.at[k, b]
        )
        for b in range(blocks)
    ]


def start(copies):
    for copy in copies:
        copy.start()


def wait(copies):
    for copy in copies:
        copy.wait()


def small_rows(small_ref, width, inner, conv, taps):
    row = lambda k, size: small_ref.at[taps + k : taps + k + 1, :size]
    return (
        row(0, width),
        small_ref.at[:taps],
        row(1, conv),
        row(2, LANES),
        row(3, LANES),
        row(4, inner),
        row(5, inner),
    )


def column_of(segr_ref):
    row = jnp.broadcast_to(segr_ref[:1, :], (LANES, segr_ref.shape[1]))
    return jnp.transpose(row)


def write_masks(segc_ref, mask_ref, taps):
    seg = segc_ref[...]
    row = lax.broadcasted_iota(jnp.int32, seg.shape, 0)
    for lag in range(1, taps):
        same = (pltpu.roll(seg, lag, 0) == seg) & (row >= lag)
        mask_ref[lag - 1] = jnp.where(same, 1.0, 0.0)


def conv_chunk(s, start, cw_ref, cb_ref, mask_ref, taps):
    at = cols(start)
    total = cb_ref[:, at] + s * cw_ref[pl.ds(taps - 1, 1), at]
    for lag in range(1, taps):
        shifted = pltpu.roll(s, lag, 0) * twice(mask_ref[lag - 1])
        total = total + shifted * cw_ref[pl.ds(taps - 1 - lag, 1), at]
    return total


def step_sizes(dt, dtb_ref, dl_ref, heads):
    length = dt.shape[0]
    pad = jnp.zeros((length, LANES - heads), F32)
    v = jnp.concatenate([dt, pad], axis=1) + dtb_ref[...]
    step = jnp.maximum(v, 0.0) + jnp.log1p(jnp.exp(-jnp.abs(v)))
    rate = -jnp.exp(dl_ref[...]) * step
    i = lax.broadcasted_iota(jnp.int32, (length, length), 0)
    j = lax.broadcasted_iota(jnp.int32, (length, length), 1)
    lower = jnp.where(i >= j, 1.0, 0.0)
    scaled = rate * LOG2E
    cumul = lax.dot_general(lower, scaled, (((1,), (0,)), ((), ())), precision=HIGH, preferred_element_type=F32)
    return v, step, rate, cumul


def head_lanes(v, quad, per):
    return pltpu.roll(v, lax.rem(LANES - per * quad, LANES), 1)


def spread(v, i0, head_dim):
    length = v.shape[0]
    lane = lax.broadcasted_iota(jnp.int32, (length, LANES), 1)
    a = jnp.broadcast_to(v[:, i0 : i0 + 1], (length, LANES))
    b = jnp.broadcast_to(v[:, i0 + 1 : i0 + 2], (length, LANES))
    return jnp.where(lane < head_dim, a, b)


def forward_body(
    sizes, keep, u_ref, segr_ref, small_ref, w_hbm, *refs
):
    length, width, inner, conv, heads, taps = sizes
    ng_ref, cw_ref, cb_ref, dtb_ref, dl_ref, sk_ref, gg_ref = small_rows(small_ref, width, inner, conv, taps)
    ow_hbm, refs = (refs[0], refs[1:]) if keep else (None, refs)
    count = 10 if keep else 1
    outs, held, refs = refs[:count], refs[count : count + 10], refs[count + 10 :]
    out_ref, zs_ref, zslope_ref, yf_ref, x_ref, slope_ref, stream_ref, dt_ref, normed_ref, mixed_ref = held
    w, ow, segc_ref, mask_ref, s_ref, gated_ref, gate_ref, cum_ref, step_ref, cumt_ref, sem, osem, wsem = refs
    state = (conv - inner) // 2
    head_dim = inner // heads
    per = WIDE // head_dim
    quads = inner // WIDE
    half = length // 2
    proj = w.shape[0]
    tail = 2 * inner

    def written(k, at, j):
        if keep or k == 9:
            return [pltpu.make_async_copy(held[k].at[:, at], outs[k if keep else 0].at[:, at], wsem.at[k, j])]
        return []


    def copies(at, k):
        return weight_copies(w_hbm, w, at, sem, k)

    def stream_copy(q):
        return copies(cols(inner + q * WIDE), 1 + 2 * q)

    def gate_copy(q):
        return copies(cols(q * WIDE), 2 + 2 * q)

    tail_copy = copies(pl.ds(tail, proj - tail), 0)
    start(tail_copy)
    ahead = min(3, quads)
    for q in range(ahead):
        start(stream_copy(q))
        start(gate_copy(q))
    out_copy = pltpu.make_async_copy(ow_hbm, ow, osem) if keep else None

    u = u_ref[...].astype(F32)
    scale = lax.rsqrt(jnp.mean(u * u, axis=-1, keepdims=True) + EPS)
    normed_ref[...] = (u * scale * ng_ref[...]).astype(BF16)
    start(written(8, pl.ds(0, width), 0))
    segc_ref[...] = column_of(segr_ref)
    write_masks(segc_ref, mask_ref, taps)

    def project(q):
        rows = cols(inner + q * WIDE)
        stream_ref[:, cols(q * WIDE)] = dot_nt(normed_ref[...], w[rows, :]).astype(BF16)
        gate_ref[:, cols(q * WIDE)] = dot_nt(normed_ref[...], w[cols(q * WIDE), :])

    wait(tail_copy)
    dt = dot_nt(normed_ref[...], w[inner + conv : proj, :])
    dt_ref[...] = dt
    start(written(7, pl.ds(0, heads), 0))
    stream_ref[:, cols(inner)] = dot_nt(normed_ref[...], w[tail : tail + 2 * state, :]).astype(BF16)
    _, step, _, cumul = step_sizes(dt, dtb_ref, dl_ref, heads)
    step_ref[...] = step
    cum_ref[...] = cumul
    cumt_ref[...] = jnp.transpose(cumul)
    wait(stream_copy(0))
    wait(gate_copy(0))
    project(0)

    def conv_of(first):
        at = cols(first)
        total = conv_chunk(stream_ref[:, at].astype(F32), first, cw_ref, cb_ref, mask_ref, taps)
        sig = sigmoid(total)
        x = total * sig
        if keep:
            x_ref[:, at] = x.astype(BF16)
            slope_ref[:, at] = (sig + x * (1.0 - sig)).astype(BF16)
        return x

    bc = conv_of(inner)
    start(written(4, cols(inner), quads) + written(5, cols(inner), quads) + written(6, cols(inner), quads))
    keys = bc[:, :state].astype(BF16)
    queries = bc[:, state:].astype(BF16)
    i = lax.broadcasted_iota(jnp.int32, (length, length), 0)
    j = lax.broadcasted_iota(jnp.int32, (length, length), 1)
    within = (i >= j) & (segc_ref[:, :1] == segr_ref[:1, :])
    s_ref[...] = jnp.where(within, dot_nt(queries, keys), 0.0)

    def quad_step(q, squares, more=True):
        at = cols(q * WIDE)
        if more:

            @pl.when(q + ahead < quads)
            def _():
                start(stream_copy(q + ahead))
                start(gate_copy(q + ahead))

            if keep:

                @pl.when(q + ahead == quads)
                def _():
                    out_copy.start()

            wait(stream_copy(q + 1))
            wait(gate_copy(q + 1))
        x = conv_of(q * WIDE)
        z = gate_ref[:, at]
        sig = sigmoid(z)
        zs = z * sig
        if keep:
            zs_ref[:, at] = zs.astype(BF16)
            zslope_ref[:, at] = (sig + zs * (1.0 - sig)).astype(BF16)
        if more:
            project(q + 1)
        cum_q = head_lanes(cum_ref[...], q, per)
        step_q = head_lanes(step_ref[...], q, per)
        ys = []
        for pair in range(per // 2):
            part = slice(pair * LANES, (pair + 1) * LANES)
            xdt = (x[:, part] * spread(step_q, 2 * pair, head_dim)).astype(BF16)
            got = []
            for k in range(2):
                h = 2 * pair + k
                col = cum_q[:, h : h + 1]
                row = cumt_ref[pl.ds(per * q + h, 1), :]
                top = jnp.exp2(jnp.minimum(col[:half] - row[:, :half], 0.0)) * s_ref[:half, :half]
                low = jnp.exp2(jnp.minimum(col[half:] - row, 0.0)) * s_ref[half:, :]
                got.append(
                    jnp.concatenate(
                        [dot(top.astype(BF16), xdt[:half]), dot(low.astype(BF16), xdt)], axis=0
                    )
                )
            lane = lax.broadcasted_iota(jnp.int32, (length, LANES), 1)
            ys.append(jnp.where(lane < head_dim, got[0], got[1]))
        yf = jnp.concatenate(ys, axis=1) + sk_ref[:, at] * x
        gated = yf * zs
        if keep:
            yf_ref[:, at] = yf.astype(BF16)
        gated_ref[:, at] = gated
        for k in range(1, 7):
            start(written(k, at, q))
        return squares + fold(gated * gated)

    squares = lax.fori_loop(0, quads - 1, quad_step, jnp.zeros((length, LANES), F32))
    squares = quad_step(quads - 1, squares, more=False)
    scale2 = lax.rsqrt(jnp.sum(squares, axis=-1, keepdims=True) * (1.0 / inner) + EPS)

    for q in range(quads):
        at = cols(q * WIDE)
        mixed_ref[:, at] = (gated_ref[:, at] * scale2 * gg_ref[:, at]).astype(BF16)
        start(written(9, at, q))
    if keep:
        out_copy.wait()
    for n in range(width // WIDE if keep else 0):
        at = cols(n * WIDE)
        out_ref[:, at] = (u_ref[:, at].astype(F32) + dot(mixed_ref[...], ow[:, at])).astype(BF16)
        start(written(0, at, n))
    for n in range(width // WIDE if keep else 0):
        wait(written(0, cols(n * WIDE), n))
    wait(written(7, pl.ds(0, heads), 0) + written(8, pl.ds(0, width), 0))
    wait(written(4, cols(inner), quads) + written(5, cols(inner), quads) + written(6, cols(inner), quads))
    for q in range(quads):
        for k in (1, 2, 3, 4, 5, 6, 9):
            wait(written(k, cols(q * WIDE), q))


def vmem():
    return pl.BlockSpec(memory_space=pltpu.VMEM)


def hbm():
    return pl.BlockSpec(memory_space=pl.ANY)


def forward(u, seg_row, small, sizes, w, ow=None):
    keep = ow is not None
    length, width, inner, conv, heads, taps = sizes
    blocks, proj = w.shape[:2]
    quads = inner // WIDE
    held = (
        ((length, width), BF16),
        ((length, inner), BF16),
        ((length, inner), BF16),
        ((length, inner), BF16),
        ((length, conv), BF16),
        ((length, conv), BF16),
        ((length, conv), BF16),
        ((length, heads), F32),
        ((length, width), BF16),
        ((length, inner), BF16),
    )
    outs = held if keep else held[9:]
    weights = (w, ow) if keep else (w,)
    return pl.pallas_call(
        functools.partial(forward_body, sizes, keep),
        out_shape=tuple(jax.ShapeDtypeStruct(*out) for out in outs),
        in_specs=[vmem()] * 3 + [hbm()] * len(weights),
        out_specs=[hbm()] * len(outs),
        scratch_shapes=[pltpu.VMEM(*one) for one in held]
        + [
            pltpu.VMEM((proj, width), BF16),
            pltpu.VMEM((inner, width), BF16),
            pltpu.VMEM((length, LANES), F32),
            pltpu.VMEM((taps - 1, length, LANES), F32),
            pltpu.VMEM((length, length), F32),
            pltpu.VMEM((length, inner), F32),
            pltpu.VMEM((length, inner), F32),
            pltpu.VMEM((length, LANES), F32),
            pltpu.VMEM((length, LANES), F32),
            pltpu.VMEM((LANES, length), F32),
            pltpu.SemaphoreType.DMA((1 + 2 * quads, blocks)),
            pltpu.SemaphoreType.DMA,
            pltpu.SemaphoreType.DMA((10, quads + 1)),
        ],
        compiler_params=pltpu.CompilerParams(vmem_limit_bytes=VMEM_BYTES),
        cost_estimate=pl.CostEstimate(
            flops=2 * length * (width * proj + inner * width + 2 * length * inner),
            bytes_accessed=2 * (width * proj + inner * width),
            transcendentals=length * (length * heads + 2 * inner),
        ),
        name="layer_forward",
    )(u, seg_row, small, *weights)


def backward_body(
    sizes, full, u_ref, g_ref, segr_ref, small_ref, zs_hbm, zslope_hbm, yf_hbm, x_hbm, slope_hbm, stream_hbm, dt_ref, w_hbm, ow_hbm,
    dlowt_hbm, low_ref, dsmall_ref, *refs,
):
    length, width, inner, conv, heads, taps = sizes
    ng_ref, cw_ref, cb_ref, dtb_ref, dl_ref, sk_ref, gg_ref = small_rows(small_ref, width, inner, conv, taps)
    dng_ref, dcw_ref, dcb_ref, ddtb_ref, ddl_ref, dsk_ref, dgg_ref = small_rows(
        dsmall_ref, width, inner, conv, taps
    )
    gin_ref = refs[0] if full else None
    (
        w, ow, zs_ref, zslope_ref, yf_ref, x_ref, slope_ref, stream_ref, dlowt_ref, segc_ref, mask_ref, dm_ref, st_ref, dst_ref,
        cum_ref, step_ref, cumt_ref, heads_ref, direct_ref, rows_ref, dn_ref, dlow_ref, sem, osem, rsem, wsem,
    ) = refs[1 if full else 0 :]
    state = (conv - inner) // 2
    head_dim = inner // heads
    per = WIDE // head_dim
    quads = inner // WIDE
    half = length // 2
    proj = w.shape[0]

    def fetch(k, source, target, at, j):
        return pltpu.make_async_copy(source.at[:, at], target.at[:, at], rsem.at[k, j])

    def read(q):
        at = pl.ds(pl.multiple_of(q * WIDE, WIDE), WIDE)
        return [
            pltpu.make_async_copy(ow_hbm.at[at, :], ow.at[at, :], osem.at[q]),
            fetch(0, zs_hbm, zs_ref, at, q),
            fetch(1, yf_hbm, yf_ref, at, q),
        ]

    def read_later(q):
        at = pl.ds(pl.multiple_of(q * WIDE, WIDE), WIDE)
        return [
            fetch(2, x_hbm, x_ref, at, q),
            fetch(3, slope_hbm, slope_ref, at, q),
            fetch(4, stream_hbm, stream_ref, at, q),
            fetch(5, zslope_hbm, zslope_ref, at, q),
        ]

    last = pl.ds(inner, conv - inner)
    read_last = [
        fetch(2, x_hbm, x_ref, last, quads),
        fetch(3, slope_hbm, slope_ref, last, quads),
        fetch(4, stream_hbm, stream_ref, last, quads),
    ]
    for q in range(quads):
        start(read(q))
    start(read_last)
    in_copy = weight_copies(w_hbm, w, pl.ds(0, proj), sem, 0)

    def written(first, size, j):
        rows = pl.ds(pl.multiple_of(first, 32), size)
        return [pltpu.make_async_copy(dlowt_ref.at[rows, :], dlowt_hbm.at[rows, :], wsem.at[j])]

    dsmall_ref[...] = jnp.zeros_like(dsmall_ref)
    segc_ref[...] = column_of(segr_ref)
    write_masks(segc_ref, mask_ref, taps)
    v, step, rate, cumul = step_sizes(dt_ref[...], dtb_ref, dl_ref, heads)
    step_ref[...] = step
    cum_ref[...] = cumul
    cumt_ref[...] = jnp.transpose(cumul)
    heads_ref[...] = jnp.zeros_like(heads_ref)
    direct_ref[...] = jnp.zeros_like(direct_ref)
    dst_ref[...] = jnp.zeros_like(dst_ref)
    rows_ref[...] = jnp.zeros_like(rows_ref)

    def first_step(q, carry):
        squares, cross = carry
        at = cols(q * WIDE)
        wait(read(q))
        start(read_later(q))
        dm = dot_nt(g_ref[...], ow[pl.ds(pl.multiple_of(q * WIDE, WIDE), WIDE), :])
        gated = yf_ref[:, at].astype(F32) * zs_ref[:, at].astype(F32)
        dm_ref[:, at] = dm
        return squares + fold(gated * gated), cross + fold(gated * (dm * gg_ref[:, at]))

    zero = jnp.zeros((length, LANES), F32)
    squares, cross = lax.fori_loop(0, quads, first_step, (zero, zero))
    scale2 = lax.rsqrt(jnp.sum(squares, axis=-1, keepdims=True) * (1.0 / inner) + EPS)
    back2 = jnp.sum(cross, axis=-1, keepdims=True) * scale2 * scale2 * scale2 * (1.0 / inner)

    start(in_copy)
    wait(read_last)
    keys = x_ref[:, inner : inner + state]
    queries = x_ref[:, inner + state : inner + 2 * state]
    j = lax.broadcasted_iota(jnp.int32, (length, length), 0)
    i = lax.broadcasted_iota(jnp.int32, (length, length), 1)
    within = (i >= j) & (segc_ref[:, :1] == segr_ref[:1, :])
    st_ref[...] = jnp.where(within, dot_nt(keys, queries), 0.0)

    def write_low(at, value):
        low = value.astype(BF16)
        dlow_ref[:, at] = low
        dlowt_ref[at, :] = jnp.transpose(low)

    def conv_back(start, d_conv):
        at = cols(start)
        d_total = d_conv * slope_ref[:, at].astype(F32)
        s = stream_ref[:, at].astype(F32)
        dcb_ref[:, at] = jnp.sum(d_total, axis=0, keepdims=True)
        dcw_ref[pl.ds(taps - 1, 1), at] = jnp.sum(d_total * s, axis=0, keepdims=True)
        d_stream = d_total * cw_ref[pl.ds(taps - 1, 1), at]
        for lag in range(1, taps):
            back = pltpu.roll(d_total * twice(mask_ref[lag - 1]), length - lag, 0)
            dcw_ref[pl.ds(taps - 1 - lag, 1), at] = jnp.sum(back * s, axis=0, keepdims=True)
            d_stream = d_stream + back * cw_ref[pl.ds(taps - 1 - lag, 1), at]
        write_low(cols(inner + start), d_stream)

    for q in range(quads):
        wait(read_later(q))

    def second_step(q, _):
        at = cols(q * WIDE)
        x = x_ref[:, at].astype(F32)
        zs = zs_ref[:, at].astype(F32)
        yf = yf_ref[:, at].astype(F32)
        gated = yf * zs
        scaled = dm_ref[:, at] * scale2
        dgg_ref[:, at] = jnp.sum(scaled * gated, axis=0, keepdims=True)
        d_gated = scaled * gg_ref[:, at] - gated * back2
        dy = d_gated * zs
        write_low(at, d_gated * yf * zslope_ref[:, at].astype(F32))
        dsk_ref[:, at] = jnp.sum(dy * x, axis=0, keepdims=True)
        dy_low = dy.astype(BF16)
        cum_q = head_lanes(cum_ref[...], q, per)
        step_q = head_lanes(step_ref[...], q, per)
        lane = lax.broadcasted_iota(jnp.int32, (length, LANES), 1)
        dst_top = jnp.zeros((half, length), F32)
        dst_low = jnp.zeros((half, half), F32)
        xdts, dxdts, steps = [], [], []
        for pair in range(per // 2):
            part = slice(pair * LANES, (pair + 1) * LANES)
            step_p = spread(step_q, 2 * pair, head_dim)
            xdt = (x[:, part] * step_p).astype(BF16)
            dyp = dy_low[:, part]
            got = []
            for k in range(2):
                h = 2 * pair + k
                mine = (lane < head_dim) if k == 0 else (lane >= head_dim)
                xm = jnp.where(mine, xdt.astype(F32), 0.0).astype(BF16)
                col = cum_q[:, h : h + 1]
                row = cumt_ref[pl.ds(per * q + h, 1), :]
                decay_top = jnp.exp2(jnp.minimum(row - col[:half], 0.0))
                decay_low = jnp.exp2(jnp.minimum(row[:, half:] - col[half:], 0.0))
                top = (decay_top * st_ref[:half, :]).astype(BF16)
                low = (decay_low * st_ref[half:, half:]).astype(BF16)
                got.append(jnp.concatenate([dot(top, dyp), dot(low, dyp[half:])], axis=0))
                dm_top = dot_nt(xm[:half], dyp)
                dm_low = dot_nt(xm[half:], dyp[half:])
                dst_top = dst_top + dm_top * decay_top
                dst_low = dst_low + dm_low * decay_low
                sums = jnp.sum(dm_top * top.astype(F32), axis=0, keepdims=True)
                more = jnp.sum(dm_low * low.astype(F32), axis=0, keepdims=True)
                rows_ref[pl.ds(per * q + h, 1), :] = jnp.concatenate([sums[:, :half], sums[:, half:] + more], axis=1)
            xdts.append(xdt.astype(F32))
            steps.append(step_p)
            dxdts.append(jnp.where(lane < head_dim, got[0], got[1]))
        dst_ref[:half, :] += dst_top
        dst_ref[half:, half:] += dst_low
        xdt = jnp.concatenate(xdts, axis=1)
        dxdt = jnp.concatenate(dxdts, axis=1)
        steps = jnp.concatenate(steps, axis=1)
        pick_row = lax.broadcasted_iota(jnp.int32, (WIDE, LANES), 0)
        pick_col = lax.broadcasted_iota(jnp.int32, (WIDE, LANES), 1)
        pick = jnp.where(pick_row // head_dim + per * q == pick_col, 1.0, 0.0).astype(BF16)
        both = xdt * dxdt
        high = both.astype(BF16)
        rest = (both - high.astype(F32)).astype(BF16)
        heads_ref[...] += dot(high, pick) + dot(rest, pick)
        direct_ref[...] += dot((dxdt * x).astype(BF16), pick)
        conv_back(q * WIDE, dxdt * steps + sk_ref[:, at] * dy)
        start(written(q * WIDE, WIDE, q) + written(inner + q * WIDE, WIDE, quads + q))
        return 0

    lax.fori_loop(0, quads, second_step, 0, unroll=2)

    d_scores = jnp.where(within, dst_ref[...], 0.0).astype(BF16)
    conv_back(inner, jnp.concatenate([dot(d_scores, queries), dot_tn(d_scores, keys)], axis=1))

    upper = jnp.where(within, 1.0, 0.0)
    d_rate = lax.dot_general(
        upper, jnp.transpose(rows_ref[...]) - heads_ref[...], (((1,), (0,)), ((), ())), precision=HIGH, preferred_element_type=F32
    )
    ddl_ref[...] = jnp.sum(d_rate * rate, axis=0, keepdims=True)
    d_step = direct_ref[...] - d_rate * jnp.exp(dl_ref[...])
    d_dt = d_step / (1.0 + jnp.exp(-v))
    ddtb_ref[...] = jnp.sum(d_dt, axis=0, keepdims=True)
    d_dt_low = d_dt[:, :heads].astype(BF16)
    dlowt_ref[inner + conv : proj, :] = jnp.transpose(d_dt)[:heads].astype(BF16)
    start(written(2 * inner, proj - 2 * inner, 2 * quads))

    wait(in_copy)
    u = u_ref[...].astype(F32)
    scale = lax.rsqrt(jnp.mean(u * u, axis=-1, keepdims=True) + EPS)

    def normed_step(n, _):
        at = cols(n * WIDE)
        dn_ref[:, at] = dot(dlow_ref[...], w[: inner + conv, at]) + dot(d_dt_low, w[inner + conv : proj, at])
        return 0

    lax.fori_loop(0, width // WIDE, normed_step, 0)
    dn = dn_ref[...]
    dng_ref[...] = jnp.sum(dn * u * scale, axis=0, keepdims=True)
    dn = dn * ng_ref[...]
    back = jnp.mean(dn * u, axis=-1, keepdims=True) * scale * scale * scale
    gin = g_ref[...].astype(F32) + dn * scale - u * back
    if full:
        gin_ref[...] = gin
    low_ref[...] = gin.astype(BF16)
    for q in range(quads):
        wait(written(q * WIDE, WIDE, q) + written(inner + q * WIDE, WIDE, quads + q))
    wait(written(2 * inner, proj - 2 * inner, 2 * quads))


def backward(u, g, seg_row, small, sizes, kept, w, ow, full=False):
    length, width, inner, conv, heads, taps = sizes
    blocks, proj = w.shape[:2]
    quads = inner // WIDE
    shape = jax.ShapeDtypeStruct
    outs = (shape((proj, length), BF16), shape((length, width), BF16), shape(small.shape, F32))
    outs += (shape((length, width), F32),) if full else ()
    zs, zslope, yf, x, slope, stream, dt = kept
    return pl.pallas_call(
        functools.partial(backward_body, sizes, full),
        out_shape=outs,
        in_specs=[vmem()] * 4 + [hbm()] * 6 + [vmem()] + [hbm()] * 2,
        out_specs=[hbm()] + [vmem()] * (len(outs) - 1),
        scratch_shapes=[
            pltpu.VMEM((proj, width), BF16),
            pltpu.VMEM((inner, width), BF16),
            pltpu.VMEM((length, inner), BF16),
            pltpu.VMEM((length, inner), BF16),
            pltpu.VMEM((length, inner), BF16),
            pltpu.VMEM((length, conv), BF16),
            pltpu.VMEM((length, conv), BF16),
            pltpu.VMEM((length, conv), BF16),
            pltpu.VMEM((proj, length), BF16),
            pltpu.VMEM((length, LANES), F32),
            pltpu.VMEM((taps - 1, length, LANES), F32),
            pltpu.VMEM((length, inner), F32),
            pltpu.VMEM((length, length), F32),
            pltpu.VMEM((length, length), F32),
            pltpu.VMEM((length, LANES), F32),
            pltpu.VMEM((length, LANES), F32),
            pltpu.VMEM((LANES, length), F32),
            pltpu.VMEM((length, LANES), F32),
            pltpu.VMEM((length, LANES), F32),
            pltpu.VMEM((LANES, length), F32),
            pltpu.VMEM((length, width), F32),
            pltpu.VMEM((length, inner + conv), BF16),
            pltpu.SemaphoreType.DMA((1, blocks)),
            pltpu.SemaphoreType.DMA((quads,)),
            pltpu.SemaphoreType.DMA((6, quads + 1)),
            pltpu.SemaphoreType.DMA((2 * quads + 1,)),
        ],
        compiler_params=pltpu.CompilerParams(vmem_limit_bytes=VMEM_BYTES),
        cost_estimate=pl.CostEstimate(
            flops=2 * length * (width * proj + inner * width + 4 * length * inner),
            bytes_accessed=2 * (width * proj + inner * width) + 8 * length * proj,
            transcendentals=length * (length * heads + 4 * inner),
        ),
        name="layer_backward",
    )(u, g, seg_row, small, zs, zslope, yf, x, slope, stream, dt, w, ow)


def flip(value, axis, distance):
    pairs = [(source, source ^ distance) for source in range(lax.axis_size(axis))]
    return lax.ppermute(value, axis, pairs)


def rotate(value, axis):
    count = lax.axis_size(axis)
    return lax.ppermute(value, axis, [(source, (source + 1) % count) for source in range(count)])


def distances(axis):
    found, d = [], 1
    while d < lax.axis_size(axis):
        found.append(d)
        d *= 2
    return found


def after(value, *others):
    return lax.optimization_barrier((value,) + others)[0]


def blank(shape, dtype):
    return pl.pallas_call(
        lambda out: None,
        out_shape=jax.ShapeDtypeStruct(shape, dtype),
        out_specs=hbm(),
        compiler_params=pltpu.CompilerParams(vmem_limit_bytes=1024 * 1024),
        name="blank",
    )()


class Line:
    def __init__(self):
        self.last = None

    def take(self, value):
        if self.last is not None:
            value, _ = lax.optimization_barrier((value, self.last))
        self.last = value
        return value


def gather_all(large, little, row, *early):
    ring, share = lax.axis_size("fsdp"), lax.axis_size("dp")
    z, q = lax.axis_index("fsdp"), lax.axis_index("dp")
    far, near = distances("dp")[-1], list(reversed(distances("dp")[:-1]))
    line = Line()

    def own_part(own):
        return lax.dynamic_index_in_dim(own, q, 0, keepdims=False)

    def begin(own):
        return lax.dynamic_update_slice(blank((ring,) + own.shape, own.dtype), own[None], (z, 0, 0, 0))

    def place(whole, step, here, arrived):
        parts = {0: here, far: arrived}
        for d in near:
            parts.update({m | d: flip(v, "dp", d) for m, v in list(parts.items())})
        source = lax.rem(z - step + ring, ring)
        for m, v in parts.items():
            whole = lax.dynamic_update_slice(whole, v[None, None], (source, q ^ m, 0, 0))
        return whole

    travelling = own_part(large)
    arriving = rotate(travelling, "fsdp")
    rows = [after(row, travelling)]
    row_next = rotate(rows[0], "fsdp")
    large_all = after(begin(large), *early)
    little_all = begin(little)
    waiting, little_next = None, None
    for step in range(1, ring):
        here = line.take(arriving)
        if step + 1 < ring:
            arriving = rotate(here, "fsdp")
        arrived = flip(here, "dp", far)
        if step + 2 >= ring and little_next is None:
            little_next = rotate(after(own_part(little), here), "fsdp")
        if waiting is not None:
            large_all = place(large_all, step - 1, waiting[0], line.take(waiting[1]))
        waiting = (here, arrived)
        rows.append(line.take(row_next))
        if step + 1 < ring:
            row_next = rotate(rows[-1], "fsdp")
    pending = []
    for step in range(1, ring):
        here = line.take(little_next)
        if step + 1 < ring:
            little_next = rotate(here, "fsdp")
        pending.append((here, flip(here, "dp", far)))
        if step + 1 == max(ring - 1, 2):
            large_all = place(large_all, ring - 1, waiting[0], line.take(waiting[1]))
    if ring < 3:
        large_all = place(large_all, ring - 1, waiting[0], line.take(waiting[1]))
    placed = large_all
    large_all = after(large_all, pending[-1][0])

    def finish(*behind):
        whole = little_all
        for step, (here, arrived) in enumerate(pending, 1):
            whole = place(whole, step, here, after(arrived, *behind) if step > 1 else after(arrived, placed))
        return whole

    at = jnp.arange(ring)
    chosen = (lax.rem(z - at[:, None] + ring, ring) == at[None, :]).astype(row.dtype)
    return large_all, finish, jnp.dot(chosen, jnp.concatenate(rows, axis=0), preferred_element_type=F32)


def ring_places():
    ring, z = lax.axis_size("fsdp"), lax.axis_index("fsdp")
    return [lax.rem(z + 2 * ring - 1 - s, ring) for s in range(ring)]


def add(a, b):
    return a.astype(F32) + b.astype(F32)


def sum_far(near, level, mask):
    if level == 0:
        return near[mask]
    d = distances("dp")[level]
    away = [flip(v, "dp", d) for v in sum_far(near, level - 1, mask | d)]
    line = Line()
    return [add(a, line.take(b)).astype(BF16) for a, b in zip(sum_far(near, level - 1, mask), away)]


def sum_rings(near, early, rows):
    ring, levels = lax.axis_size("fsdp"), len(distances("dp")) - 1
    d = distances("dp")[-1]
    order = Line()
    ready = [order.take(v) for v in sum_far(near, levels - 1, d)]
    away = [flip(v, "dp", d) for v in ready]
    here = [order.take(v) for v in sum_far(near, levels - 1, 0)]
    line = Line()
    value, value_next = None, None
    early_value, early_at = early[0], 0
    early_next = rotate(early[0], "fsdp")

    def early_step(value, arrived, at):
        value = add(arrived, early[at + 1]).astype(BF16)
        return value, (rotate(value, "fsdp") if at + 2 < ring else None), at + 1

    early_value, early_next, early_at = early_step(early_value, after(early_next, ready[-1]), early_at)
    rows = after(rows, ready[-1])
    rows = rows + flip(rows, "dp", distances("dp")[0])
    small = [lax.dynamic_index_in_dim(rows, at, 0) for at in ring_places()]
    small_value, small_at = small[0], 0
    small_next = rotate(small_value, "fsdp")

    def small_step(value, arrived, at):
        value = arrived + small[at + 1]
        return value, (rotate(value, "fsdp") if at + 2 < ring else None), at + 1

    for s in range(ring):
        part = add(here[s], line.take(away[s])).astype(BF16)
        if s > 0 and small_next is not None:
            small_value, small_next, small_at = small_step(small_value, line.take(small_next), small_at)
        value = part if s == 0 else add(line.take(value_next), part).astype(BF16)
        if s + 1 < ring:
            value_next = rotate(value, "fsdp")
        if early_next is not None:
            early_value, early_next, early_at = early_step(early_value, line.take(early_next), early_at)
        if s == 0 and small_next is not None and ring > 2:
            small_value, small_next, small_at = small_step(small_value, line.take(small_next), small_at)
    for d in distances("dp")[1:]:
        small_value = small_value + after(flip(small_value, "dp", d), value)
    return value, early_value, small_value


def share_out(value, *behind):
    q = lax.axis_index("dp")
    owned = {0: value}
    for d in reversed(distances("dp")):
        arrived = {m | d: flip(v, "dp", d) for m, v in owned.items()}
        owned.update({m: after(v, *behind) if behind else v for m, v in arrived.items()})
    whole = blank((lax.axis_size("dp"),) + value.shape, F32)
    for m, v in owned.items():
        whole = lax.dynamic_update_slice(whole, v.astype(F32)[None], (q ^ m, 0, 0))
    return whole.reshape(-1, value.shape[1])


def far_masks():
    return range(0, lax.axis_size("dp"), 2)


def rows_far(left, right):
    ring, _, rows, depth = left.shape
    q, order = lax.axis_index("dp"), ring_places()

    def products(masks):
        chosen = [lax.dynamic_index_in_dim(left, q ^ mask, 1, keepdims=False) for mask in masks]
        chosen = [lax.dynamic_index_in_dim(one, at, 0) for one in chosen for at in order]
        product = jnp.dot(jnp.concatenate(chosen).reshape(-1, depth), right, preferred_element_type=F32)
        return product.astype(BF16).reshape(len(masks), ring, rows, -1)

    steps = distances("dp")
    masks = list(far_masks())
    arrived = flip(products([mask | 1 for mask in masks]), "dp", 1)
    both = sent = add(products(masks), arrived).astype(BF16)
    for d in steps[1:]:
        here = [k for k, mask in enumerate(masks) if not mask & d]
        away = [masks.index(masks[k] | d) for k in here]
        arrived = flip(jnp.stack([both[k] for k in away]), "dp", d)
        both = add(jnp.stack([both[k] for k in here]), arrived).astype(BF16)
        masks = [masks[k] for k in here]
    return [both[0, s] for s in range(ring)], sent


def ring_blocks(right):
    ring, depth = lax.axis_size("fsdp"), right.shape[0]
    block = right.shape[1] // ring
    return [lax.dynamic_slice(right, (0, at * block), (depth, block)) for at in ring_places()]


def columns_near(left, rights):
    ring, block = len(rights), rights[0].shape[1]
    every = jnp.concatenate(rights, axis=1)
    near = {}
    for mask in reversed(far_masks()):
        away = jnp.dot(left(mask | 1), every, preferred_element_type=F32).astype(BF16)
        arrived = flip(away, "dp", 1)
        here = left(mask)
        near[mask] = [
            add(jnp.dot(here, rights[s], preferred_element_type=F32), arrived[:, s * block : (s + 1) * block]).astype(BF16)
            for s in range(ring)
        ]
    return near


def shards(
    inputs,
    cotangent,
    segments,
    norm_gain,
    in_weight,
    conv_weight,
    conv_bias,
    dt_bias,
    decay_log,
    skip_gain,
    gate_gain,
    out_weight,
):
    first = lax.axis_index("section") == 0
    z = lax.axis_index("fsdp")
    ring, share = lax.axis_size("fsdp"), lax.axis_size("dp")
    length, width = inputs.shape[2], inputs.shape[3]
    taps = conv_weight.shape[1]
    heads = dt_bias.shape[1] * ring
    inner = gate_gain.shape[1] * ring
    head_dim = inner // heads

    seg = segments[:, 0].astype(F32)
    seg_rows = [jnp.broadcast_to(seg[m][None], (8, length)) for m in range(2)]
    pick = functools.partial(jnp.where, first)

    seg1, seg3 = pick(seg_rows[1], seg_rows[0]), pick(seg_rows[0], seg_rows[1])
    pieces = (norm_gain[0], conv_bias[0], dt_bias[0], decay_log[0], skip_gain[0], gate_gain[0], conv_weight[0].reshape(-1))
    sizes = [piece.shape[0] for piece in pieces]
    proj = in_weight.shape[2]
    w, finish, packed = gather_all(
        in_weight[0].T.reshape(share, proj // share, -1),
        out_weight[0].reshape(share, -1, width),
        jnp.concatenate(pieces)[None],
        *seg_rows,
        seg1,
        seg3,
    )
    w = w.reshape(ring, proj, -1)
    fields, start = [], 0
    for size in sizes:
        fields.append(packed[:, start : start + size])
        start += size
    taps_w = fields[6].reshape(ring, taps, -1).transpose(1, 0, 2).reshape(taps, -1)
    rows = [field.reshape(1, -1) for field in fields[:6]]

    conv_width = conv_bias.shape[1] * ring

    def padded(row):
        return jnp.pad(row, ((0, 0), (0, conv_width - row.shape[1])))

    wide_rows = [rows[0], rows[1], rows[2], rows[3], jnp.repeat(rows[4], head_dim, axis=1), rows[5]]
    filler = jnp.zeros((-(taps + len(wide_rows)) % 8, conv_width), F32)
    small = jnp.concatenate([taps_w] + [padded(row) for row in wide_rows] + [filler], axis=0)
    sizes_of = (length, width, inner, conv_width, heads, taps)
    def to_second(value):
        return lax.ppermute(value, "section", [(0, 1)])

    def to_first(value):
        return lax.ppermute(value, "section", [(1, 0)])

    u_a, u_b = inputs[0, 0], inputs[1, 0]
    g_a, g_b = cotangent[0, 0], cotangent[1, 0]

    w, small, u_a, u_b, g_a, g_b, seg1, seg3, seg0 = lax.optimization_barrier(
        (w, small, u_a, u_b, g_a, g_b, seg1, seg3, seg_rows[0])
    )
    mixed0 = forward(u_a, seg0, small, sizes_of, w)[0]
    ow = finish(mixed0).reshape(inner, width)
    out0 = (u_a.astype(F32) + jnp.dot(mixed0, ow, preferred_element_type=F32)).astype(BF16)
    u1 = pick(u_b, to_second(out0))
    out1, *kept1, normed1, mixed1 = forward(u1, seg1, small, sizes_of, w, ow)
    stream_b = to_second(out1)
    back2 = backward(u1, g_a, seg1, small, sizes_of, kept1, w, ow)
    grad_a = to_first(back2[1])
    u3 = pick(u_a, stream_b)
    out3, *kept3, normed3, mixed3 = forward(u3, seg3, small, sizes_of, w, ow)
    g4 = pick(grad_a, g_b)
    back4 = backward(u3, g4, seg3, small, sizes_of, kept3, w, ow, full=True)
    grad_b = to_first(back4[1])

    mixed_both = after(jnp.concatenate([mixed3, mixed1], axis=0), back4[1])
    mixed_t = mixed_both.T.reshape(ring, share, -1, 2 * length)
    rights = ring_blocks(after(jnp.concatenate([normed3, normed1], axis=0), back4[1]))
    grad_b = after(grad_b, *rights)
    far_out, sent = rows_far(mixed_t, jnp.concatenate([g4, pick(grad_b, g_a)], axis=0))
    back5 = backward(after(u1, sent), grad_b, seg1, small, sizes_of, kept1, w, ow)

    q = lax.axis_index("dp")
    back5_t = after(back5[0], *far_out)

    def left(mask):
        def part(value):
            return lax.dynamic_index_in_dim(value.reshape(share, -1, length), q ^ mask, 0, keepdims=False)

        return jnp.concatenate([part(back4[0]), pick(part(back5_t), part(back2[0]))], axis=1)

    near_in = columns_near(left, rights)
    grad = back4[2] + pick(back5[2], back2[2])

    def field(k, size):
        return grad[taps + k, :size].reshape(ring, -1)

    packed = jnp.concatenate(
        [
            field(0, width),
            field(1, conv_width),
            field(2, heads),
            field(3, heads),
            jnp.sum(grad[taps + 4, :inner].reshape(heads, head_dim), axis=1).reshape(ring, -1),
            field(5, inner),
            grad[:taps].reshape(taps, ring, -1).transpose(1, 0, 2).reshape(ring, -1),
        ],
        axis=1,
    )
    own_in, own_out, packed = sum_rings(near_in, far_out, packed)
    in_grad = share_out(own_in).T[None]
    out_grad = share_out(own_out, own_in)[None]
    begun = near_in[0][0]
    output = pick(after(to_first(after(out1, begun)), own_in), out3)
    input_grad = pick(back4[3], after(to_second(after(back5[1], begun)), own_in).astype(F32))
    fields, start = [], 0
    for size in sizes:
        fields.append(packed[:, start : start + size])
        start += size
    return (
        output[None, None],
        input_grad[None, None],
        fields[0],
        in_grad,
        fields[6].reshape(1, taps, -1),
        fields[1],
        fields[2],
        fields[3],
        fields[4],
        fields[5],
        out_grad,
    )


def solution(mesh):
    spread_over = ("fsdp", "dp")
    row = P("section", "fsdp")
    matrix = P("section", "fsdp", None)
    tap = P("section", None, "fsdp")
    activation = P(None, spread_over, None, None)
    result = P("section", spread_over, None, None)
    return jax.shard_map(
        shards,
        mesh=mesh,
        in_specs=(activation, activation, P(None, spread_over, None), row, matrix, tap, row, row, row, row, row, matrix),
        out_specs=(result, result, row, matrix, tap, row, row, row, row, row, matrix),
        check_vma=False,
    )
```
